32 devices in a mesh: term: 4 (over z), pencil: 8 (over y, x, core).
Axes of the slice: x: 2, y: 2, z: 4, core: 2. Of those that a mesh axis runs over, the one named last changes fastest.
Arguments:
- present_acoustic: float32 [512, 16, 512], P('pencil'), may hold values from -6 to 6
- prior_acoustic: float32 [512, 16, 512], P('pencil'), may hold values from -6 to 6
- location_factor: float32 [16, 512, 16, 512], P('term', 'pencil'), may hold values from -1 to 1
- spectral_multiplier: float32 [16, 16, 512, 512], P('term', None, 'pencil'), may hold values from -6 to 6
- medium_kinds: int32 [512, 16, 512], P('pencil', 'term'), may hold values from 0 to 2
- organ_properties: float32 [3, 2], replicated, may hold values from 0.05 to 0.3
- thermal_increase: float32 [512, 16, 512], P('pencil', 'term'), may hold values from -6 to 6
Outputs:
- pressure_final: float32 [512, 16, 512], P('pencil', 'term')
- temperature_final: float32 [512, 16, 512], P('pencil', 'term')
The draws below stay inside these ranges and needn't reach their ends.
Inputs may be any that keep to these rules, and one draw needn't show every extreme that they name: `medium_kinds`: tissue class of each cell: 0 bone, 1 brain, 2 water.
All inputs are finite; a program needn't handle non-finite values.
Results may differ from the reference program's by a relative error of at most 0.0001.
Values sent between devices are 32-bit elements; how exact they have to be, the bound alone decides.
No kernel may reach another device: no remote copies, remote signals or barrier semaphores. Data moves between devices by JAX's collectives and lax.ppermute only.
A program may use at most 192 MiB of HBM per device.

```python
import jax
import jax.numpy as jnp

MESH_COUNT_INITIAL = 512
MESH_COUNT_FINAL = 512
MESH_COUNT_MIDDLE = 16
TERMS = 16
WAVE_STEPS = 2
HEAT_STEPS = 2


def place_ends(drawn, key, least, top_value):
    place = [jax.random.randint(jax.random.fold_in(key, axis), (), 0, length) for axis, length in enumerate(drawn.shape)]
    widest = drawn.shape.index(max(drawn.shape))
    neighbour = place[:widest] + [(place[widest] + 1) % drawn.shape[widest]] + place[widest + 1:]
    return drawn.at[tuple(place)].set(least).at[tuple(neighbour)].set(top_value)


def shard_levels(key, shape, pieces, smallest, largest):
    def one(dim, blocks):
        draws = jax.random.uniform(jax.random.fold_in(jax.random.fold_in(key, 6), dim), (blocks,), jnp.float32, smallest / len(pieces), largest / len(pieces))
        return jnp.repeat(jnp.exp(draws), shape[dim] // blocks).reshape((-1,) + (1,) * (len(shape) - dim - 1))

    loudness = one(*pieces[0])
    for cut in pieces[1:]:
        loudness = loudness * one(*cut)
    return loudness


def normal_values(key, extent, width, most, pieces=(), kind=jnp.bfloat16):
    array = width * jax.random.normal(key, extent, jnp.float32)
    if pieces:
        array = array * shard_levels(key, extent, pieces, -0.22, 0.18)
    return jnp.clip(array, -most, most).astype(kind)


def setup_inputs(seed: int = 0) -> dict:
    arg_keys = jax.random.split(jax.random.key(seed), 8)
    return {
        "present_acoustic": normal_values(arg_keys[0], (MESH_COUNT_INITIAL, MESH_COUNT_MIDDLE, MESH_COUNT_FINAL), 1.0, 6.0, ((0, 8),), jnp.float32),
        "prior_acoustic": normal_values(arg_keys[1], (MESH_COUNT_INITIAL, MESH_COUNT_MIDDLE, MESH_COUNT_FINAL), 1.0, 6.0, ((0, 8),), jnp.float32),
        "location_factor": normal_values(arg_keys[2], (TERMS, MESH_COUNT_INITIAL, MESH_COUNT_MIDDLE, MESH_COUNT_FINAL), 0.125, 1.0, ((0, 4), (1, 8)), jnp.float32),
        "spectral_multiplier": normal_values(arg_keys[3], (TERMS, MESH_COUNT_MIDDLE, MESH_COUNT_FINAL, MESH_COUNT_INITIAL), 1.0, 6.0, ((0, 4), (2, 8)), jnp.float32),
        "medium_kinds": place_ends(jax.random.randint(arg_keys[4], (MESH_COUNT_INITIAL, MESH_COUNT_MIDDLE, MESH_COUNT_FINAL), 0, 3), jax.random.fold_in(arg_keys[4], 1), 0, 2).astype(jnp.int32),
        "organ_properties": jnp.clip(jax.random.uniform(arg_keys[5], (3, 2), jnp.float32, 0.05, 0.3), 0.05, 0.3),
        "thermal_increase": normal_values(arg_keys[6], (MESH_COUNT_INITIAL, MESH_COUNT_MIDDLE, MESH_COUNT_FINAL), 1.0, 6.0, ((0, 8), (1, 4)), jnp.float32),
    }


DIFFUSION = 0.125


def spectral_sum(pressure, location_factor, spectral_multiplier):
    spectrum = jnp.fft.fftn(pressure, axes=(0, 1, 2))
    summed = jnp.zeros(pressure.shape, pressure.dtype)
    for term_index in range(TERMS):
        factor = jnp.transpose(spectral_multiplier[term_index], (2, 0, 1))
        restored = jnp.real(jnp.fft.ifftn(factor * spectrum, axes=(0, 1, 2)))
        summed = summed + location_factor[term_index] * restored
    return summed


def heat_step(present_thermal, perfuse, source):
    padded = jnp.pad(present_thermal, 1)
    near_sum = padded[2:, 1:-1, 1:-1] + padded[:-2, 1:-1, 1:-1]
    near_sum = near_sum + padded[1:-1, 2:, 1:-1] + padded[1:-1, :-2, 1:-1]
    near_sum = near_sum + padded[1:-1, 1:-1, 2:] + padded[1:-1, 1:-1, :-2]
    return present_thermal + DIFFUSION * (near_sum - 6.0 * present_thermal) - perfuse * present_thermal + source


def reference(present_acoustic, prior_acoustic, location_factor, spectral_multiplier, medium_kinds, organ_properties, thermal_increase):
    previous = prior_acoustic
    current = present_acoustic
    dose_sum = jnp.zeros(present_acoustic.shape, present_acoustic.dtype)
    for turn_index in range(WAVE_STEPS):
        advanced = 2.0 * spectral_sum(current, location_factor, spectral_multiplier) - previous
        dose_sum = dose_sum + advanced * advanced
        previous = current
        current = advanced
    absorb = jnp.where(medium_kinds == 0, organ_properties[0, 0], jnp.where(medium_kinds == 1, organ_properties[1, 0], organ_properties[2, 0]))
    perfuse = jnp.where(medium_kinds == 0, organ_properties[0, 1], jnp.where(medium_kinds == 1, organ_properties[1, 1], organ_properties[2, 1]))
    source = absorb * dose_sum
    present_thermal = thermal_increase
    for turn_index in range(HEAT_STEPS):
        present_thermal = heat_step(present_thermal, perfuse, source)
    return current, present_thermal
```

```python
import functools
import math

import jax
import jax.numpy as jnp
import ml_dtypes
import numpy as np
from jax import lax
from jax.experimental import pallas as pl
from jax.experimental.pallas import tpu as pltpu
from jax.sharding import PartitionSpec as P

WAVE_STEPS = 2
HEAT_STEPS = 2
DIFFUSION = 0.125
VMEM_BYTES = 56 * 1024 * 1024
F32 = jnp.float32
BF16 = jnp.bfloat16


def halves(table):
    high = table.astype(ml_dtypes.bfloat16)
    low = (table - high.astype(np.float64)).astype(ml_dtypes.bfloat16)
    return high, low


def angles(left, right, length):
    return (np.outer(left, right) % length) * (2.0 * math.pi / length)


def slot_wavenumbers(blocks, length_z):
    width = length_z // blocks
    half = width // 2
    slots = np.concatenate([[half], np.arange(1, half)])
    starts = np.arange(blocks) * width
    return starts[:, None] + slots[None, :], starts


def forward_z_table(blocks, length_z):
    main, first = slot_wavenumbers(blocks, length_z)
    z = np.arange(length_z)
    theta = angles(z, main.reshape(-1), length_z).reshape(length_z, blocks, -1)
    real, imag = np.cos(theta), -np.sin(theta)
    for q in range(blocks // 2):
        real[:, q, 0], imag[:, q, 0] = -imag[:, q, 0].copy(), real[:, q, 0].copy()
    theta = angles(z, first, length_z)
    real0, imag0 = np.cos(theta), -np.sin(theta)
    for q in range(blocks // 2 + 1, blocks):
        real0[:, q], imag0[:, q] = imag0[:, q].copy(), -real0[:, q].copy()
    table = np.concatenate(
        [np.stack([real, imag], 2).reshape(length_z, -1), np.stack([real0, imag0], 2).reshape(length_z, -1)], axis=1
    )
    spare = -table.shape[1] % 128
    return np.pad(table, ((0, 0), (0, spare)))


def inverse_z_table(blocks, length_z, scale):
    main, first = slot_wavenumbers(blocks, length_z)
    z = np.arange(length_z)
    theta = angles(main.reshape(-1), z, length_z).reshape(blocks, -1, length_z)
    real, imag = np.cos(theta), -np.sin(theta)
    for p in range(blocks):
        middle = theta[p, 0]
        imag[p, 0] = np.cos(middle) if p < blocks // 2 else -np.sin(middle)
        lowest = angles(first[p : p + 1], z, length_z)[0]
        real[p, 0] = np.cos(lowest) if p <= blocks // 2 else -np.sin(lowest)
    return scale * np.concatenate([real.reshape(-1, length_z), imag.reshape(-1, length_z)], axis=0)


def forward_x_table(length_x):
    x = np.arange(length_x)
    theta = angles(x, x, length_x)
    return np.concatenate([np.cos(theta), np.sin(theta)], axis=1)


def inverse_x_table(blocks, length_x):
    x = np.arange(length_x)
    theta = angles(x, x, length_x).reshape(length_x, blocks, -1)
    cosine, sine = np.cos(theta), np.sin(theta)
    real_rows = np.stack([cosine, sine], axis=2).reshape(length_x, -1)
    imag_rows = np.stack([-sine, cosine], axis=2).reshape(length_x, -1)
    return np.concatenate([real_rows, imag_rows], axis=0)


def mirror_table(length):
    x = np.arange(length)
    table = np.zeros((length, length), ml_dtypes.bfloat16)
    table[x, (-x) % length] = 1
    return table


def fourier(real, imag, sign):
    count = len(real)
    if count == 1:
        return real, imag
    if count % 2:
        out_real, out_imag = [], []
        for k in range(count):
            total_real, total_imag = real[0], imag[0]
            for n in range(1, count):
                angle = 2.0 * math.pi * (k * n % count) / count
                c, s = math.cos(angle), sign * math.sin(angle)
                total_real = total_real + (c * real[n] - s * imag[n])
                total_imag = total_imag + (c * imag[n] + s * real[n])
            out_real.append(total_real)
            out_imag.append(total_imag)
        return out_real, out_imag
    even_real, even_imag = fourier(real[::2], imag[::2], sign)
    odd_real, odd_imag = fourier(real[1::2], imag[1::2], sign)
    half = count // 2
    out_real, out_imag = [None] * count, [None] * count
    for k in range(half):
        a, b = odd_real[k], odd_imag[k]
        if k == 0:
            turned = (a, b)
        elif 4 * k == count:
            turned = (-b, a) if sign > 0 else (b, -a)
        else:
            angle = 2.0 * math.pi * k / count
            c, s = math.cos(angle), sign * math.sin(angle)
            if 8 * k == count or 8 * k == 3 * count:
                root = math.sqrt(0.5)
                sum_ab, less_ab = root * (a + b), root * (a - b)
                if c > 0:
                    turned = (less_ab, sum_ab) if s > 0 else (sum_ab, -less_ab)
                else:
                    turned = (-sum_ab, less_ab) if s > 0 else (-less_ab, -sum_ab)
            else:
                turned = (c * a - s * b, c * b + s * a)
        out_real[k] = even_real[k] + turned[0]
        out_imag[k] = even_imag[k] + turned[1]
        out_real[k + half] = even_real[k] - turned[0]
        out_imag[k + half] = even_imag[k] - turned[1]
    return out_real, out_imag


def split(values):
    high = values.astype(BF16)
    return high, (values - high.astype(F32)).astype(BF16)


def dot(left, right):
    return jnp.dot(left, right, preferred_element_type=F32)


def dot_three(high, low, table_high, table_low):
    return dot(high, table_high) + (dot(low, table_high) + dot(high, table_low))


def params(count=0):
    return pltpu.CompilerParams(vmem_limit_bytes=VMEM_BYTES, dimension_semantics=("arbitrary",) * count)


def cost(flops, moved):
    return pl.CostEstimate(flops=int(flops), bytes_accessed=int(moved), transcendentals=0)


def whole(shape, grid_rank):
    return pl.BlockSpec(shape, lambda *_: (0,) * len(shape), pipeline_mode=pl.Buffered(1)) if grid_rank else pl.BlockSpec(
        memory_space=pltpu.VMEM
    )


def forward_z_kernel(brick_ref, high_ref, low_ref, out_ref):
    width, rows, length_z = brick_ref.shape
    blocks = out_ref.shape[0]
    half = length_z // blocks // 2
    high, low = split(brick_ref[...].reshape(width * rows, length_z))
    result = dot_three(high, low, high_ref[...], low_ref[...])
    main = 2 * half
    out_ref[...] = jnp.zeros_like(out_ref)
    for q in range(blocks):
        for w in range(width):
            part = result[w * rows : (w + 1) * rows]
            out_ref[q, :, w * main : (w + 1) * main] = part[:, q * main : (q + 1) * main]
            at = blocks * main + 2 * q
            lane = width * main + w
            out_ref[q, :, lane : lane + 1] = part[:, at : at + 1]
            out_ref[q, :, lane + width : lane + width + 1] = part[:, at + 1 : at + 2]


def forward_z(brick, blocks):
    width, rows, length_z = brick.shape
    half = length_z // blocks // 2
    lanes = width * 2 * half + 2 * width
    lanes += -lanes % 128
    high, low = halves(forward_z_table(blocks, length_z))
    return pl.pallas_call(
        forward_z_kernel,
        out_shape=jax.ShapeDtypeStruct((blocks, rows, lanes), F32),
        compiler_params=params(),
        name="forward_z",
    )(brick, jnp.asarray(high), jnp.asarray(low))


def forward_x_kernel(data_ref, high_ref, low_ref, out_ref, *, width, half):
    length_x = data_ref.shape[0]
    main = width * 2 * half
    turned = data_ref[...].T
    high, low = split(turned[: out_ref.shape[0]])
    both = dot_three(high, low, high_ref[...], low_ref[...])
    by_cos, by_sin = both[:, :length_x], both[:, length_x:]
    for w in range(width):
        re, im = w * 2 * half, w * 2 * half + half
        out_ref[re : re + half] = by_cos[re : re + half] + by_sin[im : im + half]
        out_ref[im : im + half] = by_cos[im : im + half] - by_sin[re : re + half]
    re, im, end = main, main + width, main + 2 * width
    out_ref[re:im] = by_cos[re:im] + by_sin[im:end]
    out_ref[im:end] = by_cos[im:end] - by_sin[re:im]


def forward_x(data, width, half):
    length_x = data.shape[0]
    rows = width * 2 * half + 2 * width
    rows += -rows % 8
    high, low = halves(forward_x_table(length_x))
    return pl.pallas_call(
        functools.partial(forward_x_kernel, width=width, half=half),
        out_shape=jax.ShapeDtypeStruct((rows, length_x), F32),
        compiler_params=params(),
        name="forward_x",
    )(data, jnp.asarray(high), jnp.asarray(low))


def spread_kernel(
    f_ref, first_ref, own_ref, other_ref, high_ref, low_ref, out_ref,
    fk_ref, edge_ref, edge_out_ref, u_ref, u_high_ref, u_low_ref, *, width, first_term,
):
    length_y, _, half, length_x = fk_ref.shape
    lanes_out = out_ref.shape[-1]
    rows_x = lanes_out // 2
    main = width * 2 * half
    step = pl.program_id(0)
    tiles = [slice(at, at + 128) for at in range(0, length_x, 128)]

    @pl.when(step == 0)
    def _():
        @pl.loop(0, half // 8)
        def _(tile):
            for lanes in tiles:
                real, imag = [], []
                for y in range(length_y):
                    row = (y % width) * 2 * half + tile * 8
                    real.append(f_ref[y // width, pl.ds(pl.multiple_of(row, 8), 8), lanes])
                    imag.append(f_ref[y // width, pl.ds(pl.multiple_of(row + half, 8), 8), lanes])
                real, imag = fourier(real, imag, -1)
                at = pl.ds(pl.multiple_of(tile * 8, 8), 8)
                for y in range(length_y):
                    fk_ref[y, 0, at, lanes] = real[y]
                    fk_ref[y, 1, at, lanes] = imag[y]

        for index, lanes in enumerate(tiles):
            real = [f_ref[y // width, main + y % width : main + y % width + 1, lanes] for y in range(length_y)]
            imag = [
                f_ref[y // width, main + width + y % width : main + width + y % width + 1, lanes]
                for y in range(length_y)
            ]
            real, imag = fourier(real, imag, -1)
            factors = [first_ref[y, :, lanes] for y in range(length_y)]
            real = [factors[y] * real[y] for y in range(length_y)]
            imag = [factors[y] * imag[y] for y in range(length_y)]
            real, imag = fourier(real, imag, 1)
            for y in range(length_y):
                edge_ref[y, :, index * 128 : index * 128 + 128] = real[y]
                edge_ref[y, :, length_x + index * 128 : length_x + index * 128 + 128] = imag[y]
        high, low = split(edge_ref[...].reshape(-1, 2 * length_x))
        edge_out_ref[...] = dot_three(high, low, high_ref[...], low_ref[...])

    row_index = lax.broadcasted_iota(jnp.int32, (8, 128), 0)

    @pl.loop(0, half // 8)
    def _(tile):
        at = pl.ds(pl.multiple_of(tile * 8, 8), 8)
        swapped = jnp.logical_and(row_index == 0, tile == 0)
        for index, lanes in enumerate(tiles):
            real, imag = [], []
            for y in range(length_y):
                own = jnp.where(swapped, own_ref[0, y, half : half + 1, lanes], own_ref[0, y, at, lanes])
                factor = own + other_ref[0, y, at, lanes]
                real.append(factor * fk_ref[y, 0, at, lanes])
                imag.append(factor * fk_ref[y, 1, at, lanes])
            real, imag = fourier(real, imag, 1)
            for y in range(length_y):
                rows = pl.ds(pl.multiple_of(y * half + tile * 8, 8), 8)
                u_ref[rows, index * 128 : index * 128 + 128] = real[y]
                u_ref[rows, length_x + index * 128 : length_x + index * 128 + 128] = imag[y]

    @pl.loop(0, length_y * half // 64)
    def _(part):
        rows = pl.ds(pl.multiple_of(part * 64, 64), 64)
        high, low = split(u_ref[rows, :])
        u_high_ref[rows, :] = high
        u_low_ref[rows, :] = low

    term = first_term + step
    lane_index = lax.broadcasted_iota(jnp.int32, (8, lanes_out), 1)
    row_index = lax.broadcasted_iota(jnp.int32, (8, lanes_out), 0)
    swapped = jnp.logical_and(row_index == 0, lane_index < rows_x)
    count = 256 // lanes_out
    for part in range(2 * length_x // 256):
        cols = slice(part * 256, part * 256 + 256)
        result = dot_three(u_high_ref[...], u_low_ref[...], high_ref[:, cols], low_ref[:, cols])
        edges = [edge_out_ref[pl.ds(y * first_ref.shape[1] + term, 1), cols] for y in range(length_y)]
        for k in range(count):
            q = part * count + k
            inside = slice(k * lanes_out, (k + 1) * lanes_out)
            piece = result[:, inside]
            for y in range(length_y):
                top = piece[y * half : y * half + 8]
                out_ref[q, 0, y, :8, :] = jnp.where(swapped, edges[y][:, inside], top)
                out_ref[q, 0, y, 8:, :] = piece[y * half + 8 : (y + 1) * half]


def spread(f, first, own, other, blocks, width, first_term, terms):
    length_y, length_x = own.shape[1], own.shape[3]
    half = other.shape[2]
    rows_x = length_x // blocks
    high, low = halves(inverse_x_table(blocks, length_x))
    high, low = jnp.asarray(high), jnp.asarray(low)
    rows = length_y * half
    return pl.pallas_call(
        functools.partial(spread_kernel, width=width, first_term=first_term),
        grid=(terms,),
        in_specs=[
            whole(f.shape, 1),
            whole(first.shape, 1),
            pl.BlockSpec((1, length_y, half + 8, length_x), lambda t: (t + first_term, 0, 0, 0)),
            pl.BlockSpec((1, length_y, half, length_x), lambda t: (t + first_term, 0, 0, 0)),
            whole(high.shape, 1),
            whole(low.shape, 1),
        ],
        out_specs=pl.BlockSpec((blocks, 1, length_y, half, 2 * rows_x), lambda t: (0, t, 0, 0, 0)),
        out_shape=jax.ShapeDtypeStruct((blocks, terms, length_y, half, 2 * rows_x), F32),
        scratch_shapes=[
            pltpu.VMEM((length_y, 2, half, length_x), F32),
            pltpu.VMEM((length_y, first.shape[1], 2 * length_x), F32),
            pltpu.VMEM((length_y * first.shape[1], 2 * length_x), F32),
            pltpu.VMEM((rows, 2 * length_x), F32),
            pltpu.VMEM((rows, 2 * length_x), BF16),
            pltpu.VMEM((rows, 2 * length_x), BF16),
        ],
        compiler_params=params(1),
        cost_estimate=cost(terms * 6 * rows * 4 * length_x * length_x, terms * 16 * rows * length_x),
        name="spread",
    )(f, first, own, other, high, low)


def gather_kernel(data_ref, factor_ref, high_ref, low_ref, out_ref):
    blocks, terms, _, half, lanes = data_ref.shape
    rows = lanes // 2
    parts = []
    for t in range(terms):
        turned = data_ref[:, t, 0].reshape(blocks * half, lanes).T
        parts.append(jnp.concatenate([turned[:rows], turned[rows:]], axis=1))
    high, low = split(jnp.concatenate(parts, axis=0))
    fields = dot_three(high, low, high_ref[...], low_ref[...])
    total = factor_ref[0, 0] * fields[:rows]
    for t in range(1, terms):
        total = total + factor_ref[t, 0] * fields[t * rows : (t + 1) * rows]
    out_ref[0] = total


def gather(data, factor, scale):
    blocks, terms, length_y, half, lanes = data.shape
    rows, length_z = factor.shape[2], factor.shape[3]
    high, low = halves(inverse_z_table(blocks, length_z, scale))
    return pl.pallas_call(
        gather_kernel,
        grid=(length_y,),
        in_specs=[
            pl.BlockSpec((blocks, terms, 1, half, lanes), lambda y: (0, 0, y, 0, 0)),
            pl.BlockSpec((terms, 1, rows, length_z), lambda y: (0, y, 0, 0)),
            whole(high.shape, 1),
            whole(low.shape, 1),
        ],
        out_specs=pl.BlockSpec((1, rows, length_z), lambda y: (y, 0, 0)),
        out_shape=jax.ShapeDtypeStruct((length_y, rows, length_z), F32),
        compiler_params=params(1),
        cost_estimate=cost(6 * terms * length_y * rows * length_z * length_z, 4 * (data.size + factor.size)),
        name="gather_z",
    )(data, factor, jnp.asarray(high), jnp.asarray(low))


def mirror_kernel(in_ref, table_ref, out_ref, turned_ref):
    _, length_y, half, length_x = in_ref.shape
    high, low = split(in_ref[0].reshape(length_y * half, length_x))
    rest = in_ref[0].reshape(length_y * half, length_x) - high.astype(F32) - low.astype(F32)
    table = table_ref[...]
    turned = (dot(high, table) + dot(low, table)) + dot(rest.astype(BF16), table)
    turned_ref[...] = turned.reshape(length_y, half, length_x)
    for y in range(length_y):
        source = -y % length_y
        for s in range(half):
            row = -s % half
            out_ref[0, y, s : s + 1, :] = turned_ref[source, row : row + 1, :]


def mirror(multiplier):
    terms, length_y, width, length_x = multiplier.shape
    half = width // 2
    table = mirror_table(length_x)
    return pl.pallas_call(
        mirror_kernel,
        grid=(terms,),
        in_specs=[
            pl.BlockSpec((1, length_y, half, length_x), lambda t: (t, 0, 1, 0)),
            whole(table.shape, 1),
        ],
        out_specs=pl.BlockSpec((1, length_y, half, length_x), lambda t: (t, 0, 0, 0)),
        out_shape=jax.ShapeDtypeStruct((terms, length_y, half, length_x), F32),
        scratch_shapes=[pltpu.VMEM((length_y, half, length_x), F32)],
        compiler_params=params(1),
        cost_estimate=cost(6 * terms * length_y * half * length_x * length_x, 4 * multiplier.size),
        name="mirror",
    )(multiplier, jnp.asarray(table))


def flip(values, axis):
    return jnp.roll(jnp.flip(values, axis), 1, axis)


def padded_by_one(block, sides):
    for axis, dim in sides:
        count = lax.axis_size(axis)
        forward = [(i, i + 1) for i in range(count - 1)]
        backward = [(target, source) for source, target in forward]
        size = block.shape[dim]
        low = lax.ppermute(lax.slice_in_dim(block, size - 1, size, axis=dim), axis, forward)
        high = lax.ppermute(lax.slice_in_dim(block, 0, 1, axis=dim), axis, backward)
        yield dim, low, high


def heat_step(heat, perfuse):
    near = jnp.zeros_like(heat)
    for dim, low, high in padded_by_one(heat, (("term", 0), ("pencil", 1))):
        size = heat.shape[dim]
        near = near + jnp.concatenate([low, lax.slice_in_dim(heat, 0, size - 1, axis=dim)], axis=dim)
        near = near + jnp.concatenate([lax.slice_in_dim(heat, 1, size, axis=dim), high], axis=dim)
    deep = jnp.pad(heat, ((0, 0), (0, 0), (1, 1)))
    near = near + deep[:, :, 2:] + deep[:, :, :-2]
    return heat + DIFFUSION * (near - 6.0 * heat) - perfuse * heat


def on_device(
    present_acoustic,
    prior_acoustic,
    location_factor,
    spectral_multiplier,
    medium_kinds,
    organ_properties,
    thermal_increase,
):
    term_count = lax.axis_size("term")
    blocks = lax.axis_size("pencil")
    rows, length_y, length_z = present_acoustic.shape
    length_x = rows * blocks
    width = length_y // term_count
    half = length_z // blocks // 2
    terms = location_factor.shape[0]
    brick_start = lax.axis_index("term") * width
    scale = 2.0 / (length_x * length_y * length_z)

    def to_brick(values):
        return jnp.transpose(lax.dynamic_slice_in_dim(values, brick_start, width, 1), (1, 0, 2))

    other = lax.ppermute(mirror(spectral_multiplier), "pencil", [(p, blocks - 1 - p) for p in range(blocks)])
    lowest = spectral_multiplier[:, :, 0, :]
    lowest = lowest + lax.ppermute(
        flip(flip(lowest, 1), 2), "pencil", [(p, blocks - p) for p in range(1, blocks) if 2 * p != blocks]
    )
    lowest = jnp.transpose(lowest, (1, 0, 2))
    lowest = jnp.pad(lowest, ((0, 0), (0, -terms % 8), (0, 0)))
    factor = jnp.transpose(location_factor, (0, 2, 1, 3))

    def doubled(brick):
        sent = forward_z(brick, blocks)
        rows_spec = lax.all_to_all(sent, "pencil", 0, 0, tiled=True)
        part = forward_x(rows_spec.reshape(length_x, -1), width, half)
        spectrum = lax.all_gather(part, "term", axis=0, tiled=False)
        restored = spread(spectrum, lowest, spectral_multiplier, other, blocks, width, 0, terms)
        restored = lax.all_to_all(restored, "pencil", 0, 0, tiled=True)
        partial = gather(restored, factor, scale)
        return lax.psum_scatter(partial, "term", scatter_dimension=0, tiled=True)

    kinds = jnp.transpose(medium_kinds, (1, 0, 2))
    absorb, perfuse = [
        jnp.where(
            kinds == 0,
            organ_properties[0, at],
            jnp.where(kinds == 1, organ_properties[1, at], organ_properties[2, at]),
        )
        for at in range(2)
    ]
    heat = heat_step(jnp.transpose(thermal_increase, (1, 0, 2)), perfuse)

    previous = to_brick(prior_acoustic)
    current = to_brick(present_acoustic)
    dose = jnp.zeros(current.shape, F32)
    for _ in range(WAVE_STEPS):
        advanced = doubled(current) - previous
        dose = dose + advanced * advanced
        previous = current
        current = advanced
    source = absorb * dose
    heat = heat + source
    for _ in range(HEAT_STEPS - 1):
        heat = heat_step(heat, perfuse) + source
    return jnp.transpose(current, (1, 0, 2)), jnp.transpose(heat, (1, 0, 2))


def solution(mesh):
    return jax.shard_map(
        on_device,
        mesh=mesh,
        in_specs=(
            P("pencil", None, None),
            P("pencil", None, None),
            P("term", "pencil", None, None),
            P("term", None, "pencil", None),
            P("pencil", "term", None),
            P(),
            P("pencil", "term", None),
        ),
        out_specs=(P("pencil", "term", None), P("pencil", "term", None)),
        check_vma=False,
    )
```

```python
import functools
import math

import jax
import jax.numpy as jnp
import ml_dtypes
import numpy as np
from jax import lax
from jax.experimental import pallas as pl
from jax.experimental.pallas import tpu as pltpu
from jax.sharding import PartitionSpec as P

WAVE_STEPS = 2
HEAT_STEPS = 2
DIFFUSION = 0.125
VMEM_BYTES = 56 * 1024 * 1024
F32 = jnp.float32
BF16 = jnp.bfloat16


def halves(table):
    high = table.astype(ml_dtypes.bfloat16)
    low = (table - high.astype(np.float64)).astype(ml_dtypes.bfloat16)
    return high, low


def angles(left, right, length):
    return (np.outer(left, right) % length) * (2.0 * math.pi / length)


def slot_wavenumbers(blocks, length_z):
    width = length_z // blocks
    half = width // 2
    slots = np.concatenate([[half], np.arange(1, half)])
    starts = np.arange(blocks) * width
    return starts[:, None] + slots[None, :], starts


def forward_z_table(blocks, length_z):
    main, first = slot_wavenumbers(blocks, length_z)
    z = np.arange(length_z)
    theta = angles(z, main.reshape(-1), length_z).reshape(length_z, blocks, -1)
    real, imag = np.cos(theta), -np.sin(theta)
    for q in range(blocks // 2):
        real[:, q, 0], imag[:, q, 0] = -imag[:, q, 0].copy(), real[:, q, 0].copy()
    theta = angles(z, first, length_z)
    real0, imag0 = np.cos(theta), -np.sin(theta)
    for q in range(blocks // 2 + 1, blocks):
        real0[:, q], imag0[:, q] = imag0[:, q].copy(), -real0[:, q].copy()
    table = np.concatenate(
        [np.stack([real, imag], 2).reshape(length_z, -1), np.stack([real0, imag0], 2).reshape(length_z, -1)], axis=1
    )
    spare = -table.shape[1] % 128
    return np.pad(table, ((0, 0), (0, spare)))


def inverse_z_table(blocks, length_z, scale):
    main, first = slot_wavenumbers(blocks, length_z)
    z = np.arange(length_z)
    theta = angles(main.reshape(-1), z, length_z).reshape(blocks, -1, length_z)
    real, imag = np.cos(theta), -np.sin(theta)
    for p in range(blocks):
        middle = theta[p, 0]
        imag[p, 0] = np.cos(middle) if p < blocks // 2 else -np.sin(middle)
        lowest = angles(first[p : p + 1], z, length_z)[0]
        real[p, 0] = np.cos(lowest) if p <= blocks // 2 else -np.sin(lowest)
    return scale * np.concatenate([real.reshape(-1, length_z), imag.reshape(-1, length_z)], axis=0)


def forward_x_table(length_x):
    x = np.arange(length_x)
    theta = angles(x, x, length_x)
    return np.concatenate([np.cos(theta), np.sin(theta)], axis=1)


def inverse_x_table(blocks, length_x):
    x = np.arange(length_x)
    theta = angles(x, x, length_x).reshape(length_x, blocks, -1)
    cosine, sine = np.cos(theta), np.sin(theta)
    real_rows = np.stack([cosine, sine], axis=2).reshape(length_x, -1)
    imag_rows = np.stack([-sine, cosine], axis=2).reshape(length_x, -1)
    return np.concatenate([real_rows, imag_rows], axis=0)


def mirror_table(length):
    x = np.arange(length)
    table = np.zeros((length, length), ml_dtypes.bfloat16)
    table[x, (-x) % length] = 1
    return table


def turned_by(a, b, k, count, sign):
    if k == 0:
        return a, b
    if 4 * k == count:
        return (-b, a) if sign > 0 else (b, -a)
    angle = 2.0 * math.pi * k / count
    c, s = math.cos(angle), sign * math.sin(angle)
    if 8 * k == count or 8 * k == 3 * count:
        root = math.sqrt(0.5)
        sum_ab, less_ab = root * (a + b), root * (a - b)
        if c > 0:
            return (less_ab, sum_ab) if s > 0 else (sum_ab, -less_ab)
        return (-sum_ab, less_ab) if s > 0 else (-less_ab, -sum_ab)
    return c * a - s * b, c * b + s * a


def fourier(values, sign, wanted=None):
    count = len(values)
    wanted = range(count) if wanted is None else wanted
    if not wanted:
        return {}
    if count == 1:
        return {0: values[0]}
    if count % 2:
        out = {}
        for k in wanted:
            real, imag = values[0]
            for n in range(1, count):
                angle = 2.0 * math.pi * (k * n % count) / count
                c, s = math.cos(angle), sign * math.sin(angle)
                a, b = values[n]
                real, imag = real + (c * a - s * b), imag + (c * b + s * a)
            out[k] = (real, imag)
        return out
    half = count // 2
    out = {}
    even = [k // 2 for k in wanted if k % 2 == 0]
    odd = [k // 2 for k in wanted if k % 2]
    if even:
        added = [(values[n][0] + values[n + half][0], values[n][1] + values[n + half][1]) for n in range(half)]
        for k, value in fourier(added, sign, even).items():
            out[2 * k] = value
    if odd:
        less = [
            turned_by(values[n][0] - values[n + half][0], values[n][1] - values[n + half][1], n, count, sign)
            for n in range(half)
        ]
        for k, value in fourier(less, sign, odd).items():
            out[2 * k + 1] = value
    return out


def split(values):
    high = values.astype(BF16)
    return high, (values - high.astype(F32)).astype(BF16)


def dot(left, right):
    return jnp.dot(left, right, preferred_element_type=F32)


def dot_across(left, right):
    return lax.dot_general(left, right, (((1,), (1,)), ((), ())), preferred_element_type=F32)


def dot_three(high, low, table_high, table_low):
    return dot(high, table_high) + (dot(low, table_high) + dot(high, table_low))


def params(count=0):
    return pltpu.CompilerParams(vmem_limit_bytes=VMEM_BYTES, dimension_semantics=("arbitrary",) * count)


def cost(flops, moved):
    return pl.CostEstimate(flops=int(flops), bytes_accessed=int(moved), transcendentals=0)


def whole(shape, grid_rank):
    return pl.BlockSpec(shape, lambda *_: (0,) * len(shape), pipeline_mode=pl.Buffered(1)) if grid_rank else pl.BlockSpec(
        memory_space=pltpu.VMEM
    )


def forward_z_kernel(brick_ref, high_ref, low_ref, first_high_ref, first_low_ref, out_ref):
    width, rows, length_z = brick_ref.shape
    blocks = out_ref.shape[0]
    main = length_z // blocks
    high, low = split(brick_ref[...].reshape(width * rows, length_z))
    result = dot_three(high, low, high_ref[...], low_ref[...])
    first = (
        dot_across(first_high_ref[...], high)
        + (dot_across(first_low_ref[...], high) + dot_across(first_high_ref[...], low))
    )
    out_ref[:, rows:, :] = jnp.zeros_like(out_ref[:, rows:, :])
    for q in range(blocks):
        for w in range(width):
            out_ref[q, :rows, w * main : (w + 1) * main] = result[w * rows : (w + 1) * rows, q * main : (q + 1) * main]
            for c in range(2):
                row = rows + c * width + w
                out_ref[q, row : row + 1, :rows] = first[2 * q + c : 2 * q + c + 1, w * rows : (w + 1) * rows]


def forward_z(brick, blocks):
    width, rows, length_z = brick.shape
    lanes = max(width * length_z // blocks, rows)
    table = forward_z_table(blocks, length_z)
    high, low = halves(table[:, :length_z])
    first_high, first_low = halves(table[:, length_z : length_z + 2 * blocks].T)
    tables = [jnp.asarray(each) for each in (high, low, first_high, first_low)]
    return pl.pallas_call(
        forward_z_kernel,
        out_shape=jax.ShapeDtypeStruct((blocks, rows + 2 * width + (-2 * width) % 8, lanes), F32),
        compiler_params=params(),
        cost_estimate=cost(6 * width * rows * length_z * length_z, 16 * width * rows * length_z),
        name="forward_z",
    )(brick, *tables)


def forward_x_kernel(data_ref, high_ref, low_ref, out_ref, *, width, half, rows):
    blocks = data_ref.shape[0]
    length_x = blocks * rows
    main = width * 2 * half
    turned = data_ref[:, :rows, :main].reshape(length_x, main).T
    first = jnp.concatenate([data_ref[q, rows:, :rows] for q in range(blocks)], axis=1)
    high, low = split(jnp.concatenate([turned, first], axis=0))
    both = dot_three(high, low, high_ref[...], low_ref[...])
    by_cos, by_sin = both[:, :length_x], both[:, length_x:]
    for w in range(width):
        re, im = w * 2 * half, w * 2 * half + half
        out_ref[re : re + half] = by_cos[re : re + half] + by_sin[im : im + half]
        out_ref[im : im + half] = by_cos[im : im + half] - by_sin[re : re + half]
    re, im, end = main, main + width, main + 2 * width
    out_ref[re:im] = by_cos[re:im] + by_sin[im:end]
    out_ref[im:end] = by_cos[im:end] - by_sin[re:im]
    if end < out_ref.shape[0]:
        out_ref[end:] = jnp.zeros_like(out_ref[end:])


def forward_x(data, width, half, rows):
    blocks = data.shape[0]
    length_x = blocks * rows
    out_rows = width * 2 * half + data.shape[1] - rows
    high, low = halves(forward_x_table(length_x))
    return pl.pallas_call(
        functools.partial(forward_x_kernel, width=width, half=half, rows=rows),
        out_shape=jax.ShapeDtypeStruct((out_rows, length_x), F32),
        compiler_params=params(),
        cost_estimate=cost(12 * out_rows * length_x * length_x, 8 * out_rows * length_x),
        name="forward_x",
    )(data, jnp.asarray(high), jnp.asarray(low))


def spread_kernel(*refs, groups, group):
    f_refs = refs[:groups]
    (
        first_ref, own_ref, other_ref, high_ref, low_ref, out_ref,
        fk_ref, edge_ref, edge_out_ref, u_ref, u_high_ref, u_low_ref,
    ) = refs[groups:]
    length_y, _, half, length_x = fk_ref.shape
    lanes_out = out_ref.shape[-1]
    rows_x = lanes_out // 2
    count_y = out_ref.shape[2]
    wide = count_y // f_refs[0].shape[0]
    width = wide * groups
    main = wide * 2 * half
    step = pl.program_id(0)
    tiles = [slice(at, at + 128) for at in range(0, length_x, 128)]
    wanted = [y for y in range(length_y) if y % width // wide == group]

    def place(y):
        return f_refs[y % width // wide], y // width, y % wide

    @pl.when(step == 0)
    def _():
        @pl.loop(0, half // 8)
        def _(tile):
            for lanes in tiles:
                values = []
                for y in range(length_y):
                    ref, at, w = place(y)
                    row = w * 2 * half + tile * 8
                    values.append((
                        ref[at, pl.ds(pl.multiple_of(row, 8), 8), lanes],
                        ref[at, pl.ds(pl.multiple_of(row + half, 8), 8), lanes],
                    ))
                values = fourier(values, -1)
                at = pl.ds(pl.multiple_of(tile * 8, 8), 8)
                for y in range(length_y):
                    fk_ref[y, 0, at, lanes] = values[y][0]
                    fk_ref[y, 1, at, lanes] = values[y][1]

        for index, lanes in enumerate(tiles):
            values = []
            for y in range(length_y):
                ref, at, w = place(y)
                values.append((
                    ref[at, main + w : main + w + 1, lanes],
                    ref[at, main + wide + w : main + wide + w + 1, lanes],
                ))
            values = fourier(values, -1)
            factors = [first_ref[y, :, lanes] for y in range(length_y)]
            values = [(factors[y] * values[y][0], factors[y] * values[y][1]) for y in range(length_y)]
            values = fourier(values, 1, wanted)
            for n, y in enumerate(wanted):
                edge_ref[n, :, index * 128 : index * 128 + 128] = values[y][0]
                edge_ref[n, :, length_x + index * 128 : length_x + index * 128 + 128] = values[y][1]
        high, low = split(edge_ref[...].reshape(-1, 2 * length_x))
        edge_out_ref[...] = dot_three(high, low, high_ref[...], low_ref[...])

    row_index = lax.broadcasted_iota(jnp.int32, (8, 128), 0)

    @pl.loop(0, half // 8)
    def _(tile):
        at = pl.ds(pl.multiple_of(tile * 8, 8), 8)
        swapped = jnp.logical_and(row_index == 0, tile == 0)
        for index, lanes in enumerate(tiles):
            values = []
            for y in range(length_y):
                own = jnp.where(swapped, own_ref[0, y, half : half + 1, lanes], own_ref[0, y, at, lanes])
                factor = own + other_ref[0, y, at, lanes]
                values.append((factor * fk_ref[y, 0, at, lanes], factor * fk_ref[y, 1, at, lanes]))
            values = fourier(values, 1, wanted)
            for n, y in enumerate(wanted):
                rows = pl.ds(pl.multiple_of(n * half + tile * 8, 8), 8)
                u_ref[rows, index * 128 : index * 128 + 128] = values[y][0]
                u_ref[rows, length_x + index * 128 : length_x + index * 128 + 128] = values[y][1]

    @pl.loop(0, count_y * half // 64)
    def _(part):
        rows = pl.ds(pl.multiple_of(part * 64, 64), 64)
        high, low = split(u_ref[rows, :])
        u_high_ref[rows, :] = high
        u_low_ref[rows, :] = low

    lane_index = lax.broadcasted_iota(jnp.int32, (8, lanes_out), 1)
    row_index = lax.broadcasted_iota(jnp.int32, (8, lanes_out), 0)
    swapped = jnp.logical_and(row_index == 0, lane_index < rows_x)
    count = 256 // lanes_out
    for part in range(2 * length_x // 256):
        cols = slice(part * 256, part * 256 + 256)
        result = dot_three(u_high_ref[...], u_low_ref[...], high_ref[:, cols], low_ref[:, cols])
        edges = [edge_out_ref[pl.ds(n * first_ref.shape[1] + step, 1), cols] for n in range(count_y)]
        for k in range(count):
            q = part * count + k
            inside = slice(k * lanes_out, (k + 1) * lanes_out)
            piece = result[:, inside]
            for n in range(count_y):
                top = piece[n * half : n * half + 8]
                out_ref[q, 0, n, :8, :] = jnp.where(swapped, edges[n][:, inside], top)
                out_ref[q, 0, n, 8:, :] = piece[n * half + 8 : (n + 1) * half]


def spread(parts, first, own, other, blocks, group):
    terms, length_y, _, length_x = own.shape
    half = other.shape[2]
    groups = len(parts)
    count_y = length_y // groups
    rows_x = length_x // blocks
    high, low = halves(inverse_x_table(blocks, length_x))
    high, low = jnp.asarray(high), jnp.asarray(low)
    rows = count_y * half
    return pl.pallas_call(
        functools.partial(spread_kernel, groups=groups, group=group),
        grid=(terms,),
        in_specs=[whole(part.shape, 1) for part in parts] + [
            whole(first.shape, 1),
            pl.BlockSpec((1, length_y, half + 8, length_x), lambda t: (t, 0, 0, 0)),
            pl.BlockSpec((1, length_y, half, length_x), lambda t: (t, 0, 0, 0)),
            whole(high.shape, 1),
            whole(low.shape, 1),
        ],
        out_specs=pl.BlockSpec((blocks, 1, count_y, half, 2 * rows_x), lambda t: (0, t, 0, 0, 0)),
        out_shape=jax.ShapeDtypeStruct((blocks, terms, count_y, half, 2 * rows_x), F32),
        scratch_shapes=[
            pltpu.VMEM((length_y, 2, half, length_x), F32),
            pltpu.VMEM((count_y, first.shape[1], 2 * length_x), F32),
            pltpu.VMEM((count_y * first.shape[1], 2 * length_x), F32),
            pltpu.VMEM((rows, 2 * length_x), F32),
            pltpu.VMEM((rows, 2 * length_x), BF16),
            pltpu.VMEM((rows, 2 * length_x), BF16),
        ],
        compiler_params=params(1),
        cost_estimate=cost(terms * 24 * rows * length_x * length_x, terms * 16 * rows * length_x),
        name="spread",
    )(*parts, first, own, other, high, low)


def gather_kernel(data_ref, factor_ref, high_ref, low_ref, out_ref):
    blocks, terms, _, half, lanes = data_ref.shape
    rows = lanes // 2
    parts = []
    for t in range(terms):
        turned = data_ref[:, t, 0].reshape(blocks * half, lanes).T
        parts.append(jnp.concatenate([turned[:rows], turned[rows:]], axis=1))
    high, low = split(jnp.concatenate(parts, axis=0))
    fields = dot_three(high, low, high_ref[...], low_ref[...])
    total = factor_ref[0, 0] * fields[:rows]
    for t in range(1, terms):
        total = total + factor_ref[t, 0] * fields[t * rows : (t + 1) * rows]
    out_ref[0] = total


def gather(data, factor, scale, width, groups, group):
    blocks, terms, count_y, half, lanes = data.shape
    rows, length_z = factor.shape[2], factor.shape[3]
    wide = width // groups
    high, low = halves(inverse_z_table(blocks, length_z, scale))
    return pl.pallas_call(
        gather_kernel,
        grid=(count_y,),
        in_specs=[
            pl.BlockSpec((blocks, terms, 1, half, lanes), lambda n: (0, 0, n, 0, 0)),
            pl.BlockSpec((terms, 1, rows, length_z), lambda n: (0, n // wide * width + group * wide + n % wide, 0, 0)),
            whole(high.shape, 1),
            whole(low.shape, 1),
        ],
        out_specs=pl.BlockSpec((1, rows, length_z), lambda n: (n, 0, 0)),
        out_shape=jax.ShapeDtypeStruct((count_y, rows, length_z), F32),
        compiler_params=params(1),
        cost_estimate=cost(6 * terms * count_y * rows * length_z * length_z, 8 * data.size),
        name="gather_z",
    )(data, factor, jnp.asarray(high), jnp.asarray(low))


def mirror_kernel(in_ref, table_ref, out_ref, turned_ref):
    _, length_y, half, length_x = in_ref.shape
    high, low = split(in_ref[0].reshape(length_y * half, length_x))
    rest = in_ref[0].reshape(length_y * half, length_x) - high.astype(F32) - low.astype(F32)
    table = table_ref[...]
    turned = (dot(high, table) + dot(low, table)) + dot(rest.astype(BF16), table)
    turned_ref[...] = turned.reshape(length_y, half, length_x)
    for y in range(length_y):
        source = -y % length_y
        for s in range(half):
            row = -s % half
            out_ref[0, y, s : s + 1, :] = turned_ref[source, row : row + 1, :]


def mirror(multiplier):
    terms, length_y, width, length_x = multiplier.shape
    half = width // 2
    table = mirror_table(length_x)
    return pl.pallas_call(
        mirror_kernel,
        grid=(terms,),
        in_specs=[
            pl.BlockSpec((1, length_y, half, length_x), lambda t: (t, 0, 1, 0)),
            whole(table.shape, 1),
        ],
        out_specs=pl.BlockSpec((1, length_y, half, length_x), lambda t: (t, 0, 0, 0)),
        out_shape=jax.ShapeDtypeStruct((terms, length_y, half, length_x), F32),
        scratch_shapes=[pltpu.VMEM((length_y, half, length_x), F32)],
        compiler_params=params(1),
        cost_estimate=cost(6 * terms * length_y * half * length_x * length_x, 4 * multiplier.size),
        name="mirror",
    )(multiplier, jnp.asarray(table))


def flip(values, axis):
    return jnp.roll(jnp.flip(values, axis), 1, axis)


def padded_by_one(block, sides):
    for axis, dim in sides:
        count = lax.axis_size(axis)
        forward = [(i, i + 1) for i in range(count - 1)]
        backward = [(target, source) for source, target in forward]
        size = block.shape[dim]
        low = lax.ppermute(lax.slice_in_dim(block, size - 1, size, axis=dim), axis, forward)
        high = lax.ppermute(lax.slice_in_dim(block, 0, 1, axis=dim), axis, backward)
        yield dim, low, high


def heat_step(heat, perfuse):
    near = jnp.zeros_like(heat)
    for dim, low, high in padded_by_one(heat, (("term", 0), ("pencil", 1))):
        size = heat.shape[dim]
        near = near + jnp.concatenate([low, lax.slice_in_dim(heat, 0, size - 1, axis=dim)], axis=dim)
        near = near + jnp.concatenate([lax.slice_in_dim(heat, 1, size, axis=dim), high], axis=dim)
    deep = jnp.pad(heat, ((0, 0), (0, 0), (1, 1)))
    near = near + deep[:, :, 2:] + deep[:, :, :-2]
    return heat + DIFFUSION * (near - 6.0 * heat) - perfuse * heat


def on_device(
    present_acoustic,
    prior_acoustic,
    location_factor,
    spectral_multiplier,
    medium_kinds,
    organ_properties,
    thermal_increase,
):
    term_count = lax.axis_size("term")
    blocks = lax.axis_size("pencil")
    rows, length_y, length_z = present_acoustic.shape
    length_x = rows * blocks
    width = length_y // term_count
    half = length_z // blocks // 2
    terms = location_factor.shape[0]
    brick_start = lax.axis_index("term") * width
    scale = 2.0 / (length_x * length_y * length_z)

    groups = 2 if width % 4 == 0 else 1
    wide = width // groups

    def to_brick(values):
        brick = jnp.transpose(lax.dynamic_slice_in_dim(values, brick_start, width, 1), (1, 0, 2))
        return [brick[g * wide : (g + 1) * wide] for g in range(groups)]

    def rows_to_columns(brick):
        return lax.all_to_all(forward_z(brick, blocks), "pencil", 0, 0, tiled=True)

    current = to_brick(present_acoustic)
    sent = [rows_to_columns(part) for part in current]
    mirrored = mirror(spectral_multiplier)
    *sent, mirrored = lax.optimization_barrier((*sent, mirrored))
    other = lax.ppermute(mirrored, "pencil", [(p, blocks - 1 - p) for p in range(blocks)])
    lowest = spectral_multiplier[:, :, 0, :]
    lowest = lowest + lax.ppermute(
        flip(flip(lowest, 1), 2), "pencil", [(p, blocks - p) for p in range(1, blocks) if 2 * p != blocks]
    )
    lowest = jnp.transpose(lowest, (1, 0, 2))
    lowest = jnp.pad(lowest, ((0, 0), (0, -terms % 8), (0, 0)))
    factor = jnp.transpose(location_factor, (0, 2, 1, 3))

    def doubled(sent):
        parts = [lax.all_gather(forward_x(each, wide, half, rows), "term", axis=0, tiled=False) for each in sent]
        bricks = []
        for g in range(groups):
            restored = spread(parts, lowest, spectral_multiplier, other, blocks, g)
            restored = lax.all_to_all(restored, "pencil", 0, 0, tiled=True)
            partial = gather(restored, factor, scale, width, groups, g)
            bricks.append(lax.psum_scatter(partial, "term", scatter_dimension=0, tiled=True))
        return bricks

    kinds = jnp.transpose(medium_kinds, (1, 0, 2))
    absorb, perfuse = [
        jnp.where(
            kinds == 0,
            organ_properties[0, at],
            jnp.where(kinds == 1, organ_properties[1, at], organ_properties[2, at]),
        )
        for at in range(2)
    ]
    heat = heat_step(jnp.transpose(thermal_increase, (1, 0, 2)), perfuse)

    previous = to_brick(prior_acoustic)
    dose = [jnp.zeros(part.shape, F32) for part in current]
    for turn in range(WAVE_STEPS):
        if turn:
            sent = [rows_to_columns(part) for part in current]
        advanced = [fresh - old for fresh, old in zip(doubled(sent), previous)]
        dose = [total + fresh * fresh for total, fresh in zip(dose, advanced)]
        previous, current = current, advanced
    current = jnp.concatenate(current, axis=0)
    dose = jnp.concatenate(dose, axis=0)
    source = absorb * dose
    heat = heat + source
    for _ in range(HEAT_STEPS - 1):
        heat = heat_step(heat, perfuse) + source
    return jnp.transpose(current, (1, 0, 2)), jnp.transpose(heat, (1, 0, 2))


def solution(mesh):
    return jax.shard_map(
        on_device,
        mesh=mesh,
        in_specs=(
            P("pencil", None, None),
            P("pencil", None, None),
            P("term", "pencil", None, None),
            P("term", None, "pencil", None),
            P("pencil", "term", None),
            P(),
            P("pencil", "term", None),
        ),
        out_specs=(P("pencil", "term", None), P("pencil", "term", None)),
        check_vma=False,
    )
```

```python
import functools
import math

import jax
import jax.numpy as jnp
import ml_dtypes
import numpy as np
from jax import lax
from jax.experimental import pallas as pl
from jax.experimental.pallas import tpu as pltpu
from jax.sharding import PartitionSpec as P

WAVE_STEPS = 2
HEAT_STEPS = 2
DIFFUSION = 0.125
VMEM_BYTES = 56 * 1024 * 1024
F32 = jnp.float32
BF16 = jnp.bfloat16


def halves(table):
    high = table.astype(ml_dtypes.bfloat16)
    low = (table - high.astype(np.float64)).astype(ml_dtypes.bfloat16)
    return high, low


def angles(left, right, length):
    return (np.outer(left, right) % length) * (2.0 * math.pi / length)


def slot_wavenumbers(blocks, length_z):
    width = length_z // blocks
    half = width // 2
    slots = np.concatenate([[half], np.arange(1, half)])
    starts = np.arange(blocks) * width
    return starts[:, None] + slots[None, :], starts


def forward_z_table(blocks, length_z):
    main, first = slot_wavenumbers(blocks, length_z)
    z = np.arange(length_z)
    theta = angles(z, main.reshape(-1), length_z).reshape(length_z, blocks, -1)
    real, imag = np.cos(theta), -np.sin(theta)
    for q in range(blocks // 2):
        real[:, q, 0], imag[:, q, 0] = -imag[:, q, 0].copy(), real[:, q, 0].copy()
    theta = angles(z, first, length_z)
    real0, imag0 = np.cos(theta), -np.sin(theta)
    for q in range(blocks // 2 + 1, blocks):
        real0[:, q], imag0[:, q] = imag0[:, q].copy(), -real0[:, q].copy()
    table = np.concatenate(
        [np.stack([real, imag], 2).reshape(length_z, -1), np.stack([real0, imag0], 2).reshape(length_z, -1)], axis=1
    )
    spare = -table.shape[1] % 128
    return np.pad(table, ((0, 0), (0, spare)))


def inverse_z_table(blocks, length_z, scale):
    main, first = slot_wavenumbers(blocks, length_z)
    z = np.arange(length_z)
    theta = angles(main.reshape(-1), z, length_z).reshape(blocks, -1, length_z)
    real, imag = np.cos(theta), -np.sin(theta)
    for p in range(blocks):
        middle = theta[p, 0]
        imag[p, 0] = np.cos(middle) if p < blocks // 2 else -np.sin(middle)
        lowest = angles(first[p : p + 1], z, length_z)[0]
        real[p, 0] = np.cos(lowest) if p <= blocks // 2 else -np.sin(lowest)
    return scale * np.concatenate([real.reshape(-1, length_z), imag.reshape(-1, length_z)], axis=0)


def forward_x_table(length_x):
    x = np.arange(length_x)
    theta = angles(x, x, length_x)
    return np.concatenate([np.cos(theta), np.sin(theta)], axis=1)


def inverse_x_table(blocks, length_x):
    x = np.arange(length_x)
    theta = angles(x, x, length_x).reshape(length_x, blocks, -1)
    cosine, sine = np.cos(theta), np.sin(theta)
    real_rows = np.stack([cosine, sine], axis=2).reshape(length_x, -1)
    imag_rows = np.stack([-sine, cosine], axis=2).reshape(length_x, -1)
    return np.concatenate([real_rows, imag_rows], axis=0)


def mirror_table(length):
    x = np.arange(length)
    table = np.zeros((length, length), ml_dtypes.bfloat16)
    table[x, (-x) % length] = 1
    return table


def turned_by(a, b, k, count, sign):
    if k == 0:
        return a, b
    if 4 * k == count:
        return (-b, a) if sign > 0 else (b, -a)
    angle = 2.0 * math.pi * k / count
    c, s = math.cos(angle), sign * math.sin(angle)
    if 8 * k == count or 8 * k == 3 * count:
        root = math.sqrt(0.5)
        sum_ab, less_ab = root * (a + b), root * (a - b)
        if c > 0:
            return (less_ab, sum_ab) if s > 0 else (sum_ab, -less_ab)
        return (-sum_ab, less_ab) if s > 0 else (-less_ab, -sum_ab)
    return c * a - s * b, c * b + s * a


def fourier(values, sign, wanted=None):
    count = len(values)
    wanted = range(count) if wanted is None else wanted
    if not wanted:
        return {}
    if count == 1:
        return {0: values[0]}
    if count % 2:
        out = {}
        for k in wanted:
            real, imag = values[0]
            for n in range(1, count):
                angle = 2.0 * math.pi * (k * n % count) / count
                c, s = math.cos(angle), sign * math.sin(angle)
                a, b = values[n]
                real, imag = real + (c * a - s * b), imag + (c * b + s * a)
            out[k] = (real, imag)
        return out
    half = count // 2
    out = {}
    even = [k // 2 for k in wanted if k % 2 == 0]
    odd = [k // 2 for k in wanted if k % 2]
    if even:
        added = [(values[n][0] + values[n + half][0], values[n][1] + values[n + half][1]) for n in range(half)]
        for k, value in fourier(added, sign, even).items():
            out[2 * k] = value
    if odd:
        less = [
            turned_by(values[n][0] - values[n + half][0], values[n][1] - values[n + half][1], n, count, sign)
            for n in range(half)
        ]
        for k, value in fourier(less, sign, odd).items():
            out[2 * k + 1] = value
    return out


def split(values):
    high = values.astype(BF16)
    return high, (values - high.astype(F32)).astype(BF16)


def dot(left, right):
    return jnp.dot(left, right, preferred_element_type=F32)


def dot_across(left, right):
    return lax.dot_general(left, right, (((1,), (1,)), ((), ())), preferred_element_type=F32)


def dot_three(high, low, table_high, table_low):
    return dot(high, table_high) + (dot(low, table_high) + dot(high, table_low))


def params(count=0):
    return pltpu.CompilerParams(vmem_limit_bytes=VMEM_BYTES, dimension_semantics=("arbitrary",) * count)


def cost(flops, moved):
    return pl.CostEstimate(flops=int(flops), bytes_accessed=int(moved), transcendentals=0)


def whole(shape, grid_rank):
    return pl.BlockSpec(shape, lambda *_: (0,) * len(shape), pipeline_mode=pl.Buffered(1)) if grid_rank else pl.BlockSpec(
        memory_space=pltpu.VMEM
    )


def forward_z_kernel(*refs, inputs):
    fresh_ref, *older = refs[:inputs]
    high_ref, low_ref, first_high_ref, first_low_ref, out_ref, *state = refs[inputs:]
    width, rows, length_z = fresh_ref.shape
    blocks = out_ref.shape[0]
    main = length_z // blocks
    brick = fresh_ref[...]
    if older:
        brick = brick - older[0][...]
        state[0][...] = brick
        dose = brick * brick
        state[1][...] = dose + older[1][...] if len(older) > 1 else dose
    high, low = split(brick.reshape(width * rows, length_z))
    result = dot_three(high, low, high_ref[...], low_ref[...])
    first = (
        dot_across(first_high_ref[...], high)
        + (dot_across(first_low_ref[...], high) + dot_across(first_high_ref[...], low))
    )
    out_ref[:, rows:, :] = jnp.zeros_like(out_ref[:, rows:, :])
    for q in range(blocks):
        for w in range(width):
            out_ref[q, :rows, w * main : (w + 1) * main] = result[w * rows : (w + 1) * rows, q * main : (q + 1) * main]
            for c in range(2):
                row = rows + c * width + w
                out_ref[q, row : row + 1, :rows] = first[2 * q + c : 2 * q + c + 1, w * rows : (w + 1) * rows]


def forward_z(bricks, blocks):
    width, rows, length_z = bricks[0].shape
    lanes = max(width * length_z // blocks, rows)
    table = forward_z_table(blocks, length_z)
    high, low = halves(table[:, :length_z])
    first_high, first_low = halves(table[:, length_z : length_z + 2 * blocks].T)
    tables = [jnp.asarray(each) for each in (high, low, first_high, first_low)]
    out = [jax.ShapeDtypeStruct((blocks, rows + 2 * width + (-2 * width) % 8, lanes), F32)]
    if len(bricks) > 1:
        out += [jax.ShapeDtypeStruct(bricks[0].shape, F32)] * 2
    return pl.pallas_call(
        functools.partial(forward_z_kernel, inputs=len(bricks)),
        out_shape=out,
        compiler_params=params(),
        cost_estimate=cost(6 * width * rows * length_z * length_z, 16 * width * rows * length_z),
        name="forward_z",
    )(*bricks, *tables)


def forward_x_kernel(data_ref, high_ref, low_ref, out_ref, *, width, half, rows):
    blocks = data_ref.shape[0]
    length_x = blocks * rows
    main = width * 2 * half
    turned = data_ref[:, :rows, :main].reshape(length_x, main).T
    first = jnp.concatenate([data_ref[q, rows:, :rows] for q in range(blocks)], axis=1)
    high, low = split(jnp.concatenate([turned, first], axis=0))
    both = dot_three(high, low, high_ref[...], low_ref[...])
    by_cos, by_sin = both[:, :length_x], both[:, length_x:]
    for w in range(width):
        re, im = w * 2 * half, w * 2 * half + half
        out_ref[re : re + half] = by_cos[re : re + half] + by_sin[im : im + half]
        out_ref[im : im + half] = by_cos[im : im + half] - by_sin[re : re + half]
    re, im, end = main, main + width, main + 2 * width
    out_ref[re:im] = by_cos[re:im] + by_sin[im:end]
    out_ref[im:end] = by_cos[im:end] - by_sin[re:im]
    if end < out_ref.shape[0]:
        out_ref[end:] = jnp.zeros_like(out_ref[end:])


def forward_x(data, width, half, rows):
    blocks = data.shape[0]
    length_x = blocks * rows
    out_rows = width * 2 * half + data.shape[1] - rows
    high, low = halves(forward_x_table(length_x))
    return pl.pallas_call(
        functools.partial(forward_x_kernel, width=width, half=half, rows=rows),
        out_shape=jax.ShapeDtypeStruct((out_rows, length_x), F32),
        compiler_params=params(),
        cost_estimate=cost(12 * out_rows * length_x * length_x, 8 * out_rows * length_x),
        name="forward_x",
    )(data, jnp.asarray(high), jnp.asarray(low))


def spread_kernel(*refs, spans, counts, group, pieces, first_term):
    parts, at = [], 0
    for count in counts:
        parts.append(refs[at : at + count])
        at += count
    me_ref, first_ref, own_ref = refs[at : at + 3]
    others = refs[at + 3 : at + 3 + len(pieces)]
    (
        high_ref, low_ref, out_ref,
        fk_ref, edge_in_ref, edge_ref, edge_out_ref, u_ref, u_high_ref, u_low_ref,
    ) = refs[at + 3 + len(pieces) :]
    length_y, _, half, length_x = fk_ref.shape
    lanes_out = out_ref.shape[-1]
    rows_x = lanes_out // 2
    count_y = out_ref.shape[2]
    width = spans[-1][1]
    holders = length_y // width
    step = pl.program_id(0)
    tiles = [slice(at, at + 128) for at in range(0, length_x, 128)]
    wanted = [y for y in range(length_y) if group[0] <= y % width < group[1]]

    @pl.when(step == 0)
    def _():
        for part, (start, end) in zip(parts, spans):
            wide = end - start
            for d in range(holders):
                if len(part) == 1:
                    source, holder = part[0].at[d], d
                else:
                    source, holder = part[d], lax.rem(me_ref[0] + d, holders)
                for w in range(wide):
                    y = holder * width + start + w
                    fk_ref[y, 0] = source[w * 2 * half : w * 2 * half + half]
                    fk_ref[y, 1] = source[w * 2 * half + half : (w + 1) * 2 * half]
                    row = wide * 2 * half + w
                    edge_in_ref[y, :1] = source[row : row + 1]
                    edge_in_ref[y, 1:2] = source[row + wide : row + wide + 1]

        @pl.loop(0, half // 8)
        def _(tile):
            at = pl.ds(pl.multiple_of(tile * 8, 8), 8)
            for lanes in tiles:
                values = [(fk_ref[y, 0, at, lanes], fk_ref[y, 1, at, lanes]) for y in range(length_y)]
                values = fourier(values, -1)
                for y in range(length_y):
                    fk_ref[y, 0, at, lanes] = values[y][0]
                    fk_ref[y, 1, at, lanes] = values[y][1]

        for index, lanes in enumerate(tiles):
            values = [(edge_in_ref[y, :1, lanes], edge_in_ref[y, 1:2, lanes]) for y in range(length_y)]
            values = fourier(values, -1)
            factors = [first_ref[y, :, lanes] for y in range(length_y)]
            values = [(factors[y] * values[y][0], factors[y] * values[y][1]) for y in range(length_y)]
            values = fourier(values, 1, wanted)
            for n, y in enumerate(wanted):
                edge_ref[n, :, index * 128 : index * 128 + 128] = values[y][0]
                edge_ref[n, :, length_x + index * 128 : length_x + index * 128 + 128] = values[y][1]
        high, low = split(edge_ref[...].reshape(-1, 2 * length_x))
        edge_out_ref[...] = dot_three(high, low, high_ref[...], low_ref[...])

    row_index = lax.broadcasted_iota(jnp.int32, (8, 128), 0)

    def weigh(other_ref):
        @pl.loop(0, half // 8)
        def _(tile):
            at = pl.ds(pl.multiple_of(tile * 8, 8), 8)
            swapped = jnp.logical_and(row_index == 0, tile == 0)
            for index, lanes in enumerate(tiles):
                values = []
                for y in range(length_y):
                    own = jnp.where(swapped, own_ref[0, y, half : half + 1, lanes], own_ref[0, y, at, lanes])
                    factor = own + other_ref[0, y, at, lanes]
                    values.append((factor * fk_ref[y, 0, at, lanes], factor * fk_ref[y, 1, at, lanes]))
                values = fourier(values, 1, wanted)
                for n, y in enumerate(wanted):
                    rows = pl.ds(pl.multiple_of(n * half + tile * 8, 8), 8)
                    u_ref[rows, index * 128 : index * 128 + 128] = values[y][0]
                    u_ref[rows, length_x + index * 128 : length_x + index * 128 + 128] = values[y][1]

    if len(others) == 1:
        weigh(others[0])
    else:
        for other_ref, (start, end) in zip(others, pieces):
            pl.when(jnp.logical_and(step >= start, step < end))(functools.partial(weigh, other_ref))

    @pl.loop(0, count_y * half // 64)
    def _(part):
        rows = pl.ds(pl.multiple_of(part * 64, 64), 64)
        high, low = split(u_ref[rows, :])
        u_high_ref[rows, :] = high
        u_low_ref[rows, :] = low

    lane_index = lax.broadcasted_iota(jnp.int32, (8, lanes_out), 1)
    row_index = lax.broadcasted_iota(jnp.int32, (8, lanes_out), 0)
    swapped = jnp.logical_and(row_index == 0, lane_index < rows_x)
    count = 256 // lanes_out
    for part in range(2 * length_x // 256):
        cols = slice(part * 256, part * 256 + 256)
        result = dot_three(u_high_ref[...], u_low_ref[...], high_ref[:, cols], low_ref[:, cols])
        edges = [edge_out_ref[pl.ds(n * first_ref.shape[1] + step + first_term, 1), cols] for n in range(count_y)]
        for k in range(count):
            q = part * count + k
            inside = slice(k * lanes_out, (k + 1) * lanes_out)
            piece = result[:, inside]
            for n in range(count_y):
                top = piece[n * half : n * half + 8]
                out_ref[q, 0, n, :8, :] = jnp.where(swapped, edges[n][:, inside], top)
                out_ref[q, 0, n, 8:, :] = piece[n * half + 8 : (n + 1) * half]


def spread(parts, spans, me, first, own, others, blocks, group, chosen):
    _, length_y, _, length_x = own.shape
    half = own.shape[2] // 2
    first_term, end_term = chosen
    terms = end_term - first_term
    count_y = length_y // spans[-1][1] * (group[1] - group[0])
    rows_x = length_x // blocks
    high, low = halves(inverse_x_table(blocks, length_x))
    high, low = jnp.asarray(high), jnp.asarray(low)
    rows = count_y * half
    others = [each for each in others if each[0] < end_term and each[1] > first_term]

    def piece_spec(start, end):
        return pl.BlockSpec(
            (1, length_y, half, length_x), lambda t: (jnp.clip(t + first_term - start, 0, end - start - 1), 0, 0, 0)
        )

    return pl.pallas_call(
        functools.partial(
            spread_kernel, spans=spans, counts=[len(part) for part in parts], group=group, first_term=first_term,
            pieces=[(start - first_term, end - first_term) for start, end, _ in others],
        ),
        grid=(terms,),
        in_specs=[whole(array.shape, 1) for part in parts for array in part] + [
            pl.BlockSpec(memory_space=pltpu.SMEM),
            whole(first.shape, 1),
            pl.BlockSpec((1, length_y, half + 8, length_x), lambda t: (t + first_term, 0, 0, 0)),
        ] + [piece_spec(start, end) for start, end, _ in others] + [
            whole(high.shape, 1),
            whole(low.shape, 1),
        ],
        out_specs=pl.BlockSpec((blocks, 1, count_y, half, 2 * rows_x), lambda t: (0, t, 0, 0, 0)),
        out_shape=jax.ShapeDtypeStruct((blocks, terms, count_y, half, 2 * rows_x), F32),
        scratch_shapes=[
            pltpu.VMEM((length_y, 2, half, length_x), F32),
            pltpu.VMEM((length_y, 8, length_x), F32),
            pltpu.VMEM((count_y, first.shape[1], 2 * length_x), F32),
            pltpu.VMEM((count_y * first.shape[1], 2 * length_x), F32),
            pltpu.VMEM((rows, 2 * length_x), F32),
            pltpu.VMEM((rows, 2 * length_x), BF16),
            pltpu.VMEM((rows, 2 * length_x), BF16),
        ],
        compiler_params=params(1),
        cost_estimate=cost(terms * 24 * rows * length_x * length_x, terms * 16 * rows * length_x),
        name="spread",
    )(*[array for part in parts for array in part], me, first, own, *[array for _, _, array in others], high, low)


def gather_kernel(*refs):
    *data_refs, factor_ref, high_ref, low_ref, out_ref = refs
    blocks, _, _, half, lanes = data_refs[0].shape
    rows = lanes // 2
    parts = []
    for data_ref in data_refs:
        for t in range(data_ref.shape[1]):
            turned = data_ref[:, t, 0].reshape(blocks * half, lanes).T
            parts.append(jnp.concatenate([turned[:rows], turned[rows:]], axis=1))
    high, low = split(jnp.concatenate(parts, axis=0))
    fields = dot_three(high, low, high_ref[...], low_ref[...])
    total = factor_ref[0, 0] * fields[:rows]
    for t in range(1, len(parts)):
        total = total + factor_ref[t, 0] * fields[t * rows : (t + 1) * rows]
    out_ref[0] = total


def gather(chunks, factor, scale, width, group):
    blocks, _, _, half, lanes = chunks[0].shape
    terms, length_y, rows, length_z = factor.shape
    wide = group[1] - group[0]
    count_y = length_y // width * wide

    def row(n):
        return n // wide * width + group[0] + n % wide

    def chunk_spec(shape):
        full = shape[2] == length_y
        return pl.BlockSpec((blocks, shape[1], 1, half, lanes), lambda n: (0, 0, row(n) if full else n, 0, 0))
    high, low = halves(inverse_z_table(blocks, length_z, scale))
    return pl.pallas_call(
        gather_kernel,
        grid=(count_y,),
        in_specs=[
            chunk_spec(chunk.shape) for chunk in chunks
        ] + [
            pl.BlockSpec((terms, 1, rows, length_z), lambda n: (0, row(n), 0, 0)),
            whole(high.shape, 1),
            whole(low.shape, 1),
        ],
        out_specs=pl.BlockSpec((1, rows, length_z), lambda n: (n, 0, 0)),
        out_shape=jax.ShapeDtypeStruct((count_y, rows, length_z), F32),
        compiler_params=params(1),
        cost_estimate=cost(6 * terms * count_y * rows * length_z * length_z, 8 * terms * count_y * rows * length_z),
        name="gather_z",
    )(*chunks, factor, jnp.asarray(high), jnp.asarray(low))


def mirror_kernel(in_ref, table_ref, out_ref, turned_ref):
    _, length_y, half, length_x = in_ref.shape
    high, low = split(in_ref[0].reshape(length_y * half, length_x))
    rest = in_ref[0].reshape(length_y * half, length_x) - high.astype(F32) - low.astype(F32)
    table = table_ref[...]
    turned = (dot(high, table) + dot(low, table)) + dot(rest.astype(BF16), table)
    turned_ref[...] = turned.reshape(length_y, half, length_x)
    for y in range(length_y):
        source = -y % length_y
        for s in range(half):
            row = -s % half
            out_ref[0, y, s : s + 1, :] = turned_ref[source, row : row + 1, :]


def mirror(multiplier, start, end):
    _, length_y, width, length_x = multiplier.shape
    half = width // 2
    terms = end - start
    table = mirror_table(length_x)
    return pl.pallas_call(
        mirror_kernel,
        grid=(terms,),
        in_specs=[
            pl.BlockSpec((1, length_y, half, length_x), lambda t: (t + start, 0, 1, 0)),
            whole(table.shape, 1),
        ],
        out_specs=pl.BlockSpec((1, length_y, half, length_x), lambda t: (t, 0, 0, 0)),
        out_shape=jax.ShapeDtypeStruct((terms, length_y, half, length_x), F32),
        scratch_shapes=[pltpu.VMEM((length_y, half, length_x), F32)],
        compiler_params=params(1),
        cost_estimate=cost(6 * terms * length_y * half * length_x * length_x, 8 * terms * length_y * half * length_x),
        name="mirror",
    )(multiplier, jnp.asarray(table))


def flip(values, axis):
    return jnp.roll(jnp.flip(values, axis), 1, axis)


def padded_by_one(block, sides):
    for axis, dim in sides:
        count = lax.axis_size(axis)
        forward = [(i, i + 1) for i in range(count - 1)]
        backward = [(target, source) for source, target in forward]
        size = block.shape[dim]
        low = lax.ppermute(lax.slice_in_dim(block, size - 1, size, axis=dim), axis, forward)
        high = lax.ppermute(lax.slice_in_dim(block, 0, 1, axis=dim), axis, backward)
        yield dim, low, high


def heat_step(heat, perfuse):
    near = jnp.zeros_like(heat)
    for dim, low, high in padded_by_one(heat, (("term", 0), ("pencil", 1))):
        size = heat.shape[dim]
        near = near + jnp.concatenate([low, lax.slice_in_dim(heat, 0, size - 1, axis=dim)], axis=dim)
        near = near + jnp.concatenate([lax.slice_in_dim(heat, 1, size, axis=dim), high], axis=dim)
    deep = jnp.pad(heat, ((0, 0), (0, 0), (1, 1)))
    near = near + deep[:, :, 2:] + deep[:, :, :-2]
    return heat + DIFFUSION * (near - 6.0 * heat) - perfuse * heat


def update_kernel(fresh_ref, old_ref, dose_ref, heat_ref, absorb_ref, pressure_ref, source_ref, out_ref):
    field = fresh_ref[...] - old_ref[...]
    source = absorb_ref[...] * (dose_ref[...] + field * field)
    pressure_ref[...] = field
    source_ref[...] = source
    out_ref[...] = heat_ref[...] + source


def update(fresh, old, dose, heat, absorb):
    return pl.pallas_call(
        update_kernel,
        out_shape=[jax.ShapeDtypeStruct(fresh.shape, F32)] * 3,
        compiler_params=params(),
        cost_estimate=cost(5 * fresh.size, 32 * fresh.size),
        name="update",
    )(fresh, old, dose, heat, absorb)


def warm_kernel(*refs, groups, turned):
    heat_refs, source_refs, low_refs, high_refs = [refs[k * groups : (k + 1) * groups] for k in range(4)]
    below_ref, above_ref, perfuse_ref, out_ref = refs[4 * groups :]
    rows, length_z = below_ref.shape[1:]
    planes, sources, lows, highs = [], [], [], []
    for heat_ref, source_ref, low_ref, high_ref in zip(heat_refs, source_refs, low_refs, high_refs):
        for w in range(heat_ref.shape[0]):
            planes.append(heat_ref[w])
            sources.append(source_ref[w])
            lows.append(low_ref[w])
            highs.append(high_ref[w])
    row = lax.broadcasted_iota(jnp.int32, (rows, length_z), 0)
    lane = lax.broadcasted_iota(jnp.int32, (rows, length_z), 1)
    for w, heat in enumerate(planes):
        near = jnp.where(row == 0, lows[w], pltpu.roll(heat, 1, 0))
        near = near + jnp.where(row == rows - 1, highs[w], pltpu.roll(heat, rows - 1, 0))
        near = near + (planes[w - 1] if w else below_ref[0])
        near = near + (planes[w + 1] if w + 1 < len(planes) else above_ref[0])
        near = near + jnp.where(lane == 0, 0.0, pltpu.roll(heat, 1, 1))
        near = near + jnp.where(lane == length_z - 1, 0.0, pltpu.roll(heat, length_z - 1, 1))
        fresh = heat + DIFFUSION * (near - 6.0 * heat) - perfuse_ref[w] * heat + sources[w]
        if turned:
            out_ref[:, w, :] = fresh
        else:
            out_ref[w] = fresh


def halo(heat, lowest):
    (_, low, high), = padded_by_one(heat, (("pencil", 1),))
    if not lowest:
        return [low, high]
    backward = [(i + 1, i) for i in range(lax.axis_size("term") - 1)]
    return [low, high, lax.ppermute(heat[:1], "term", backward)]


def warm(heats, sources, sides, perfuse, turned):
    width, rows, length_z = perfuse.shape
    above = sides[0][2]
    below = lax.ppermute(heats[-1][-1:], "term", [(i, i + 1) for i in range(lax.axis_size("term") - 1)])
    return pl.pallas_call(
        functools.partial(warm_kernel, groups=len(heats), turned=turned),
        out_shape=jax.ShapeDtypeStruct((rows, width, length_z) if turned else perfuse.shape, F32),
        compiler_params=params(),
        cost_estimate=cost(16 * perfuse.size, 16 * perfuse.size),
        name="warm",
    )(*heats, *sources, *[side[0] for side in sides], *[side[1] for side in sides], below, above, perfuse)


def on_device(
    present_acoustic,
    prior_acoustic,
    location_factor,
    spectral_multiplier,
    medium_kinds,
    organ_properties,
    thermal_increase,
):
    term_count = lax.axis_size("term")
    blocks = lax.axis_size("pencil")
    rows, length_y, length_z = present_acoustic.shape
    length_x = rows * blocks
    width = length_y // term_count
    half = length_z // blocks // 2
    terms = location_factor.shape[0]
    brick_start = lax.axis_index("term") * width
    scale = 2.0 / (length_x * length_y * length_z)

    cut = width // 2 if width >= 4 else width
    spans = [(0, cut), (cut, width)] if cut < width else [(0, width)]

    def to_brick(values):
        return jnp.transpose(lax.dynamic_slice_in_dim(values, brick_start, width, 1), (1, 0, 2))

    def cut_up(brick):
        return [brick[start:end] for start, end in spans]

    def exchange(values):
        return lax.all_to_all(values, "pencil", 0, 0, tiled=True)

    lowest = spectral_multiplier[:, :, 0, :]
    lowest = lowest + lax.ppermute(
        flip(flip(lowest, 1), 2), "pencil", [(p, blocks - p) for p in range(1, blocks) if 2 * p != blocks]
    )
    lowest = jnp.transpose(lowest, (1, 0, 2))
    lowest = jnp.pad(lowest, ((0, 0), (0, -terms % 8), (0, 0)))
    opposite = [(p, blocks - 1 - p) for p in range(blocks)]
    middle = terms // 2
    sent = exchange(forward_z([to_brick(present_acoustic)], blocks)[0])
    others = []
    sent, lowest = lax.optimization_barrier((sent, lowest))
    before = sent
    for start, end in ((0, middle), (middle, terms)):
        if end > start:
            before, mirrored = lax.optimization_barrier((before, mirror(spectral_multiplier, start, end)))
            if not others:
                sent = before
            before = lax.ppermute(mirrored, "pencil", opposite)
            others.append((start, end, before))
    me = lax.axis_index("term").reshape(1).astype(jnp.int32)
    factor = jnp.transpose(location_factor, (0, 2, 1, 3))
    last, factor = lax.optimization_barrier((others[0][2], factor))
    others[0] = (*others[0][:2], last)

    def gathered(part):
        return [part] + [
            lax.ppermute(part, "term", [(i, (i - d) % term_count) for i in range(term_count)])
            for d in range(1, term_count)
        ]

    def spread_from(parts, sent_spans, group, chosen):
        out = spread(parts, sent_spans, me, lowest, spectral_multiplier, others, blocks, group, chosen)
        flat, tree = jax.tree.flatten(parts)
        out, *flat = lax.optimization_barrier((out, *flat))
        return out, jax.tree.unflatten(tree, flat)

    def summed(chunks, group):
        partial = gather(chunks, factor, scale, width, group)
        return lax.psum_scatter(partial, "term", scatter_dimension=0, tiled=True)

    def doubled_first(part, tied):
        parts = [[lax.all_gather(part, "term", axis=0, tiled=False)]]
        shared, chunks, bricks = [], {}, []
        if middle:
            out, parts = spread_from(parts, [(0, width)], (0, width), (0, middle))
            out, last = lax.optimization_barrier((out, others[-1][2]))
            others[-1] = (*others[-1][:2], last)
            shared = [exchange(out)]
        before = shared
        for index, group in enumerate(spans):
            out, parts = spread_from(parts, [(0, width)], group, (middle, terms))
            out, *before = lax.optimization_barrier((out, *before))
            if index == 0:
                shared = before
            out = exchange(out)
            before = [out]
            if index == 0:
                out, *tied = lax.optimization_barrier((out, *tied))
            bricks.append(summed(shared + [out], group))
        return bricks, tied

    def doubled(parts):
        bricks, before = [], []
        for group in spans:
            out, parts = spread_from(parts, spans, group, (0, terms))
            out, *before = lax.optimization_barrier((out, *before))
            if before:
                chunks[0] = before[0]
                bricks.append(summed(chunks, spans[0]))
            chunks = [exchange(out)]
            before = list(chunks)
        bricks.append(summed(chunks, spans[-1]))
        return bricks

    def forward(bricks):
        parts, states, before = [], [], []
        for (start, end), (fresh, *older) in zip(spans, bricks):
            fresh, *before = lax.optimization_barrier((fresh, *before))
            if before:
                parts.append(gathered(before[0]))
            sent, *state = forward_z([fresh, *older], blocks)
            sent = exchange(sent)
            if parts:
                sent, *parts[-1] = lax.optimization_barrier((sent, *parts[-1]))
            before = [forward_x(sent, end - start, half, rows)]
            states.append(state)
        parts.append(gathered(before[0]))
        return parts, states

    kinds = jnp.transpose(medium_kinds, (1, 0, 2))
    absorb, perfuse = [
        jnp.where(
            kinds == 0,
            organ_properties[0, at],
            jnp.where(kinds == 1, organ_properties[1, at], organ_properties[2, at]),
        )
        for at in range(2)
    ]
    heat = heat_step(jnp.transpose(thermal_increase, (1, 0, 2)), perfuse)

    previous = cut_up(to_brick(prior_acoustic))
    current = cut_up(to_brick(present_acoustic))
    dose = []
    doubles, (heat, absorb, perfuse) = doubled_first(forward_x(sent, width, half, rows), (heat, absorb, perfuse))
    for _ in range(WAVE_STEPS - 1):
        parts, states = forward(list(zip(doubles, previous, *dose)))
        previous, current = current, [field for field, _ in states]
        dose = [[total for _, total in states]]
        doubles = doubled(parts)
    dose = dose[0] if dose else [jnp.zeros(each.shape, F32) for each in current]
    updated, sides, ahead = [], [], []
    for fresh, *rest in zip(doubles, previous, dose, cut_up(heat), cut_up(absorb)):
        fresh, *ahead = lax.optimization_barrier((fresh, *ahead))
        if ahead:
            sides.append(ahead)
        updated.append(update(fresh, *rest))
        ahead = halo(updated[-1][2], not sides)
    sides.append(ahead)
    pressure = jnp.concatenate([each[0] for each in updated], axis=0)
    sources = [each[1] for each in updated]
    heats = [each[2] for each in updated]
    for _ in range(HEAT_STEPS - 2):
        heats = cut_up(warm(heats, sources, sides, perfuse, False))
        sides = [halo(each, index == 0) for index, each in enumerate(heats)]
    return jnp.transpose(pressure, (1, 0, 2)), warm(heats, sources, sides, perfuse, True)


def solution(mesh):
    return jax.shard_map(
        on_device,
        mesh=mesh,
        in_specs=(
            P("pencil", None, None),
            P("pencil", None, None),
            P("term", "pencil", None, None),
            P("term", None, "pencil", None),
            P("pencil", "term", None),
            P(),
            P("pencil", "term", None),
        ),
        out_specs=(P("pencil", "term", None), P("pencil", "term", None)),
        check_vma=False,
    )
```

```python
import functools
import math

import jax
import jax.numpy as jnp
import ml_dtypes
import numpy as np
from jax import lax
from jax.experimental import pallas as pl
from jax.experimental.pallas import tpu as pltpu
from jax.sharding import PartitionSpec as P

WAVE_STEPS = 2
HEAT_STEPS = 2
DIFFUSION = 0.125
VMEM_BYTES = 56 * 1024 * 1024
F32 = jnp.float32
BF16 = jnp.bfloat16


def halves(table):
    high = table.astype(ml_dtypes.bfloat16)
    low = (table - high.astype(np.float64)).astype(ml_dtypes.bfloat16)
    return high, low


def angles(left, right, length):
    return (np.outer(left, right) % length) * (2.0 * math.pi / length)


def slot_wavenumbers(blocks, length_z):
    width = length_z // blocks
    half = width // 2
    slots = np.concatenate([[half], np.arange(1, half)])
    starts = np.arange(blocks) * width
    return starts[:, None] + slots[None, :], starts


def forward_z_table(blocks, length_z):
    main, first = slot_wavenumbers(blocks, length_z)
    z = np.arange(length_z)
    theta = angles(z, main.reshape(-1), length_z).reshape(length_z, blocks, -1)
    real, imag = np.cos(theta), -np.sin(theta)
    for q in range(blocks // 2):
        real[:, q, 0], imag[:, q, 0] = -imag[:, q, 0].copy(), real[:, q, 0].copy()
    theta = angles(z, first, length_z)
    real0, imag0 = np.cos(theta), -np.sin(theta)
    for q in range(blocks // 2 + 1, blocks):
        real0[:, q], imag0[:, q] = imag0[:, q].copy(), -real0[:, q].copy()
    table = np.concatenate(
        [np.stack([real, imag], 2).reshape(length_z, -1), np.stack([real0, imag0], 2).reshape(length_z, -1)], axis=1
    )
    spare = -table.shape[1] % 128
    return np.pad(table, ((0, 0), (0, spare)))


def inverse_z_table(blocks, length_z, scale):
    main, first = slot_wavenumbers(blocks, length_z)
    z = np.arange(length_z)
    theta = angles(main.reshape(-1), z, length_z).reshape(blocks, -1, length_z)
    real, imag = np.cos(theta), -np.sin(theta)
    for p in range(blocks):
        middle = theta[p, 0]
        imag[p, 0] = np.cos(middle) if p < blocks // 2 else -np.sin(middle)
        lowest = angles(first[p : p + 1], z, length_z)[0]
        real[p, 0] = np.cos(lowest) if p <= blocks // 2 else -np.sin(lowest)
    return scale * np.concatenate([real.reshape(-1, length_z), imag.reshape(-1, length_z)], axis=0)


def forward_x_table(length_x):
    x = np.arange(length_x)
    theta = angles(x, x, length_x)
    return np.concatenate([np.cos(theta), np.sin(theta)], axis=1)


def inverse_x_table(blocks, length_x):
    x = np.arange(length_x)
    theta = angles(x, x, length_x).reshape(length_x, blocks, -1)
    cosine, sine = np.cos(theta), np.sin(theta)
    real_rows = np.stack([cosine, sine], axis=2).reshape(length_x, -1)
    imag_rows = np.stack([-sine, cosine], axis=2).reshape(length_x, -1)
    return np.concatenate([real_rows, imag_rows], axis=0)


def mirror_table(length):
    x = np.arange(length)
    table = np.zeros((length, length), ml_dtypes.bfloat16)
    table[x, (-x) % length] = 1
    return table


def turned_by(a, b, k, count, sign):
    if k == 0:
        return a, b
    if 4 * k == count:
        return (-b, a) if sign > 0 else (b, -a)
    angle = 2.0 * math.pi * k / count
    c, s = math.cos(angle), sign * math.sin(angle)
    if 8 * k == count or 8 * k == 3 * count:
        root = math.sqrt(0.5)
        sum_ab, less_ab = root * (a + b), root * (a - b)
        if c > 0:
            return (less_ab, sum_ab) if s > 0 else (sum_ab, -less_ab)
        return (-sum_ab, less_ab) if s > 0 else (-less_ab, -sum_ab)
    return c * a - s * b, c * b + s * a


def fourier(values, sign, wanted=None):
    count = len(values)
    wanted = range(count) if wanted is None else wanted
    if not wanted:
        return {}
    if count == 1:
        return {0: values[0]}
    if count % 2:
        out = {}
        for k in wanted:
            real, imag = values[0]
            for n in range(1, count):
                angle = 2.0 * math.pi * (k * n % count) / count
                c, s = math.cos(angle), sign * math.sin(angle)
                a, b = values[n]
                real, imag = real + (c * a - s * b), imag + (c * b + s * a)
            out[k] = (real, imag)
        return out
    half = count // 2
    out = {}
    even = [k // 2 for k in wanted if k % 2 == 0]
    odd = [k // 2 for k in wanted if k % 2]
    if even:
        added = [(values[n][0] + values[n + half][0], values[n][1] + values[n + half][1]) for n in range(half)]
        for k, value in fourier(added, sign, even).items():
            out[2 * k] = value
    if odd:
        less = [
            turned_by(values[n][0] - values[n + half][0], values[n][1] - values[n + half][1], n, count, sign)
            for n in range(half)
        ]
        for k, value in fourier(less, sign, odd).items():
            out[2 * k + 1] = value
    return out


def split(values):
    high = values.astype(BF16)
    return high, (values - high.astype(F32)).astype(BF16)


def dot(left, right):
    return jnp.dot(left, right, preferred_element_type=F32)


def dot_across(left, right):
    return lax.dot_general(left, right, (((1,), (1,)), ((), ())), preferred_element_type=F32)


def dot_three(high, low, table_high, table_low):
    return dot(high, table_high) + (dot(low, table_high) + dot(high, table_low))


def dot_stacked(both, table_high, table_low):
    count = both.shape[0] // 2
    by_high = dot(both, table_high)
    return by_high[:count] + (by_high[count:] + dot(both[:count], table_low))


def params(count=0):
    return pltpu.CompilerParams(vmem_limit_bytes=VMEM_BYTES, dimension_semantics=("arbitrary",) * count)


def cost(flops, moved):
    return pl.CostEstimate(flops=int(flops), bytes_accessed=int(moved), transcendentals=0)


def whole(shape, grid_rank):
    return pl.BlockSpec(shape, lambda *_: (0,) * len(shape), pipeline_mode=pl.Buffered(1)) if grid_rank else pl.BlockSpec(
        memory_space=pltpu.VMEM
    )


def forward_z_kernel(*refs, inputs):
    fresh_ref, *older = refs[:inputs]
    high_ref, low_ref, first_high_ref, first_low_ref, out_ref, *state = refs[inputs:]
    width, rows, length_z = fresh_ref.shape
    blocks = out_ref.shape[0]
    main = length_z // blocks
    brick = fresh_ref[...]
    if older:
        brick = brick - older[0][...]
        state[0][...] = brick
        dose = brick * brick
        state[1][...] = dose + older[1][...] if len(older) > 1 else dose
    high, low = split(brick.reshape(width * rows, length_z))
    result = dot_three(high, low, high_ref[...], low_ref[...])
    first = (
        dot_across(first_high_ref[...], high)
        + (dot_across(first_low_ref[...], high) + dot_across(first_high_ref[...], low))
    )
    out_ref[:, rows:, :] = jnp.zeros_like(out_ref[:, rows:, :])
    for q in range(blocks):
        for w in range(width):
            out_ref[q, :rows, w * main : (w + 1) * main] = result[w * rows : (w + 1) * rows, q * main : (q + 1) * main]
            for c in range(2):
                row = rows + c * width + w
                out_ref[q, row : row + 1, :rows] = first[2 * q + c : 2 * q + c + 1, w * rows : (w + 1) * rows]


def forward_z(bricks, blocks):
    width, rows, length_z = bricks[0].shape
    lanes = max(width * length_z // blocks, rows)
    table = forward_z_table(blocks, length_z)
    high, low = halves(table[:, :length_z])
    first_high, first_low = halves(table[:, length_z : length_z + 2 * blocks].T)
    tables = [jnp.asarray(each) for each in (high, low, first_high, first_low)]
    out = [jax.ShapeDtypeStruct((blocks, rows + 2 * width + (-2 * width) % 8, lanes), F32)]
    if len(bricks) > 1:
        out += [jax.ShapeDtypeStruct(bricks[0].shape, F32)] * 2
    return pl.pallas_call(
        functools.partial(forward_z_kernel, inputs=len(bricks)),
        out_shape=out,
        compiler_params=params(),
        cost_estimate=cost(6 * width * rows * length_z * length_z, 16 * width * rows * length_z),
        name="forward_z",
    )(*bricks, *tables)


def forward_x_kernel(data_ref, high_ref, low_ref, out_ref, *, width, half, rows):
    blocks = data_ref.shape[0]
    length_x = blocks * rows
    main = width * 2 * half
    turned = data_ref[:, :rows, :main].reshape(length_x, main).T
    first = jnp.concatenate([data_ref[q, rows:, :rows] for q in range(blocks)], axis=1)
    high, low = split(jnp.concatenate([turned, first], axis=0))
    both = dot_three(high, low, high_ref[...], low_ref[...])
    by_cos, by_sin = both[:, :length_x], both[:, length_x:]
    for w in range(width):
        re, im = w * 2 * half, w * 2 * half + half
        out_ref[re : re + half] = by_cos[re : re + half] + by_sin[im : im + half]
        out_ref[im : im + half] = by_cos[im : im + half] - by_sin[re : re + half]
    re, im, end = main, main + width, main + 2 * width
    out_ref[re:im] = by_cos[re:im] + by_sin[im:end]
    out_ref[im:end] = by_cos[im:end] - by_sin[re:im]
    if end < out_ref.shape[0]:
        out_ref[end:] = jnp.zeros_like(out_ref[end:])


def forward_x(data, width, half, rows):
    blocks = data.shape[0]
    length_x = blocks * rows
    out_rows = width * 2 * half + data.shape[1] - rows
    high, low = halves(forward_x_table(length_x))
    return pl.pallas_call(
        functools.partial(forward_x_kernel, width=width, half=half, rows=rows),
        out_shape=jax.ShapeDtypeStruct((out_rows, length_x), F32),
        compiler_params=params(),
        cost_estimate=cost(12 * out_rows * length_x * length_x, 8 * out_rows * length_x),
        name="forward_x",
    )(data, jnp.asarray(high), jnp.asarray(low))


def spread_kernel(*refs, spans, counts, group, pieces, first_term):
    parts, at = [], 0
    for count in counts:
        parts.append(refs[at : at + count])
        at += count
    me_ref, first_ref, own_ref = refs[at : at + 3]
    others = refs[at + 3 : at + 3 + len(pieces)]
    (
        high_ref, low_ref, out_ref,
        fk_ref, edge_in_ref, edge_ref, edge_out_ref, u_ref, u_both_ref,
    ) = refs[at + 3 + len(pieces) :]
    length_y, _, half, length_x = fk_ref.shape
    lanes_out = out_ref.shape[-1]
    rows_x = lanes_out // 2
    count_y = out_ref.shape[2]
    width = spans[-1][1]
    holders = length_y // width
    step = pl.program_id(0)
    tiles = [slice(at, at + 128) for at in range(0, length_x, 128)]
    wanted = [y for y in range(length_y) if group[0] <= y % width < group[1]]

    @pl.when(step == 0)
    def _():
        for part, (start, end) in zip(parts, spans):
            wide = end - start
            for d in range(holders):
                if len(part) == 1:
                    source, holder = part[0].at[d], d
                else:
                    source, holder = part[d], lax.rem(me_ref[0] + d, holders)
                for w in range(wide):
                    y = holder * width + start + w
                    fk_ref[y, 0] = source[w * 2 * half : w * 2 * half + half]
                    fk_ref[y, 1] = source[w * 2 * half + half : (w + 1) * 2 * half]
                    row = wide * 2 * half + w
                    edge_in_ref[y, :1] = source[row : row + 1]
                    edge_in_ref[y, 1:2] = source[row + wide : row + wide + 1]

        @pl.loop(0, half // 8)
        def _(tile):
            at = pl.ds(pl.multiple_of(tile * 8, 8), 8)
            for lanes in tiles:
                values = [(fk_ref[y, 0, at, lanes], fk_ref[y, 1, at, lanes]) for y in range(length_y)]
                values = fourier(values, -1)
                for y in range(length_y):
                    fk_ref[y, 0, at, lanes] = values[y][0]
                    fk_ref[y, 1, at, lanes] = values[y][1]

        for index, lanes in enumerate(tiles):
            values = [(edge_in_ref[y, :1, lanes], edge_in_ref[y, 1:2, lanes]) for y in range(length_y)]
            values = fourier(values, -1)
            factors = [first_ref[y, :, lanes] for y in range(length_y)]
            values = [(factors[y] * values[y][0], factors[y] * values[y][1]) for y in range(length_y)]
            values = fourier(values, 1, wanted)
            for n, y in enumerate(wanted):
                edge_ref[n, :, index * 128 : index * 128 + 128] = values[y][0]
                edge_ref[n, :, length_x + index * 128 : length_x + index * 128 + 128] = values[y][1]
        high, low = split(edge_ref[...].reshape(-1, 2 * length_x))
        edge_out_ref[...] = dot_three(high, low, high_ref[...], low_ref[...])

    row_index = lax.broadcasted_iota(jnp.int32, (8, 128), 0)

    def weigh(other_ref):
        @pl.loop(0, half // 8)
        def _(tile):
            at = pl.ds(pl.multiple_of(tile * 8, 8), 8)
            swapped = jnp.logical_and(row_index == 0, tile == 0)
            for index, lanes in enumerate(tiles):
                values = []
                for y in range(length_y):
                    own = jnp.where(swapped, own_ref[0, y, half : half + 1, lanes], own_ref[0, y, at, lanes])
                    factor = own + other_ref[0, y, at, lanes]
                    values.append((factor * fk_ref[y, 0, at, lanes], factor * fk_ref[y, 1, at, lanes]))
                values = fourier(values, 1, wanted)
                for n, y in enumerate(wanted):
                    rows = pl.ds(pl.multiple_of(n * half + tile * 8, 8), 8)
                    u_ref[rows, index * 128 : index * 128 + 128] = values[y][0]
                    u_ref[rows, length_x + index * 128 : length_x + index * 128 + 128] = values[y][1]

    if len(others) == 1:
        weigh(others[0])
    else:
        for other_ref, (start, end) in zip(others, pieces):
            pl.when(jnp.logical_and(step >= start, step < end))(functools.partial(weigh, other_ref))

    @pl.loop(0, count_y * half // 64)
    def _(part):
        rows = pl.ds(pl.multiple_of(part * 64, 64), 64)
        high, low = split(u_ref[rows, :])
        u_both_ref[rows, :] = high
        u_both_ref[pl.ds(pl.multiple_of(count_y * half + part * 64, 64), 64), :] = low

    lane_index = lax.broadcasted_iota(jnp.int32, (8, lanes_out), 1)
    row_index = lax.broadcasted_iota(jnp.int32, (8, lanes_out), 0)
    swapped = jnp.logical_and(row_index == 0, lane_index < rows_x)
    count = 256 // lanes_out
    for part in range(2 * length_x // 256):
        cols = slice(part * 256, part * 256 + 256)
        result = dot_stacked(u_both_ref[...], high_ref[:, cols], low_ref[:, cols])
        edges = [edge_out_ref[pl.ds(n * first_ref.shape[1] + step + first_term, 1), cols] for n in range(count_y)]
        for k in range(count):
            q = part * count + k
            inside = slice(k * lanes_out, (k + 1) * lanes_out)
            piece = result[:, inside]
            for n in range(count_y):
                top = piece[n * half : n * half + 8]
                out_ref[q, 0, n, :8, :] = jnp.where(swapped, edges[n][:, inside], top)
                out_ref[q, 0, n, 8:, :] = piece[n * half + 8 : (n + 1) * half]


def spread(parts, spans, me, first, own, others, blocks, group, chosen):
    _, length_y, _, length_x = own.shape
    half = own.shape[2] // 2
    first_term, end_term = chosen
    terms = end_term - first_term
    count_y = length_y // spans[-1][1] * (group[1] - group[0])
    rows_x = length_x // blocks
    high, low = halves(inverse_x_table(blocks, length_x))
    high, low = jnp.asarray(high), jnp.asarray(low)
    rows = count_y * half
    others = [each for each in others if each[0] < end_term and each[1] > first_term]

    def piece_spec(start, end):
        return pl.BlockSpec(
            (1, length_y, half, length_x), lambda t: (jnp.clip(t + first_term - start, 0, end - start - 1), 0, 0, 0)
        )

    return pl.pallas_call(
        functools.partial(
            spread_kernel, spans=spans, counts=[len(part) for part in parts], group=group, first_term=first_term,
            pieces=[(start - first_term, end - first_term) for start, end, _ in others],
        ),
        grid=(terms,),
        in_specs=[whole(array.shape, 1) for part in parts for array in part] + [
            pl.BlockSpec(memory_space=pltpu.SMEM),
            whole(first.shape, 1),
            pl.BlockSpec((1, length_y, half + 8, length_x), lambda t: (t + first_term, 0, 0, 0)),
        ] + [piece_spec(start, end) for start, end, _ in others] + [
            whole(high.shape, 1),
            whole(low.shape, 1),
        ],
        out_specs=pl.BlockSpec((blocks, 1, count_y, half, 2 * rows_x), lambda t: (0, t, 0, 0, 0)),
        out_shape=jax.ShapeDtypeStruct((blocks, terms, count_y, half, 2 * rows_x), F32),
        scratch_shapes=[
            pltpu.VMEM((length_y, 2, half, length_x), F32),
            pltpu.VMEM((length_y, 8, length_x), F32),
            pltpu.VMEM((count_y, first.shape[1], 2 * length_x), F32),
            pltpu.VMEM((count_y * first.shape[1], 2 * length_x), F32),
            pltpu.VMEM((rows, 2 * length_x), F32),
            pltpu.VMEM((2 * rows, 2 * length_x), BF16),
        ],
        compiler_params=params(1),
        cost_estimate=cost(terms * 24 * rows * length_x * length_x, terms * 16 * rows * length_x),
        name="spread",
    )(*[array for part in parts for array in part], me, first, own, *[array for _, _, array in others], high, low)


def gather_kernel(*refs):
    *data_refs, factor_ref, high_ref, low_ref, out_ref = refs
    blocks, _, wide, half, lanes = data_refs[0].shape
    rows = lanes // 2
    parts = []
    for y in range(wide):
        for data_ref in data_refs:
            for t in range(data_ref.shape[1]):
                turned = data_ref[:, t, y].reshape(blocks * half, lanes).T
                parts.append(jnp.concatenate([turned[:rows], turned[rows:]], axis=1))
    high, low = split(jnp.concatenate(parts, axis=0))
    fields = dot_stacked(jnp.concatenate([high, low], axis=0), high_ref[...], low_ref[...])
    terms = len(parts) // wide
    for y in range(wide):
        total = factor_ref[0, y] * fields[y * terms * rows : (y * terms + 1) * rows]
        for t in range(1, terms):
            at = (y * terms + t) * rows
            total = total + factor_ref[t, y] * fields[at : at + rows]
        out_ref[y] = total


def gather(chunks, factor, scale, width, group):
    blocks, _, _, half, lanes = chunks[0].shape
    terms, length_y, rows, length_z = factor.shape
    wide = group[1] - group[0]
    holders = length_y // width
    high, low = halves(inverse_z_table(blocks, length_z, scale))

    def row(n):
        return (n * width + group[0]) // wide

    def chunk_spec(shape):
        full = shape[2] == length_y
        return pl.BlockSpec((blocks, shape[1], wide, half, lanes), lambda n: (0, 0, row(n) if full else n, 0, 0))

    return pl.pallas_call(
        gather_kernel,
        grid=(holders,),
        in_specs=[chunk_spec(chunk.shape) for chunk in chunks] + [
            pl.BlockSpec((terms, wide, rows, length_z), lambda n: (0, row(n), 0, 0)),
            whole(high.shape, 1),
            whole(low.shape, 1),
        ],
        out_specs=pl.BlockSpec((wide, rows, length_z), lambda n: (n, 0, 0)),
        out_shape=jax.ShapeDtypeStruct((holders * wide, rows, length_z), F32),
        compiler_params=params(1),
        cost_estimate=cost(
            6 * terms * holders * wide * rows * length_z * length_z, 8 * terms * holders * wide * rows * length_z
        ),
        name="gather_z",
    )(*chunks, factor, jnp.asarray(high), jnp.asarray(low))


def mirror_kernel(in_ref, table_ref, out_ref, turned_ref):
    _, length_y, half, length_x = in_ref.shape
    high, low = split(in_ref[0].reshape(length_y * half, length_x))
    rest = in_ref[0].reshape(length_y * half, length_x) - high.astype(F32) - low.astype(F32)
    table = table_ref[...]
    turned = (dot(high, table) + dot(low, table)) + dot(rest.astype(BF16), table)
    turned_ref[...] = turned.reshape(length_y, half, length_x)
    for y in range(length_y):
        source = -y % length_y
        for s in range(half):
            row = -s % half
            out_ref[0, y, s : s + 1, :] = turned_ref[source, row : row + 1, :]


def mirror(multiplier, start, end):
    _, length_y, width, length_x = multiplier.shape
    half = width // 2
    terms = end - start
    table = mirror_table(length_x)
    return pl.pallas_call(
        mirror_kernel,
        grid=(terms,),
        in_specs=[
            pl.BlockSpec((1, length_y, half, length_x), lambda t: (t + start, 0, 1, 0)),
            whole(table.shape, 1),
        ],
        out_specs=pl.BlockSpec((1, length_y, half, length_x), lambda t: (t, 0, 0, 0)),
        out_shape=jax.ShapeDtypeStruct((terms, length_y, half, length_x), F32),
        scratch_shapes=[pltpu.VMEM((length_y, half, length_x), F32)],
        compiler_params=params(1),
        cost_estimate=cost(6 * terms * length_y * half * length_x * length_x, 8 * terms * length_y * half * length_x),
        name="mirror",
    )(multiplier, jnp.asarray(table))


def flip(values, axis):
    return jnp.roll(jnp.flip(values, axis), 1, axis)


def padded_by_one(block, sides):
    for axis, dim in sides:
        count = lax.axis_size(axis)
        forward = [(i, i + 1) for i in range(count - 1)]
        backward = [(target, source) for source, target in forward]
        size = block.shape[dim]
        low = lax.ppermute(lax.slice_in_dim(block, size - 1, size, axis=dim), axis, forward)
        high = lax.ppermute(lax.slice_in_dim(block, 0, 1, axis=dim), axis, backward)
        yield dim, low, high


def heat_step(heat, perfuse):
    near = jnp.zeros_like(heat)
    for dim, low, high in padded_by_one(heat, (("term", 0), ("pencil", 1))):
        size = heat.shape[dim]
        near = near + jnp.concatenate([low, lax.slice_in_dim(heat, 0, size - 1, axis=dim)], axis=dim)
        near = near + jnp.concatenate([lax.slice_in_dim(heat, 1, size, axis=dim), high], axis=dim)
    deep = jnp.pad(heat, ((0, 0), (0, 0), (1, 1)))
    near = near + deep[:, :, 2:] + deep[:, :, :-2]
    return heat + DIFFUSION * (near - 6.0 * heat) - perfuse * heat


def update_kernel(fresh_ref, old_ref, dose_ref, heat_ref, absorb_ref, pressure_ref, source_ref, out_ref):
    field = fresh_ref[...] - old_ref[...]
    source = absorb_ref[...] * (dose_ref[...] + field * field)
    pressure_ref[...] = field
    source_ref[...] = source
    out_ref[...] = heat_ref[...] + source


def update(fresh, old, dose, heat, absorb):
    return pl.pallas_call(
        update_kernel,
        out_shape=[jax.ShapeDtypeStruct(fresh.shape, F32)] * 3,
        compiler_params=params(),
        cost_estimate=cost(5 * fresh.size, 32 * fresh.size),
        name="update",
    )(fresh, old, dose, heat, absorb)


def warm_kernel(*refs, groups, turned):
    heat_refs, source_refs, low_refs, high_refs = [refs[k * groups : (k + 1) * groups] for k in range(4)]
    below_ref, above_ref, perfuse_ref, out_ref = refs[4 * groups :]
    rows, length_z = below_ref.shape[1:]
    planes, sources, lows, highs = [], [], [], []
    for heat_ref, source_ref, low_ref, high_ref in zip(heat_refs, source_refs, low_refs, high_refs):
        for w in range(heat_ref.shape[0]):
            planes.append(heat_ref[w])
            sources.append(source_ref[w])
            lows.append(low_ref[w])
            highs.append(high_ref[w])
    row = lax.broadcasted_iota(jnp.int32, (rows, length_z), 0)
    lane = lax.broadcasted_iota(jnp.int32, (rows, length_z), 1)
    for w, heat in enumerate(planes):
        near = jnp.where(row == 0, lows[w], pltpu.roll(heat, 1, 0))
        near = near + jnp.where(row == rows - 1, highs[w], pltpu.roll(heat, rows - 1, 0))
        near = near + (planes[w - 1] if w else below_ref[0])
        near = near + (planes[w + 1] if w + 1 < len(planes) else above_ref[0])
        near = near + jnp.where(lane == 0, 0.0, pltpu.roll(heat, 1, 1))
        near = near + jnp.where(lane == length_z - 1, 0.0, pltpu.roll(heat, length_z - 1, 1))
        fresh = heat + DIFFUSION * (near - 6.0 * heat) - perfuse_ref[w] * heat + sources[w]
        if turned:
            out_ref[:, w, :] = fresh
        else:
            out_ref[w] = fresh


def halo(heat, lowest):
    (_, low, high), = padded_by_one(heat, (("pencil", 1),))
    if not lowest:
        return [low, high]
    backward = [(i + 1, i) for i in range(lax.axis_size("term") - 1)]
    return [low, high, lax.ppermute(heat[:1], "term", backward)]


def warm(heats, sources, sides, perfuse, turned):
    width, rows, length_z = perfuse.shape
    above = sides[0][2]
    below = lax.ppermute(heats[-1][-1:], "term", [(i, i + 1) for i in range(lax.axis_size("term") - 1)])
    return pl.pallas_call(
        functools.partial(warm_kernel, groups=len(heats), turned=turned),
        out_shape=jax.ShapeDtypeStruct((rows, width, length_z) if turned else perfuse.shape, F32),
        compiler_params=params(),
        cost_estimate=cost(16 * perfuse.size, 16 * perfuse.size),
        name="warm",
    )(*heats, *sources, *[side[0] for side in sides], *[side[1] for side in sides], below, above, perfuse)


def on_device(
    present_acoustic,
    prior_acoustic,
    location_factor,
    spectral_multiplier,
    medium_kinds,
    organ_properties,
    thermal_increase,
):
    term_count = lax.axis_size("term")
    blocks = lax.axis_size("pencil")
    rows, length_y, length_z = present_acoustic.shape
    length_x = rows * blocks
    width = length_y // term_count
    half = length_z // blocks // 2
    terms = location_factor.shape[0]
    brick_start = lax.axis_index("term") * width
    scale = 2.0 / (length_x * length_y * length_z)

    cut = width // 2 if width >= 4 else width
    spans = [(0, cut), (cut, width)] if cut < width else [(0, width)]

    def to_brick(values):
        return jnp.transpose(lax.dynamic_slice_in_dim(values, brick_start, width, 1), (1, 0, 2))

    def cut_up(brick):
        return [brick[start:end] for start, end in spans]

    def exchange(values):
        return lax.all_to_all(values, "pencil", 0, 0, tiled=True)

    opposite = [(p, blocks - 1 - p) for p in range(blocks)]
    middle = terms // 2
    sent = forward_z([to_brick(present_acoustic)], blocks)[0]
    sent, multiplier = lax.optimization_barrier((sent, spectral_multiplier))
    sent = exchange(sent)
    lowest = spectral_multiplier[:, :, 0, :]
    others, before = [], None
    for start, end in ((0, middle), (middle, terms)):
        if end > start:
            mirrored = mirror(multiplier, start, end)
            if others:
                mirrored, before, lowest = lax.optimization_barrier((mirrored, before, lowest))
                others = [(*others[0][:2], before)]
            else:
                mirrored, lowest = lax.optimization_barrier((mirrored, lowest))
            before = lax.ppermute(mirrored, "pencil", opposite)
            if not others:
                lowest = lowest + lax.ppermute(
                    flip(flip(lowest, 1), 2),
                    "pencil",
                    [(p, blocks - p) for p in range(1, blocks) if 2 * p != blocks],
                )
            others.append((start, end, before))
    lowest = jnp.transpose(lowest, (1, 0, 2))
    lowest = jnp.pad(lowest, ((0, 0), (0, -terms % 8), (0, 0)))
    me = lax.axis_index("term").reshape(1).astype(jnp.int32)
    factor = jnp.transpose(location_factor, (0, 2, 1, 3))
    last, factor = lax.optimization_barrier((others[0][2], factor))
    others[0] = (*others[0][:2], last)

    def gathered(part, offload):
        if offload or term_count == 1:
            return [lax.all_gather(part, "term", axis=0, tiled=False)]
        return [part] + [
            lax.ppermute(part, "term", [(i, (i - d) % term_count) for i in range(term_count)])
            for d in range(1, term_count)
        ]

    def spread_from(parts, sent_spans, group, chosen):
        out = spread(parts, sent_spans, me, lowest, spectral_multiplier, others, blocks, group, chosen)
        flat, tree = jax.tree.flatten(parts)
        out, *flat = lax.optimization_barrier((out, *flat))
        return out, jax.tree.unflatten(tree, flat)

    def summed(chunks, group):
        partial = gather(chunks, factor, scale, width, group)
        return lax.psum_scatter(partial, "term", scatter_dimension=0, tiled=True)

    def doubled_first(part, tied):
        parts = [[lax.all_gather(part, "term", axis=0, tiled=False)]]
        shared, chunks, bricks = [], {}, []
        if middle:
            out, parts = spread_from(parts, [(0, width)], (0, width), (0, middle))
            out, last = lax.optimization_barrier((out, others[-1][2]))
            others[-1] = (*others[-1][:2], last)
            shared = [exchange(out)]
        before = shared
        for index, group in enumerate(spans):
            out, parts = spread_from(parts, [(0, width)], group, (middle, terms))
            out, *before = lax.optimization_barrier((out, *before))
            if index == 0:
                shared = before
            out = exchange(out)
            before = [out]
            if index == 0:
                out, *tied = lax.optimization_barrier((out, *tied))
            bricks.append(summed(shared + [out], group))
        return bricks, tied

    def doubled(parts):
        bricks, before = [], []
        for group in spans:
            out, parts = spread_from(parts, spans, group, (0, terms))
            out, *before = lax.optimization_barrier((out, *before))
            if before:
                chunks[0] = before[0]
                bricks.append(summed(chunks, spans[0]))
            chunks = [exchange(out)]
            before = list(chunks)
        bricks.append(summed(chunks, spans[-1]))
        return bricks

    def forward(bricks):
        parts, states, before = [], [], []
        for (start, end), (fresh, *older) in zip(spans, bricks):
            fresh, *before = lax.optimization_barrier((fresh, *before))
            if before:
                parts.append(gathered(before[0], True))
            sent, *state = forward_z([fresh, *older], blocks)
            sent = exchange(sent)
            before = [forward_x(sent, end - start, half, rows)]
            states.append(state)
        parts.append(gathered(before[0], False))
        return parts, states

    kinds = jnp.transpose(medium_kinds, (1, 0, 2))
    absorb, perfuse = [
        jnp.where(
            kinds == 0,
            organ_properties[0, at],
            jnp.where(kinds == 1, organ_properties[1, at], organ_properties[2, at]),
        )
        for at in range(2)
    ]
    heat = heat_step(jnp.transpose(thermal_increase, (1, 0, 2)), perfuse)

    previous = cut_up(to_brick(prior_acoustic))
    current = cut_up(to_brick(present_acoustic))
    dose = []
    doubles, (heat, absorb, perfuse) = doubled_first(forward_x(sent, width, half, rows), (heat, absorb, perfuse))
    for _ in range(WAVE_STEPS - 1):
        parts, states = forward(list(zip(doubles, previous, *dose)))
        previous, current = current, [field for field, _ in states]
        dose = [[total for _, total in states]]
        doubles = doubled(parts)
    dose = dose[0] if dose else [jnp.zeros(each.shape, F32) for each in current]
    updated, sides, ahead = [], [], []
    for fresh, *rest in zip(doubles, previous, dose, cut_up(heat), cut_up(absorb)):
        fresh, *ahead = lax.optimization_barrier((fresh, *ahead))
        if ahead:
            sides.append(ahead)
        updated.append(update(fresh, *rest))
        ahead = halo(updated[-1][2], not sides)
    sides.append(ahead)
    pressure = jnp.concatenate([each[0] for each in updated], axis=0)
    sources = [each[1] for each in updated]
    heats = [each[2] for each in updated]
    for _ in range(HEAT_STEPS - 2):
        heats = cut_up(warm(heats, sources, sides, perfuse, False))
        sides = [halo(each, index == 0) for index, each in enumerate(heats)]
    return jnp.transpose(pressure, (1, 0, 2)), warm(heats, sources, sides, perfuse, True)


def solution(mesh):
    return jax.shard_map(
        on_device,
        mesh=mesh,
        in_specs=(
            P("pencil", None, None),
            P("pencil", None, None),
            P("term", "pencil", None, None),
            P("term", None, "pencil", None),
            P("pencil", "term", None),
            P(),
            P("pencil", "term", None),
        ),
        out_specs=(P("pencil", "term", None), P("pencil", "term", None)),
        check_vma=False,
    )
```

```python
import functools
import math

import jax
import jax.numpy as jnp
import ml_dtypes
import numpy as np
from jax import lax
from jax.experimental import pallas as pl
from jax.experimental.pallas import tpu as pltpu
from jax.sharding import PartitionSpec as P

WAVE_STEPS = 2
HEAT_STEPS = 2
DIFFUSION = 0.125
VMEM_BYTES = 56 * 1024 * 1024
F32 = jnp.float32
BF16 = jnp.bfloat16


def halves(table):
    high = table.astype(ml_dtypes.bfloat16)
    low = (table - high.astype(np.float64)).astype(ml_dtypes.bfloat16)
    return high, low


def angles(left, right, length):
    return (np.outer(left, right) % length) * (2.0 * math.pi / length)


def slot_wavenumbers(blocks, length_z):
    width = length_z // blocks
    half = width // 2
    slots = np.concatenate([[half], np.arange(1, half)])
    starts = np.arange(blocks) * width
    return starts[:, None] + slots[None, :], starts


def forward_z_table(blocks, length_z):
    main, first = slot_wavenumbers(blocks, length_z)
    z = np.arange(length_z)
    theta = angles(z, main.reshape(-1), length_z).reshape(length_z, blocks, -1)
    real, imag = np.cos(theta), -np.sin(theta)
    for q in range(blocks // 2):
        real[:, q, 0], imag[:, q, 0] = -imag[:, q, 0].copy(), real[:, q, 0].copy()
    theta = angles(z, first, length_z)
    real0, imag0 = np.cos(theta), -np.sin(theta)
    for q in range(blocks // 2 + 1, blocks):
        real0[:, q], imag0[:, q] = imag0[:, q].copy(), -real0[:, q].copy()
    table = np.concatenate(
        [np.stack([real, imag], 2).reshape(length_z, -1), np.stack([real0, imag0], 2).reshape(length_z, -1)], axis=1
    )
    spare = -table.shape[1] % 128
    return np.pad(table, ((0, 0), (0, spare)))


def inverse_z_table(blocks, length_z, scale):
    main, first = slot_wavenumbers(blocks, length_z)
    z = np.arange(length_z)
    theta = angles(main.reshape(-1), z, length_z).reshape(blocks, -1, length_z)
    real, imag = np.cos(theta), -np.sin(theta)
    for p in range(blocks):
        middle = theta[p, 0]
        imag[p, 0] = np.cos(middle) if p < blocks // 2 else -np.sin(middle)
        lowest = angles(first[p : p + 1], z, length_z)[0]
        real[p, 0] = np.cos(lowest) if p <= blocks // 2 else -np.sin(lowest)
    return scale * np.concatenate([real.reshape(-1, length_z), imag.reshape(-1, length_z)], axis=0)


def forward_x_table(length_x):
    x = np.arange(length_x)
    theta = angles(x, x, length_x)
    return np.concatenate([np.cos(theta), np.sin(theta)], axis=1)


def inverse_x_table(blocks, length_x):
    x = np.arange(length_x)
    theta = angles(x, x, length_x).reshape(length_x, blocks, -1)
    cosine, sine = np.cos(theta), np.sin(theta)
    real_rows = np.stack([cosine, sine], axis=2).reshape(length_x, -1)
    imag_rows = np.stack([-sine, cosine], axis=2).reshape(length_x, -1)
    return np.concatenate([real_rows, imag_rows], axis=0)


def mirror_table(length):
    x = np.arange(length)
    table = np.zeros((length, length), ml_dtypes.bfloat16)
    table[x, (-x) % length] = 1
    return table


def turned_by(a, b, k, count, sign):
    if k == 0:
        return a, b
    if 4 * k == count:
        return (-b, a) if sign > 0 else (b, -a)
    angle = 2.0 * math.pi * k / count
    c, s = math.cos(angle), sign * math.sin(angle)
    if 8 * k == count or 8 * k == 3 * count:
        root = math.sqrt(0.5)
        sum_ab, less_ab = root * (a + b), root * (a - b)
        if c > 0:
            return (less_ab, sum_ab) if s > 0 else (sum_ab, -less_ab)
        return (-sum_ab, less_ab) if s > 0 else (-less_ab, -sum_ab)
    return c * a - s * b, c * b + s * a


def fourier(values, sign, wanted=None):
    count = len(values)
    wanted = range(count) if wanted is None else wanted
    if not wanted:
        return {}
    if count == 1:
        return {0: values[0]}
    if count % 2:
        out = {}
        for k in wanted:
            real, imag = values[0]
            for n in range(1, count):
                angle = 2.0 * math.pi * (k * n % count) / count
                c, s = math.cos(angle), sign * math.sin(angle)
                a, b = values[n]
                real, imag = real + (c * a - s * b), imag + (c * b + s * a)
            out[k] = (real, imag)
        return out
    half = count // 2
    out = {}
    even = [k // 2 for k in wanted if k % 2 == 0]
    odd = [k // 2 for k in wanted if k % 2]
    if even:
        added = [(values[n][0] + values[n + half][0], values[n][1] + values[n + half][1]) for n in range(half)]
        for k, value in fourier(added, sign, even).items():
            out[2 * k] = value
    if odd:
        less = [
            turned_by(values[n][0] - values[n + half][0], values[n][1] - values[n + half][1], n, count, sign)
            for n in range(half)
        ]
        for k, value in fourier(less, sign, odd).items():
            out[2 * k + 1] = value
    return out


def split(values):
    high = values.astype(BF16)
    return high, (values - high.astype(F32)).astype(BF16)


def dot(left, right):
    return jnp.dot(left, right, preferred_element_type=F32)


def dot_across(left, right):
    return lax.dot_general(left, right, (((1,), (1,)), ((), ())), preferred_element_type=F32)


def dot_three(high, low, table_high, table_low):
    return dot(high, table_high) + (dot(low, table_high) + dot(high, table_low))


def dot_stacked(both, table_high, table_low):
    count = both.shape[0] // 2
    by_high = dot(both, table_high)
    return by_high[:count] + (by_high[count:] + dot(both[:count], table_low))


def params(count=0):
    return pltpu.CompilerParams(vmem_limit_bytes=VMEM_BYTES, dimension_semantics=("arbitrary",) * count)


def cost(flops, moved):
    return pl.CostEstimate(flops=int(flops), bytes_accessed=int(moved), transcendentals=0)


def whole(shape, grid_rank):
    return pl.BlockSpec(shape, lambda *_: (0,) * len(shape), pipeline_mode=pl.Buffered(1)) if grid_rank else pl.BlockSpec(
        memory_space=pltpu.VMEM
    )


def forward_z_kernel(*refs, inputs):
    fresh_ref, *older = refs[:inputs]
    high_ref, low_ref, first_high_ref, first_low_ref, out_ref, *state = refs[inputs:]
    width, rows, length_z = fresh_ref.shape
    blocks = out_ref.shape[0]
    main = length_z // blocks
    brick = fresh_ref[...]
    if older:
        brick = brick - older[0][...]
        state[0][...] = brick
        dose = brick * brick
        state[1][...] = dose + older[1][...] if len(older) > 1 else dose
    high, low = split(brick.reshape(width * rows, length_z))
    result = dot_three(high, low, high_ref[...], low_ref[...])
    first = (
        dot_across(first_high_ref[...], high)
        + (dot_across(first_low_ref[...], high) + dot_across(first_high_ref[...], low))
    )
    out_ref[:, rows:, :] = jnp.zeros_like(out_ref[:, rows:, :])
    for q in range(blocks):
        for w in range(width):
            out_ref[q, :rows, w * main : (w + 1) * main] = result[w * rows : (w + 1) * rows, q * main : (q + 1) * main]
            for c in range(2):
                row = rows + c * width + w
                out_ref[q, row : row + 1, :rows] = first[2 * q + c : 2 * q + c + 1, w * rows : (w + 1) * rows]


def forward_z(bricks, blocks):
    width, rows, length_z = bricks[0].shape
    lanes = max(width * length_z // blocks, rows)
    table = forward_z_table(blocks, length_z)
    high, low = halves(table[:, :length_z])
    first_high, first_low = halves(table[:, length_z : length_z + 2 * blocks].T)
    tables = [jnp.asarray(each) for each in (high, low, first_high, first_low)]
    out = [jax.ShapeDtypeStruct((blocks, rows + 2 * width + (-2 * width) % 8, lanes), F32)]
    if len(bricks) > 1:
        out += [jax.ShapeDtypeStruct(bricks[0].shape, F32)] * 2
    return pl.pallas_call(
        functools.partial(forward_z_kernel, inputs=len(bricks)),
        out_shape=out,
        compiler_params=params(),
        cost_estimate=cost(6 * width * rows * length_z * length_z, 16 * width * rows * length_z),
        name="forward_z",
    )(*bricks, *tables)


def forward_x_kernel(data_ref, high_ref, low_ref, out_ref, *, width, half, rows):
    blocks = data_ref.shape[0]
    length_x = blocks * rows
    main = width * 2 * half
    turned = data_ref[:, :rows, :main].reshape(length_x, main).T
    first = jnp.concatenate([data_ref[q, rows:, :rows] for q in range(blocks)], axis=1)
    high, low = split(jnp.concatenate([turned, first], axis=0))
    both = dot_three(high, low, high_ref[...], low_ref[...])
    by_cos, by_sin = both[:, :length_x], both[:, length_x:]
    for w in range(width):
        re, im = w * 2 * half, w * 2 * half + half
        out_ref[re : re + half] = by_cos[re : re + half] + by_sin[im : im + half]
        out_ref[im : im + half] = by_cos[im : im + half] - by_sin[re : re + half]
    re, im, end = main, main + width, main + 2 * width
    out_ref[re:im] = by_cos[re:im] + by_sin[im:end]
    out_ref[im:end] = by_cos[im:end] - by_sin[re:im]
    if end < out_ref.shape[0]:
        out_ref[end:] = jnp.zeros_like(out_ref[end:])


def forward_x(data, width, half, rows):
    blocks = data.shape[0]
    length_x = blocks * rows
    out_rows = width * 2 * half + data.shape[1] - rows
    high, low = halves(forward_x_table(length_x))
    return pl.pallas_call(
        functools.partial(forward_x_kernel, width=width, half=half, rows=rows),
        out_shape=jax.ShapeDtypeStruct((out_rows, length_x), F32),
        compiler_params=params(),
        cost_estimate=cost(12 * out_rows * length_x * length_x, 8 * out_rows * length_x),
        name="forward_x",
    )(data, jnp.asarray(high), jnp.asarray(low))


def spread_kernel(*refs, spans, counts, group, pieces, first_term):
    parts, at = [], 0
    for count in counts:
        parts.append(refs[at : at + count])
        at += count
    me_ref, first_ref, own_ref = refs[at : at + 3]
    others = refs[at + 3 : at + 3 + len(pieces)]
    (
        high_ref, low_ref, out_ref,
        fk_ref, edge_in_ref, edge_ref, edge_out_ref, u_ref, u_both_ref,
    ) = refs[at + 3 + len(pieces) :]
    length_y, _, half, length_x = fk_ref.shape
    lanes_out = out_ref.shape[-1]
    rows_x = lanes_out // 2
    count_y = out_ref.shape[2]
    width = spans[-1][1]
    holders = length_y // width
    step = pl.program_id(0)
    tiles = [slice(at, at + 128) for at in range(0, length_x, 128)]
    wanted = [y for y in range(length_y) if group[0] <= y % width < group[1]]

    @pl.when(step == 0)
    def _():
        for part, (start, end) in zip(parts, spans):
            wide = end - start
            for d in range(holders):
                if len(part) == 1:
                    source, holder = part[0].at[d], d
                else:
                    source, holder = part[d], lax.rem(me_ref[0] + d, holders)
                for w in range(wide):
                    y = holder * width + start + w
                    fk_ref[y, 0] = source[w * 2 * half : w * 2 * half + half]
                    fk_ref[y, 1] = source[w * 2 * half + half : (w + 1) * 2 * half]
                    row = wide * 2 * half + w
                    edge_in_ref[y, :1] = source[row : row + 1]
                    edge_in_ref[y, 1:2] = source[row + wide : row + wide + 1]

        @pl.loop(0, half // 8)
        def _(tile):
            at = pl.ds(pl.multiple_of(tile * 8, 8), 8)
            for lanes in tiles:
                values = [(fk_ref[y, 0, at, lanes], fk_ref[y, 1, at, lanes]) for y in range(length_y)]
                values = fourier(values, -1)
                for y in range(length_y):
                    fk_ref[y, 0, at, lanes] = values[y][0]
                    fk_ref[y, 1, at, lanes] = values[y][1]

        for index, lanes in enumerate(tiles):
            values = [(edge_in_ref[y, :1, lanes], edge_in_ref[y, 1:2, lanes]) for y in range(length_y)]
            values = fourier(values, -1)
            factors = [first_ref[y, :, lanes] for y in range(length_y)]
            values = [(factors[y] * values[y][0], factors[y] * values[y][1]) for y in range(length_y)]
            values = fourier(values, 1, wanted)
            for n, y in enumerate(wanted):
                edge_ref[n, :, index * 128 : index * 128 + 128] = values[y][0]
                edge_ref[n, :, length_x + index * 128 : length_x + index * 128 + 128] = values[y][1]
        high, low = split(edge_ref[...].reshape(-1, 2 * length_x))
        edge_out_ref[...] = dot_three(high, low, high_ref[...], low_ref[...])

    row_index = lax.broadcasted_iota(jnp.int32, (8, 128), 0)

    def weigh(other_ref):
        @pl.loop(0, half // 8)
        def _(tile):
            at = pl.ds(pl.multiple_of(tile * 8, 8), 8)
            swapped = jnp.logical_and(row_index == 0, tile == 0)
            for index, lanes in enumerate(tiles):
                values = []
                for y in range(length_y):
                    own = jnp.where(swapped, own_ref[0, y, half : half + 1, lanes], own_ref[0, y, at, lanes])
                    factor = own + other_ref[0, y, at, lanes]
                    values.append((factor * fk_ref[y, 0, at, lanes], factor * fk_ref[y, 1, at, lanes]))
                values = fourier(values, 1, wanted)
                for n, y in enumerate(wanted):
                    rows = pl.ds(pl.multiple_of(n * half + tile * 8, 8), 8)
                    u_ref[rows, index * 128 : index * 128 + 128] = values[y][0]
                    u_ref[rows, length_x + index * 128 : length_x + index * 128 + 128] = values[y][1]

    if len(others) == 1:
        weigh(others[0])
    else:
        for other_ref, (start, end) in zip(others, pieces):
            pl.when(jnp.logical_and(step >= start, step < end))(functools.partial(weigh, other_ref))

    @pl.loop(0, count_y * half // 64)
    def _(part):
        rows = pl.ds(pl.multiple_of(part * 64, 64), 64)
        high, low = split(u_ref[rows, :])
        u_both_ref[rows, :] = high
        u_both_ref[pl.ds(pl.multiple_of(count_y * half + part * 64, 64), 64), :] = low

    lane_index = lax.broadcasted_iota(jnp.int32, (8, lanes_out), 1)
    row_index = lax.broadcasted_iota(jnp.int32, (8, lanes_out), 0)
    swapped = jnp.logical_and(row_index == 0, lane_index < rows_x)
    count = 256 // lanes_out
    for part in range(2 * length_x // 256):
        cols = slice(part * 256, part * 256 + 256)
        result = dot_stacked(u_both_ref[...], high_ref[:, cols], low_ref[:, cols])
        edges = [edge_out_ref[pl.ds(n * first_ref.shape[1] + step + first_term, 1), cols] for n in range(count_y)]
        for k in range(count):
            q = part * count + k
            inside = slice(k * lanes_out, (k + 1) * lanes_out)
            piece = result[:, inside]
            for n in range(count_y):
                top = piece[n * half : n * half + 8]
                out_ref[q, 0, n, :8, :] = jnp.where(swapped, edges[n][:, inside], top)
                out_ref[q, 0, n, 8:, :] = piece[n * half + 8 : (n + 1) * half]


def spread(parts, spans, me, first, own, others, blocks, group, chosen):
    _, length_y, _, length_x = own.shape
    half = own.shape[2] // 2
    first_term, end_term = chosen
    terms = end_term - first_term
    count_y = length_y // spans[-1][1] * (group[1] - group[0])
    rows_x = length_x // blocks
    high, low = halves(inverse_x_table(blocks, length_x))
    high, low = jnp.asarray(high), jnp.asarray(low)
    rows = count_y * half
    others = [each for each in others if each[0] < end_term and each[1] > first_term]

    def piece_spec(start, end):
        return pl.BlockSpec(
            (1, length_y, half, length_x), lambda t: (jnp.clip(t + first_term - start, 0, end - start - 1), 0, 0, 0)
        )

    return pl.pallas_call(
        functools.partial(
            spread_kernel, spans=spans, counts=[len(part) for part in parts], group=group, first_term=first_term,
            pieces=[(start - first_term, end - first_term) for start, end, _ in others],
        ),
        grid=(terms,),
        in_specs=[whole(array.shape, 1) for part in parts for array in part] + [
            pl.BlockSpec(memory_space=pltpu.SMEM),
            whole(first.shape, 1),
            pl.BlockSpec((1, length_y, half + 8, length_x), lambda t: (t + first_term, 0, 0, 0)),
        ] + [piece_spec(start, end) for start, end, _ in others] + [
            whole(high.shape, 1),
            whole(low.shape, 1),
        ],
        out_specs=pl.BlockSpec((blocks, 1, count_y, half, 2 * rows_x), lambda t: (0, t, 0, 0, 0)),
        out_shape=jax.ShapeDtypeStruct((blocks, terms, count_y, half, 2 * rows_x), F32),
        scratch_shapes=[
            pltpu.VMEM((length_y, 2, half, length_x), F32),
            pltpu.VMEM((length_y, 8, length_x), F32),
            pltpu.VMEM((count_y, first.shape[1], 2 * length_x), F32),
            pltpu.VMEM((count_y * first.shape[1], 2 * length_x), F32),
            pltpu.VMEM((rows, 2 * length_x), F32),
            pltpu.VMEM((2 * rows, 2 * length_x), BF16),
        ],
        compiler_params=params(1),
        cost_estimate=cost(terms * 24 * rows * length_x * length_x, terms * 16 * rows * length_x),
        name="spread",
    )(*[array for part in parts for array in part], me, first, own, *[array for _, _, array in others], high, low)


def gather_kernel(*refs):
    *data_refs, factor_ref, high_ref, low_ref, out_ref = refs
    blocks, _, wide, half, lanes = data_refs[0].shape
    rows = lanes // 2
    for y in range(wide):
        parts = []
        for data_ref in data_refs:
            for t in range(data_ref.shape[1]):
                turned = data_ref[:, t, y].reshape(blocks * half, lanes).T
                parts.append(jnp.concatenate([turned[:rows], turned[rows:]], axis=1))
        high, low = split(jnp.concatenate(parts, axis=0))
        fields = dot_stacked(jnp.concatenate([high, low], axis=0), high_ref[...], low_ref[...])
        total = factor_ref[0, y] * fields[:rows]
        for t in range(1, len(parts)):
            total = total + factor_ref[t, y] * fields[t * rows : (t + 1) * rows]
        out_ref[y] = total


def gather(chunks, factor, scale, width, group):
    blocks, _, _, half, lanes = chunks[0].shape
    terms, length_y, rows, length_z = factor.shape
    wide = group[1] - group[0]
    holders = length_y // width
    high, low = halves(inverse_z_table(blocks, length_z, scale))

    def row(n):
        return (n * width + group[0]) // wide

    def chunk_spec(shape):
        full = shape[2] == length_y
        return pl.BlockSpec((blocks, shape[1], wide, half, lanes), lambda n: (0, 0, row(n) if full else n, 0, 0))

    return pl.pallas_call(
        gather_kernel,
        grid=(holders,),
        in_specs=[chunk_spec(chunk.shape) for chunk in chunks] + [
            pl.BlockSpec((terms, wide, rows, length_z), lambda n: (0, row(n), 0, 0)),
            whole(high.shape, 1),
            whole(low.shape, 1),
        ],
        out_specs=pl.BlockSpec((wide, rows, length_z), lambda n: (n, 0, 0)),
        out_shape=jax.ShapeDtypeStruct((holders * wide, rows, length_z), F32),
        compiler_params=params(1),
        cost_estimate=cost(
            6 * terms * holders * wide * rows * length_z * length_z, 8 * terms * holders * wide * rows * length_z
        ),
        name="gather_z",
    )(*chunks, factor, jnp.asarray(high), jnp.asarray(low))


def mirror_kernel(in_ref, table_ref, out_ref, turned_ref):
    _, length_y, half, length_x = in_ref.shape
    high, low = split(in_ref[0].reshape(length_y * half, length_x))
    rest = in_ref[0].reshape(length_y * half, length_x) - high.astype(F32) - low.astype(F32)
    table = table_ref[...]
    turned = (dot(high, table) + dot(low, table)) + dot(rest.astype(BF16), table)
    turned_ref[...] = turned.reshape(length_y, half, length_x)
    for y in range(length_y):
        source = -y % length_y
        for s in range(half):
            row = -s % half
            out_ref[0, y, s : s + 1, :] = turned_ref[source, row : row + 1, :]


def mirror(multiplier, start, end):
    _, length_y, width, length_x = multiplier.shape
    half = width // 2
    terms = end - start
    table = mirror_table(length_x)
    return pl.pallas_call(
        mirror_kernel,
        grid=(terms,),
        in_specs=[
            pl.BlockSpec((1, length_y, half, length_x), lambda t: (t + start, 0, 1, 0)),
            whole(table.shape, 1),
        ],
        out_specs=pl.BlockSpec((1, length_y, half, length_x), lambda t: (t, 0, 0, 0)),
        out_shape=jax.ShapeDtypeStruct((terms, length_y, half, length_x), F32),
        scratch_shapes=[pltpu.VMEM((length_y, half, length_x), F32)],
        compiler_params=params(1),
        cost_estimate=cost(6 * terms * length_y * half * length_x * length_x, 8 * terms * length_y * half * length_x),
        name="mirror",
    )(multiplier, jnp.asarray(table))


def flip(values, axis):
    return jnp.roll(jnp.flip(values, axis), 1, axis)


def padded_by_one(block, sides):
    for axis, dim in sides:
        count = lax.axis_size(axis)
        forward = [(i, i + 1) for i in range(count - 1)]
        backward = [(target, source) for source, target in forward]
        size = block.shape[dim]
        low = lax.ppermute(lax.slice_in_dim(block, size - 1, size, axis=dim), axis, forward)
        high = lax.ppermute(lax.slice_in_dim(block, 0, 1, axis=dim), axis, backward)
        yield dim, low, high


def halos_of(heat):
    return [side for _, low, high in padded_by_one(heat, (("term", 0), ("pencil", 1))) for side in (low, high)]


def heat_step(heat, halos, perfuse):
    near = jnp.zeros_like(heat)
    for dim, (low, high) in enumerate(zip(halos[::2], halos[1::2])):
        size = heat.shape[dim]
        near = near + jnp.concatenate([low, lax.slice_in_dim(heat, 0, size - 1, axis=dim)], axis=dim)
        near = near + jnp.concatenate([lax.slice_in_dim(heat, 1, size, axis=dim), high], axis=dim)
    deep = jnp.pad(heat, ((0, 0), (0, 0), (1, 1)))
    near = near + deep[:, :, 2:] + deep[:, :, :-2]
    return heat + DIFFUSION * (near - 6.0 * heat) - perfuse * heat


def update_kernel(fresh_ref, old_ref, dose_ref, heat_ref, absorb_ref, pressure_ref, source_ref, out_ref):
    field = fresh_ref[...] - old_ref[...]
    source = absorb_ref[...] * (dose_ref[...] + field * field)
    pressure_ref[...] = field
    source_ref[...] = source
    out_ref[...] = heat_ref[...] + source


def update(fresh, old, dose, heat, absorb):
    return pl.pallas_call(
        update_kernel,
        out_shape=[jax.ShapeDtypeStruct(fresh.shape, F32)] * 3,
        compiler_params=params(),
        cost_estimate=cost(5 * fresh.size, 32 * fresh.size),
        name="update",
    )(fresh, old, dose, heat, absorb)


def warm_kernel(*refs, groups, turned):
    heat_refs, source_refs, low_refs, high_refs = [refs[k * groups : (k + 1) * groups] for k in range(4)]
    below_ref, above_ref, perfuse_ref, out_ref = refs[4 * groups :]
    rows, length_z = below_ref.shape[1:]
    planes, sources, lows, highs = [], [], [], []
    for heat_ref, source_ref, low_ref, high_ref in zip(heat_refs, source_refs, low_refs, high_refs):
        for w in range(heat_ref.shape[0]):
            planes.append(heat_ref[w])
            sources.append(source_ref[w])
            lows.append(low_ref[w])
            highs.append(high_ref[w])
    row = lax.broadcasted_iota(jnp.int32, (rows, length_z), 0)
    lane = lax.broadcasted_iota(jnp.int32, (rows, length_z), 1)
    for w, heat in enumerate(planes):
        near = jnp.where(row == 0, lows[w], pltpu.roll(heat, 1, 0))
        near = near + jnp.where(row == rows - 1, highs[w], pltpu.roll(heat, rows - 1, 0))
        near = near + (planes[w - 1] if w else below_ref[0])
        near = near + (planes[w + 1] if w + 1 < len(planes) else above_ref[0])
        near = near + jnp.where(lane == 0, 0.0, pltpu.roll(heat, 1, 1))
        near = near + jnp.where(lane == length_z - 1, 0.0, pltpu.roll(heat, length_z - 1, 1))
        fresh = heat + DIFFUSION * (near - 6.0 * heat) - perfuse_ref[w] * heat + sources[w]
        if turned:
            out_ref[:, w, :] = fresh
        else:
            out_ref[w] = fresh


def halo(heat, lowest):
    (_, low, high), = padded_by_one(heat, (("pencil", 1),))
    if not lowest:
        return [low, high]
    backward = [(i + 1, i) for i in range(lax.axis_size("term") - 1)]
    return [low, high, lax.ppermute(heat[:1], "term", backward)]


def warm(heats, sources, sides, perfuse, turned):
    width, rows, length_z = perfuse.shape
    above = sides[0][2]
    below = lax.ppermute(heats[-1][-1:], "term", [(i, i + 1) for i in range(lax.axis_size("term") - 1)])
    return pl.pallas_call(
        functools.partial(warm_kernel, groups=len(heats), turned=turned),
        out_shape=jax.ShapeDtypeStruct((rows, width, length_z) if turned else perfuse.shape, F32),
        compiler_params=params(),
        cost_estimate=cost(16 * perfuse.size, 16 * perfuse.size),
        name="warm",
    )(*heats, *sources, *[side[0] for side in sides], *[side[1] for side in sides], below, above, perfuse)


def on_device(
    present_acoustic,
    prior_acoustic,
    location_factor,
    spectral_multiplier,
    medium_kinds,
    organ_properties,
    thermal_increase,
):
    term_count = lax.axis_size("term")
    blocks = lax.axis_size("pencil")
    rows, length_y, length_z = present_acoustic.shape
    length_x = rows * blocks
    width = length_y // term_count
    half = length_z // blocks // 2
    terms = location_factor.shape[0]
    brick_start = lax.axis_index("term") * width
    scale = 2.0 / (length_x * length_y * length_z)

    cut = width // 2 if width >= 4 else width
    spans = [(0, cut), (cut, width)] if cut < width else [(0, width)]

    def to_brick(values):
        return jnp.transpose(lax.dynamic_slice_in_dim(values, brick_start, width, 1), (1, 0, 2))

    def cut_up(brick):
        return [brick[start:end] for start, end in spans]

    def exchange(values):
        return lax.all_to_all(values, "pencil", 0, 0, tiled=True)

    opposite = [(p, blocks - 1 - p) for p in range(blocks)]
    middle = terms // 2
    sent = forward_z([to_brick(present_acoustic)], blocks)[0]
    sent, multiplier = lax.optimization_barrier((sent, spectral_multiplier))
    sent = exchange(sent)
    lowest = spectral_multiplier[:, :, 0, :]
    thermal = jnp.transpose(thermal_increase, (1, 0, 2))
    others, before = [], None
    for start, end in ((0, middle), (middle, terms)):
        if end > start:
            mirrored = mirror(multiplier, start, end)
            if others:
                mirrored, before, lowest, *halos = lax.optimization_barrier((mirrored, before, lowest, *halos))
                others = [(*others[0][:2], before)]
            else:
                mirrored, lowest, thermal = lax.optimization_barrier((mirrored, lowest, thermal))
                halos = halos_of(thermal)
            before = lax.ppermute(mirrored, "pencil", opposite)
            if not others:
                lowest = lowest + lax.ppermute(
                    flip(flip(lowest, 1), 2),
                    "pencil",
                    [(p, blocks - p) for p in range(1, blocks) if 2 * p != blocks],
                )
            others.append((start, end, before))
    lowest = jnp.transpose(lowest, (1, 0, 2))
    lowest = jnp.pad(lowest, ((0, 0), (0, -terms % 8), (0, 0)))
    me = lax.axis_index("term").reshape(1).astype(jnp.int32)
    factor = jnp.transpose(location_factor, (0, 2, 1, 3))
    last, factor = lax.optimization_barrier((others[0][2], factor))
    others[0] = (*others[0][:2], last)

    def gathered(part, offload):
        if offload or term_count == 1:
            return [lax.all_gather(part, "term", axis=0, tiled=False)]
        return [part] + [
            lax.ppermute(part, "term", [(i, (i - d) % term_count) for i in range(term_count)])
            for d in range(1, term_count)
        ]

    def spread_from(parts, sent_spans, group, chosen):
        out = spread(parts, sent_spans, me, lowest, spectral_multiplier, others, blocks, group, chosen)
        flat, tree = jax.tree.flatten(parts)
        out, *flat = lax.optimization_barrier((out, *flat))
        return out, jax.tree.unflatten(tree, flat)

    def summed(chunks, group):
        partial = gather(chunks, factor, scale, width, group)
        return lax.psum_scatter(partial, "term", scatter_dimension=0, tiled=True)

    def doubled_first(part, tied):
        parts = [[lax.all_gather(part, "term", axis=0, tiled=False)]]
        shared, chunks, bricks = [], {}, []
        if middle:
            out, parts = spread_from(parts, [(0, width)], (0, width), (0, middle))
            out, last = lax.optimization_barrier((out, others[-1][2]))
            others[-1] = (*others[-1][:2], last)
            shared = [exchange(out)]
        before = shared
        for index, group in enumerate(spans):
            out, parts = spread_from(parts, [(0, width)], group, (middle, terms))
            out, *before = lax.optimization_barrier((out, *before))
            if index == 0:
                shared = before
            out = exchange(out)
            before = [out]
            if index == 0:
                out, *tied = lax.optimization_barrier((out, *tied))
            bricks.append(summed(shared + [out], group))
        return bricks, tied

    def doubled(parts):
        bricks, before = [], []
        for group in spans:
            out, parts = spread_from(parts, spans, group, (0, terms))
            out, *before = lax.optimization_barrier((out, *before))
            if before:
                chunks[0] = before[0]
                bricks.append(summed(chunks, spans[0]))
            chunks = [exchange(out)]
            before = list(chunks)
        bricks.append(summed(chunks, spans[-1]))
        return bricks

    def forward(bricks):
        parts, states, before = [], [], []
        for (start, end), (fresh, *older) in zip(spans, bricks):
            fresh, *before = lax.optimization_barrier((fresh, *before))
            if before:
                parts.append(gathered(before[0], True))
            sent, *state = forward_z([fresh, *older], blocks)
            sent = exchange(sent)
            before = [forward_x(sent, end - start, half, rows)]
            states.append(state)
        parts.append(gathered(before[0], False))
        return parts, states

    kinds = jnp.transpose(medium_kinds, (1, 0, 2))
    absorb, perfuse = [
        jnp.where(
            kinds == 0,
            organ_properties[0, at],
            jnp.where(kinds == 1, organ_properties[1, at], organ_properties[2, at]),
        )
        for at in range(2)
    ]
    heat = heat_step(thermal, halos, perfuse)

    previous = cut_up(to_brick(prior_acoustic))
    current = cut_up(to_brick(present_acoustic))
    dose = []
    doubles, (heat, absorb, perfuse) = doubled_first(forward_x(sent, width, half, rows), (heat, absorb, perfuse))
    for _ in range(WAVE_STEPS - 1):
        parts, states = forward(list(zip(doubles, previous, *dose)))
        previous, current = current, [field for field, _ in states]
        dose = [[total for _, total in states]]
        doubles = doubled(parts)
    dose = dose[0] if dose else [jnp.zeros(each.shape, F32) for each in current]
    updated, sides, ahead = [], [], []
    for fresh, *rest in zip(doubles, previous, dose, cut_up(heat), cut_up(absorb)):
        fresh, *ahead = lax.optimization_barrier((fresh, *ahead))
        if ahead:
            sides.append(ahead)
        updated.append(update(fresh, *rest))
        ahead = halo(updated[-1][2], not sides)
    sides.append(ahead)
    pressure = jnp.concatenate([each[0] for each in updated], axis=0)
    sources = [each[1] for each in updated]
    heats = [each[2] for each in updated]
    for _ in range(HEAT_STEPS - 2):
        heats = cut_up(warm(heats, sources, sides, perfuse, False))
        sides = [halo(each, index == 0) for index, each in enumerate(heats)]
    return jnp.transpose(pressure, (1, 0, 2)), warm(heats, sources, sides, perfuse, True)


def solution(mesh):
    return jax.shard_map(
        on_device,
        mesh=mesh,
        in_specs=(
            P("pencil", None, None),
            P("pencil", None, None),
            P("term", "pencil", None, None),
            P("term", None, "pencil", None),
            P("pencil", "term", None),
            P(),
            P("pencil", "term", None),
        ),
        out_specs=(P("pencil", "term", None), P("pencil", "term", None)),
        check_vma=False,
    )
```

```python
import functools
import math

import jax
import jax.numpy as jnp
import ml_dtypes
import numpy as np
from jax import lax
from jax.experimental import pallas as pl
from jax.experimental.pallas import tpu as pltpu
from jax.sharding import PartitionSpec as P

WAVE_STEPS = 2
HEAT_STEPS = 2
DIFFUSION = 0.125
VMEM_BYTES = 56 * 1024 * 1024
F32 = jnp.float32
BF16 = jnp.bfloat16


def halves(table):
    high = table.astype(ml_dtypes.bfloat16)
    low = (table - high.astype(np.float64)).astype(ml_dtypes.bfloat16)
    return high, low


def angles(left, right, length):
    return (np.outer(left, right) % length) * (2.0 * math.pi / length)


def slot_wavenumbers(blocks, length_z):
    width = length_z // blocks
    half = width // 2
    slots = np.concatenate([[half], np.arange(1, half)])
    starts = np.arange(blocks) * width
    return starts[:, None] + slots[None, :], starts


def forward_z_table(blocks, length_z):
    main, first = slot_wavenumbers(blocks, length_z)
    z = np.arange(length_z)
    theta = angles(z, main.reshape(-1), length_z).reshape(length_z, blocks, -1)
    real, imag = np.cos(theta), -np.sin(theta)
    for q in range(blocks // 2):
        real[:, q, 0], imag[:, q, 0] = -imag[:, q, 0].copy(), real[:, q, 0].copy()
    theta = angles(z, first, length_z)
    real0, imag0 = np.cos(theta), -np.sin(theta)
    for q in range(blocks // 2 + 1, blocks):
        real0[:, q], imag0[:, q] = imag0[:, q].copy(), -real0[:, q].copy()
    table = np.concatenate(
        [np.stack([real, imag], 2).reshape(length_z, -1), np.stack([real0, imag0], 2).reshape(length_z, -1)], axis=1
    )
    spare = -table.shape[1] % 128
    return np.pad(table, ((0, 0), (0, spare)))


def inverse_z_table(blocks, length_z, scale):
    main, first = slot_wavenumbers(blocks, length_z)
    z = np.arange(length_z)
    theta = angles(main.reshape(-1), z, length_z).reshape(blocks, -1, length_z)
    real, imag = np.cos(theta), -np.sin(theta)
    for p in range(blocks):
        middle = theta[p, 0]
        imag[p, 0] = np.cos(middle) if p < blocks // 2 else -np.sin(middle)
        lowest = angles(first[p : p + 1], z, length_z)[0]
        real[p, 0] = np.cos(lowest) if p <= blocks // 2 else -np.sin(lowest)
    return scale * np.concatenate([real.reshape(-1, length_z), imag.reshape(-1, length_z)], axis=0)


def forward_x_table(length_x):
    x = np.arange(length_x)
    theta = angles(x, x, length_x)
    return np.concatenate([np.cos(theta), np.sin(theta)], axis=1)


def inverse_x_table(blocks, length_x):
    x = np.arange(length_x)
    theta = angles(x, x, length_x).reshape(length_x, blocks, -1)
    cosine, sine = np.cos(theta), np.sin(theta)
    real_rows = np.stack([cosine, sine], axis=2).reshape(length_x, -1)
    imag_rows = np.stack([-sine, cosine], axis=2).reshape(length_x, -1)
    return np.concatenate([real_rows, imag_rows], axis=0)


def mirror_table(length):
    x = np.arange(length)
    table = np.zeros((length, length), ml_dtypes.bfloat16)
    table[x, (-x) % length] = 1
    return table


def turned_by(a, b, k, count, sign):
    if k == 0:
        return a, b
    if 4 * k == count:
        return (-b, a) if sign > 0 else (b, -a)
    angle = 2.0 * math.pi * k / count
    c, s = math.cos(angle), sign * math.sin(angle)
    if 8 * k == count or 8 * k == 3 * count:
        root = math.sqrt(0.5)
        sum_ab, less_ab = root * (a + b), root * (a - b)
        if c > 0:
            return (less_ab, sum_ab) if s > 0 else (sum_ab, -less_ab)
        return (-sum_ab, less_ab) if s > 0 else (-less_ab, -sum_ab)
    return c * a - s * b, c * b + s * a


def fourier(values, sign, wanted=None):
    count = len(values)
    wanted = range(count) if wanted is None else wanted
    if not wanted:
        return {}
    if count == 1:
        return {0: values[0]}
    if count % 2:
        out = {}
        for k in wanted:
            real, imag = values[0]
            for n in range(1, count):
                angle = 2.0 * math.pi * (k * n % count) / count
                c, s = math.cos(angle), sign * math.sin(angle)
                a, b = values[n]
                real, imag = real + (c * a - s * b), imag + (c * b + s * a)
            out[k] = (real, imag)
        return out
    half = count // 2
    out = {}
    even = [k // 2 for k in wanted if k % 2 == 0]
    odd = [k // 2 for k in wanted if k % 2]
    if even:
        added = [(values[n][0] + values[n + half][0], values[n][1] + values[n + half][1]) for n in range(half)]
        for k, value in fourier(added, sign, even).items():
            out[2 * k] = value
    if odd:
        less = [
            turned_by(values[n][0] - values[n + half][0], values[n][1] - values[n + half][1], n, count, sign)
            for n in range(half)
        ]
        for k, value in fourier(less, sign, odd).items():
            out[2 * k + 1] = value
    return out


def split(values):
    high = values.astype(BF16)
    return high, (values - high.astype(F32)).astype(BF16)


def dot(left, right):
    return jnp.dot(left, right, preferred_element_type=F32)


def dot_across(left, right):
    return lax.dot_general(left, right, (((1,), (1,)), ((), ())), preferred_element_type=F32)


def dot_three(high, low, table_high, table_low):
    return dot(high, table_high) + (dot(low, table_high) + dot(high, table_low))


def dot_stacked(both, table_high, table_low):
    count = both.shape[0] // 2
    by_high = dot(both, table_high)
    return by_high[:count] + (by_high[count:] + dot(both[:count], table_low))


def params(count=0):
    return pltpu.CompilerParams(vmem_limit_bytes=VMEM_BYTES, dimension_semantics=("arbitrary",) * count)


def cost(flops, moved):
    return pl.CostEstimate(flops=int(flops), bytes_accessed=int(moved), transcendentals=0)


def whole(shape, grid_rank):
    return pl.BlockSpec(shape, lambda *_: (0,) * len(shape), pipeline_mode=pl.Buffered(1)) if grid_rank else pl.BlockSpec(
        memory_space=pltpu.VMEM
    )


def forward_z_kernel(*refs, inputs):
    fresh_ref, *older = refs[:inputs]
    high_ref, low_ref, first_high_ref, first_low_ref, out_ref, *state = refs[inputs:]
    width, rows, length_z = fresh_ref.shape
    blocks = out_ref.shape[0]
    main = length_z // blocks
    brick = fresh_ref[...]
    if older:
        brick = brick - older[0][...]
        state[0][...] = brick
        dose = brick * brick
        state[1][...] = dose + older[1][...] if len(older) > 1 else dose
    high, low = split(brick.reshape(width * rows, length_z))
    result = dot_three(high, low, high_ref[...], low_ref[...])
    first = (
        dot_across(first_high_ref[...], high)
        + (dot_across(first_low_ref[...], high) + dot_across(first_high_ref[...], low))
    )
    out_ref[:, rows:, :] = jnp.zeros_like(out_ref[:, rows:, :])
    for q in range(blocks):
        for w in range(width):
            out_ref[q, :rows, w * main : (w + 1) * main] = result[w * rows : (w + 1) * rows, q * main : (q + 1) * main]
            for c in range(2):
                row = rows + c * width + w
                out_ref[q, row : row + 1, :rows] = first[2 * q + c : 2 * q + c + 1, w * rows : (w + 1) * rows]


def forward_z(bricks, blocks):
    width, rows, length_z = bricks[0].shape
    lanes = max(width * length_z // blocks, rows)
    table = forward_z_table(blocks, length_z)
    high, low = halves(table[:, :length_z])
    first_high, first_low = halves(table[:, length_z : length_z + 2 * blocks].T)
    tables = [jnp.asarray(each) for each in (high, low, first_high, first_low)]
    out = [jax.ShapeDtypeStruct((blocks, rows + 2 * width + (-2 * width) % 8, lanes), F32)]
    if len(bricks) > 1:
        out += [jax.ShapeDtypeStruct(bricks[0].shape, F32)] * 2
    return pl.pallas_call(
        functools.partial(forward_z_kernel, inputs=len(bricks)),
        out_shape=out,
        compiler_params=params(),
        cost_estimate=cost(6 * width * rows * length_z * length_z, 16 * width * rows * length_z),
        name="forward_z",
    )(*bricks, *tables)


def forward_x_kernel(data_ref, high_ref, low_ref, out_ref, *, width, half, rows):
    blocks = data_ref.shape[0]
    length_x = blocks * rows
    main = width * 2 * half
    turned = data_ref[:, :rows, :main].reshape(length_x, main).T
    first = jnp.concatenate([data_ref[q, rows:, :rows] for q in range(blocks)], axis=1)
    high, low = split(jnp.concatenate([turned, first], axis=0))
    both = dot_three(high, low, high_ref[...], low_ref[...])
    by_cos, by_sin = both[:, :length_x], both[:, length_x:]
    for w in range(width):
        re, im = w * 2 * half, w * 2 * half + half
        out_ref[re : re + half] = by_cos[re : re + half] + by_sin[im : im + half]
        out_ref[im : im + half] = by_cos[im : im + half] - by_sin[re : re + half]
    re, im, end = main, main + width, main + 2 * width
    out_ref[re:im] = by_cos[re:im] + by_sin[im:end]
    out_ref[im:end] = by_cos[im:end] - by_sin[re:im]
    if end < out_ref.shape[0]:
        out_ref[end:] = jnp.zeros_like(out_ref[end:])


def forward_x(data, width, half, rows):
    blocks = data.shape[0]
    length_x = blocks * rows
    out_rows = width * 2 * half + data.shape[1] - rows
    high, low = halves(forward_x_table(length_x))
    return pl.pallas_call(
        functools.partial(forward_x_kernel, width=width, half=half, rows=rows),
        out_shape=jax.ShapeDtypeStruct((out_rows, length_x), F32),
        compiler_params=params(),
        cost_estimate=cost(12 * out_rows * length_x * length_x, 8 * out_rows * length_x),
        name="forward_x",
    )(data, jnp.asarray(high), jnp.asarray(low))


def spread_kernel(*refs, spans, counts, group, pieces, first_term):
    parts, at = [], 0
    for count in counts:
        parts.append(refs[at : at + count])
        at += count
    me_ref, first_ref, own_ref = refs[at : at + 3]
    others = refs[at + 3 : at + 3 + len(pieces)]
    (
        high_ref, low_ref, out_ref,
        fk_ref, edge_in_ref, edge_ref, u_ref, u_both_ref,
    ) = refs[at + 3 + len(pieces) :]
    length_y, _, half, length_x = fk_ref.shape
    lanes_out = out_ref.shape[-1]
    rows_x = lanes_out // 2
    count_y = out_ref.shape[2]
    width = spans[-1][1]
    holders = length_y // width
    step = pl.program_id(0)
    tiles = [slice(at, at + 128) for at in range(0, length_x, 128)]
    wanted = [y for y in range(length_y) if group[0] <= y % width < group[1]]

    @pl.when(step == 0)
    def _():
        for part, (start, end) in zip(parts, spans):
            wide = end - start
            for d in range(holders):
                if len(part) == 1:
                    source, holder = part[0].at[d], d
                else:
                    source, holder = part[d], lax.rem(me_ref[0] + d, holders)
                for w in range(wide):
                    y = holder * width + start + w
                    fk_ref[y, 0] = source[w * 2 * half : w * 2 * half + half]
                    fk_ref[y, 1] = source[w * 2 * half + half : (w + 1) * 2 * half]
                    row = wide * 2 * half + w
                    edge_in_ref[y, :1] = source[row : row + 1]
                    edge_in_ref[y, 1:2] = source[row + wide : row + wide + 1]

        @pl.loop(0, half // 8)
        def _(tile):
            at = pl.ds(pl.multiple_of(tile * 8, 8), 8)
            for lanes in tiles:
                values = [(fk_ref[y, 0, at, lanes], fk_ref[y, 1, at, lanes]) for y in range(length_y)]
                values = fourier(values, -1)
                for y in range(length_y):
                    fk_ref[y, 0, at, lanes] = values[y][0]
                    fk_ref[y, 1, at, lanes] = values[y][1]

        for index, lanes in enumerate(tiles):
            values = [(edge_in_ref[y, :1, lanes], edge_in_ref[y, 1:2, lanes]) for y in range(length_y)]
            values = fourier(values, -1)
            factors = [first_ref[y, :, lanes] for y in range(length_y)]
            values = [(factors[y] * values[y][0], factors[y] * values[y][1]) for y in range(length_y)]
            values = fourier(values, 1, wanted)
            for n, y in enumerate(wanted):
                edge_ref[n, :, index * 128 : index * 128 + 128] = values[y][0]
                edge_ref[n, :, length_x + index * 128 : length_x + index * 128 + 128] = values[y][1]
    row_index = lax.broadcasted_iota(jnp.int32, (8, 128), 0)

    def weigh(other_ref):
        @pl.loop(0, half // 8)
        def _(tile):
            at = pl.ds(pl.multiple_of(tile * 8, 8), 8)
            swapped = jnp.logical_and(row_index == 0, tile == 0)
            for index, lanes in enumerate(tiles):
                values = []
                for y in range(length_y):
                    own = jnp.where(swapped, own_ref[0, y, half : half + 1, lanes], own_ref[0, y, at, lanes])
                    factor = own + other_ref[0, y, at, lanes]
                    values.append((factor * fk_ref[y, 0, at, lanes], factor * fk_ref[y, 1, at, lanes]))
                values = fourier(values, 1, wanted)
                for n, y in enumerate(wanted):
                    rows = pl.ds(pl.multiple_of(n * half + tile * 8, 8), 8)
                    u_ref[rows, index * 128 : index * 128 + 128] = values[y][0]
                    u_ref[rows, length_x + index * 128 : length_x + index * 128 + 128] = values[y][1]

    if len(others) == 1:
        weigh(others[0])
    else:
        for other_ref, (start, end) in zip(others, pieces):
            pl.when(jnp.logical_and(step >= start, step < end))(functools.partial(weigh, other_ref))

    main_rows = count_y * half
    all_rows = u_ref.shape[0]
    for n in range(count_y):
        u_ref[main_rows + n : main_rows + n + 1, :] = edge_ref[n, pl.ds(first_term + step, 1), :]
    if main_rows + count_y < all_rows:
        u_ref[main_rows + count_y :, :] = jnp.zeros_like(u_ref[main_rows + count_y :, :])

    @pl.loop(0, all_rows // 16)
    def _(part):
        high, low = split(u_ref[pl.ds(pl.multiple_of(part * 16, 16), 16), :])
        u_both_ref[pl.ds(pl.multiple_of(part * 16, 16), 16), :] = high
        u_both_ref[pl.ds(pl.multiple_of(all_rows + part * 16, 16), 16), :] = low

    lane_index = lax.broadcasted_iota(jnp.int32, (8, lanes_out), 1)
    row_index = lax.broadcasted_iota(jnp.int32, (8, lanes_out), 0)
    swapped = jnp.logical_and(row_index == 0, lane_index < rows_x)
    count = 256 // lanes_out
    for part in range(2 * length_x // 256):
        cols = slice(part * 256, part * 256 + 256)
        result = dot_stacked(u_both_ref[...], high_ref[:, cols], low_ref[:, cols])
        edges = [result[main_rows + n : main_rows + n + 1] for n in range(count_y)]
        for k in range(count):
            q = part * count + k
            inside = slice(k * lanes_out, (k + 1) * lanes_out)
            piece = result[:, inside]
            for n in range(count_y):
                top = piece[n * half : n * half + 8]
                out_ref[q, 0, n, :8, :] = jnp.where(swapped, edges[n][:, inside], top)
                out_ref[q, 0, n, 8:, :] = piece[n * half + 8 : (n + 1) * half]


def spread(parts, spans, me, first, own, others, blocks, group, chosen):
    _, length_y, _, length_x = own.shape
    half = own.shape[2] // 2
    first_term, end_term = chosen
    terms = end_term - first_term
    count_y = length_y // spans[-1][1] * (group[1] - group[0])
    rows_x = length_x // blocks
    high, low = halves(inverse_x_table(blocks, length_x))
    high, low = jnp.asarray(high), jnp.asarray(low)
    rows = count_y * half
    spare = count_y + -count_y % 16
    others = [each for each in others if each[0] < end_term and each[1] > first_term]

    def piece_spec(start, end):
        return pl.BlockSpec(
            (1, length_y, half, length_x), lambda t: (jnp.clip(t + first_term - start, 0, end - start - 1), 0, 0, 0)
        )

    return pl.pallas_call(
        functools.partial(
            spread_kernel, spans=spans, counts=[len(part) for part in parts], group=group, first_term=first_term,
            pieces=[(start - first_term, end - first_term) for start, end, _ in others],
        ),
        grid=(terms,),
        in_specs=[whole(array.shape, 1) for part in parts for array in part] + [
            pl.BlockSpec(memory_space=pltpu.SMEM),
            whole(first.shape, 1),
            pl.BlockSpec((1, length_y, half + 8, length_x), lambda t: (t + first_term, 0, 0, 0)),
        ] + [piece_spec(start, end) for start, end, _ in others] + [
            whole(high.shape, 1),
            whole(low.shape, 1),
        ],
        out_specs=pl.BlockSpec((blocks, 1, count_y, half, 2 * rows_x), lambda t: (0, t, 0, 0, 0)),
        out_shape=jax.ShapeDtypeStruct((blocks, terms, count_y, half, 2 * rows_x), F32),
        scratch_shapes=[
            pltpu.VMEM((length_y, 2, half, length_x), F32),
            pltpu.VMEM((length_y, 8, length_x), F32),
            pltpu.VMEM((count_y, first.shape[1], 2 * length_x), F32),
            pltpu.VMEM((rows + spare, 2 * length_x), F32),
            pltpu.VMEM((2 * (rows + spare), 2 * length_x), BF16),
        ],
        compiler_params=params(1),
        cost_estimate=cost(terms * 24 * rows * length_x * length_x, terms * 16 * rows * length_x),
        name="spread",
    )(*[array for part in parts for array in part], me, first, own, *[array for _, _, array in others], high, low)


def gather_kernel(*refs):
    *data_refs, factor_ref, high_ref, low_ref, out_ref = refs
    blocks, _, wide, half, lanes = data_refs[0].shape
    rows = lanes // 2
    for y in range(wide):
        parts = []
        for data_ref in data_refs:
            for t in range(data_ref.shape[1]):
                turned = data_ref[:, t, y].reshape(blocks * half, lanes).T
                parts.append(jnp.concatenate([turned[:rows], turned[rows:]], axis=1))
        high, low = split(jnp.concatenate(parts, axis=0))
        fields = dot_stacked(jnp.concatenate([high, low], axis=0), high_ref[...], low_ref[...])
        total = factor_ref[0, y] * fields[:rows]
        for t in range(1, len(parts)):
            total = total + factor_ref[t, y] * fields[t * rows : (t + 1) * rows]
        out_ref[y] = total


def gather(chunks, factor, scale, width, group):
    blocks, _, _, half, lanes = chunks[0].shape
    terms, length_y, rows, length_z = factor.shape
    wide = group[1] - group[0]
    holders = length_y // width
    high, low = halves(inverse_z_table(blocks, length_z, scale))

    def row(n):
        return (n * width + group[0]) // wide

    def chunk_spec(shape):
        full = shape[2] == length_y
        return pl.BlockSpec((blocks, shape[1], wide, half, lanes), lambda n: (0, 0, row(n) if full else n, 0, 0))

    return pl.pallas_call(
        gather_kernel,
        grid=(holders,),
        in_specs=[chunk_spec(chunk.shape) for chunk in chunks] + [
            pl.BlockSpec((terms, wide, rows, length_z), lambda n: (0, row(n), 0, 0)),
            whole(high.shape, 1),
            whole(low.shape, 1),
        ],
        out_specs=pl.BlockSpec((wide, rows, length_z), lambda n: (n, 0, 0)),
        out_shape=jax.ShapeDtypeStruct((holders * wide, rows, length_z), F32),
        compiler_params=params(1),
        cost_estimate=cost(
            6 * terms * holders * wide * rows * length_z * length_z, 8 * terms * holders * wide * rows * length_z
        ),
        name="gather_z",
    )(*chunks, factor, jnp.asarray(high), jnp.asarray(low))


def mirror_kernel(in_ref, table_ref, out_ref, turned_ref):
    _, length_y, half, length_x = in_ref.shape
    high, low = split(in_ref[0].reshape(length_y * half, length_x))
    rest = in_ref[0].reshape(length_y * half, length_x) - high.astype(F32) - low.astype(F32)
    table = table_ref[...]
    turned = (dot(high, table) + dot(low, table)) + dot(rest.astype(BF16), table)
    turned_ref[...] = turned.reshape(length_y, half, length_x)
    for y in range(length_y):
        source = -y % length_y
        for s in range(half):
            row = -s % half
            out_ref[0, y, s : s + 1, :] = turned_ref[source, row : row + 1, :]


def mirror(multiplier, start, end):
    _, length_y, width, length_x = multiplier.shape
    half = width // 2
    terms = end - start
    table = mirror_table(length_x)
    return pl.pallas_call(
        mirror_kernel,
        grid=(terms,),
        in_specs=[
            pl.BlockSpec((1, length_y, half, length_x), lambda t: (t + start, 0, 1, 0)),
            whole(table.shape, 1),
        ],
        out_specs=pl.BlockSpec((1, length_y, half, length_x), lambda t: (t, 0, 0, 0)),
        out_shape=jax.ShapeDtypeStruct((terms, length_y, half, length_x), F32),
        scratch_shapes=[pltpu.VMEM((length_y, half, length_x), F32)],
        compiler_params=params(1),
        cost_estimate=cost(6 * terms * length_y * half * length_x * length_x, 8 * terms * length_y * half * length_x),
        name="mirror",
    )(multiplier, jnp.asarray(table))


def flip(values, axis):
    return jnp.roll(jnp.flip(values, axis), 1, axis)


def padded_by_one(block, sides):
    for axis, dim in sides:
        count = lax.axis_size(axis)
        forward = [(i, i + 1) for i in range(count - 1)]
        backward = [(target, source) for source, target in forward]
        size = block.shape[dim]
        low = lax.ppermute(lax.slice_in_dim(block, size - 1, size, axis=dim), axis, forward)
        high = lax.ppermute(lax.slice_in_dim(block, 0, 1, axis=dim), axis, backward)
        yield dim, low, high


def heat_step(heat, perfuse):
    near = jnp.zeros_like(heat)
    for dim, low, high in padded_by_one(heat, (("term", 0), ("pencil", 1))):
        size = heat.shape[dim]
        near = near + jnp.concatenate([low, lax.slice_in_dim(heat, 0, size - 1, axis=dim)], axis=dim)
        near = near + jnp.concatenate([lax.slice_in_dim(heat, 1, size, axis=dim), high], axis=dim)
    deep = jnp.pad(heat, ((0, 0), (0, 0), (1, 1)))
    near = near + deep[:, :, 2:] + deep[:, :, :-2]
    return heat + DIFFUSION * (near - 6.0 * heat) - perfuse * heat


def update_kernel(
    fresh_ref, old_ref, dose_ref, heat_ref, absorb_ref,
    pressure_ref, source_ref, out_ref, low_ref, high_ref, below_ref, above_ref,
):
    width, rows, _ = fresh_ref.shape
    field = fresh_ref[...] - old_ref[...]
    source = absorb_ref[...] * (dose_ref[...] + field * field)
    heat = heat_ref[...] + source
    pressure_ref[...] = field
    source_ref[...] = source
    out_ref[...] = heat
    low_ref[...] = heat[:, :1]
    high_ref[...] = heat[:, rows - 1 :]
    below_ref[...] = heat[:1]
    above_ref[...] = heat[width - 1 :]


def update(fresh, old, dose, heat, absorb):
    width, rows, length_z = fresh.shape
    shapes = [fresh.shape] * 3 + [(width, 1, length_z)] * 2 + [(1, rows, length_z)] * 2
    return pl.pallas_call(
        update_kernel,
        out_shape=[jax.ShapeDtypeStruct(shape, F32) for shape in shapes],
        compiler_params=params(),
        cost_estimate=cost(5 * fresh.size, 32 * fresh.size),
        name="update",
    )(fresh, old, dose, heat, absorb)


def warm_kernel(*refs, groups, turned):
    heat_refs, source_refs, low_refs, high_refs = [refs[k * groups : (k + 1) * groups] for k in range(4)]
    below_ref, above_ref, perfuse_ref, out_ref = refs[4 * groups :]
    rows, length_z = below_ref.shape[1:]
    planes, sources, lows, highs = [], [], [], []
    for heat_ref, source_ref, low_ref, high_ref in zip(heat_refs, source_refs, low_refs, high_refs):
        for w in range(heat_ref.shape[0]):
            planes.append(heat_ref[w])
            sources.append(source_ref[w])
            lows.append(low_ref[w])
            highs.append(high_ref[w])
    row = lax.broadcasted_iota(jnp.int32, (rows, length_z), 0)
    lane = lax.broadcasted_iota(jnp.int32, (rows, length_z), 1)
    for w, heat in enumerate(planes):
        near = jnp.where(row == 0, lows[w], pltpu.roll(heat, 1, 0))
        near = near + jnp.where(row == rows - 1, highs[w], pltpu.roll(heat, rows - 1, 0))
        near = near + (planes[w - 1] if w else below_ref[0])
        near = near + (planes[w + 1] if w + 1 < len(planes) else above_ref[0])
        near = near + jnp.where(lane == 0, 0.0, pltpu.roll(heat, 1, 1))
        near = near + jnp.where(lane == length_z - 1, 0.0, pltpu.roll(heat, length_z - 1, 1))
        fresh = heat + DIFFUSION * (near - 6.0 * heat) - perfuse_ref[w] * heat + sources[w]
        if turned:
            out_ref[:, w, :] = fresh
        else:
            out_ref[w] = fresh


def edges_of(heat):
    return heat[:, :1], heat[:, -1:], heat[:1], heat[-1:]


def halo(edges, lowest):
    count = lax.axis_size("pencil")
    low = lax.ppermute(edges[1], "pencil", [(i, i + 1) for i in range(count - 1)])
    high = lax.ppermute(edges[0], "pencil", [(i + 1, i) for i in range(count - 1)])
    if not lowest:
        return [low, high]
    backward = [(i + 1, i) for i in range(lax.axis_size("term") - 1)]
    return [low, high, lax.ppermute(edges[2], "term", backward)]


def warm(heats, sources, sides, top, perfuse, turned):
    width, rows, length_z = perfuse.shape
    above = sides[0][2]
    below = lax.ppermute(top, "term", [(i, i + 1) for i in range(lax.axis_size("term") - 1)])
    return pl.pallas_call(
        functools.partial(warm_kernel, groups=len(heats), turned=turned),
        out_shape=jax.ShapeDtypeStruct((rows, width, length_z) if turned else perfuse.shape, F32),
        compiler_params=params(),
        cost_estimate=cost(16 * perfuse.size, 16 * perfuse.size),
        name="warm",
    )(*heats, *sources, *[side[0] for side in sides], *[side[1] for side in sides], below, above, perfuse)


def on_device(
    present_acoustic,
    prior_acoustic,
    location_factor,
    spectral_multiplier,
    medium_kinds,
    organ_properties,
    thermal_increase,
):
    term_count = lax.axis_size("term")
    blocks = lax.axis_size("pencil")
    rows, length_y, length_z = present_acoustic.shape
    length_x = rows * blocks
    width = length_y // term_count
    half = length_z // blocks // 2
    terms = location_factor.shape[0]
    brick_start = lax.axis_index("term") * width
    scale = 2.0 / (length_x * length_y * length_z)

    cut = width // 2 if width >= 4 else width
    spans = [(0, cut), (cut, width)] if cut < width else [(0, width)]

    def to_brick(values):
        return jnp.transpose(lax.dynamic_slice_in_dim(values, brick_start, width, 1), (1, 0, 2))

    def cut_up(brick):
        return [brick[start:end] for start, end in spans]

    def exchange(values):
        return lax.all_to_all(values, "pencil", 0, 0, tiled=True)

    opposite = [(p, blocks - 1 - p) for p in range(blocks)]
    middle = terms // 2
    sent = forward_z([to_brick(present_acoustic)], blocks)[0]
    sent, multiplier = lax.optimization_barrier((sent, spectral_multiplier))
    sent = exchange(sent)
    lowest = spectral_multiplier[:, :, 0, :]
    others, before = [], None
    for start, end in ((0, middle), (middle, terms)):
        if end > start:
            mirrored = mirror(multiplier, start, end)
            if others:
                mirrored, before, lowest = lax.optimization_barrier((mirrored, before, lowest))
                others = [(*others[0][:2], before)]
            else:
                mirrored, lowest = lax.optimization_barrier((mirrored, lowest))
            before = lax.ppermute(mirrored, "pencil", opposite)
            if not others:
                lowest = lowest + lax.ppermute(
                    flip(flip(lowest, 1), 2),
                    "pencil",
                    [(p, blocks - p) for p in range(1, blocks) if 2 * p != blocks],
                )
            others.append((start, end, before))
    lowest = jnp.transpose(lowest, (1, 0, 2))
    lowest = jnp.pad(lowest, ((0, 0), (0, -terms % 8), (0, 0)))
    me = lax.axis_index("term").reshape(1).astype(jnp.int32)
    factor = jnp.transpose(location_factor, (0, 2, 1, 3))
    last, factor = lax.optimization_barrier((others[0][2], factor))
    others[0] = (*others[0][:2], last)

    def gathered(part, offload):
        if offload or term_count == 1:
            return [lax.all_gather(part, "term", axis=0, tiled=False)]
        return [part] + [
            lax.ppermute(part, "term", [(i, (i - d) % term_count) for i in range(term_count)])
            for d in range(1, term_count)
        ]

    def spread_from(parts, sent_spans, group, chosen):
        out = spread(parts, sent_spans, me, lowest, spectral_multiplier, others, blocks, group, chosen)
        flat, tree = jax.tree.flatten(parts)
        out, *flat = lax.optimization_barrier((out, *flat))
        return out, jax.tree.unflatten(tree, flat)

    def summed(chunks, group):
        partial = gather(chunks, factor, scale, width, group)
        return lax.psum_scatter(partial, "term", scatter_dimension=0, tiled=True)

    def doubled_first(part, tied):
        parts = [[lax.all_gather(part, "term", axis=0, tiled=False)]]
        shared, chunks, bricks = [], {}, []
        if middle:
            out, parts = spread_from(parts, [(0, width)], (0, width), (0, middle))
            out, last = lax.optimization_barrier((out, others[-1][2]))
            others[-1] = (*others[-1][:2], last)
            shared = [exchange(out)]
        before = shared
        for index, group in enumerate(spans):
            out, parts = spread_from(parts, [(0, width)], group, (middle, terms))
            out, *before = lax.optimization_barrier((out, *before))
            if index == 0:
                shared = before
            out = exchange(out)
            before = [out]
            if index == 0:
                out, *tied = lax.optimization_barrier((out, *tied))
            bricks.append(summed(shared + [out], group))
        return bricks, tied

    def doubled(parts):
        bricks, before = [], []
        for group in spans:
            out, parts = spread_from(parts, spans, group, (0, terms))
            out, *before = lax.optimization_barrier((out, *before))
            if before:
                chunks[0] = before[0]
                bricks.append(summed(chunks, spans[0]))
            chunks = [exchange(out)]
            before = list(chunks)
        bricks.append(summed(chunks, spans[-1]))
        return bricks

    def forward(bricks):
        parts, states, before = [], [], []
        for (start, end), (fresh, *older) in zip(spans, bricks):
            fresh, *before = lax.optimization_barrier((fresh, *before))
            if before:
                parts.append(gathered(before[0], True))
            sent, *state = forward_z([fresh, *older], blocks)
            sent = exchange(sent)
            before = [forward_x(sent, end - start, half, rows)]
            states.append(state)
        parts.append(gathered(before[0], False))
        return parts, states

    kinds = jnp.transpose(medium_kinds, (1, 0, 2))
    absorb, perfuse = [
        jnp.where(
            kinds == 0,
            organ_properties[0, at],
            jnp.where(kinds == 1, organ_properties[1, at], organ_properties[2, at]),
        )
        for at in range(2)
    ]
    heat = heat_step(jnp.transpose(thermal_increase, (1, 0, 2)), perfuse)

    previous = cut_up(to_brick(prior_acoustic))
    current = cut_up(to_brick(present_acoustic))
    dose = []
    doubles, (heat, absorb, perfuse) = doubled_first(forward_x(sent, width, half, rows), (heat, absorb, perfuse))
    for _ in range(WAVE_STEPS - 1):
        parts, states = forward(list(zip(doubles, previous, *dose)))
        previous, current = current, [field for field, _ in states]
        dose = [[total for _, total in states]]
        doubles = doubled(parts)
    dose = dose[0] if dose else [jnp.zeros(each.shape, F32) for each in current]
    updated, sides, ahead = [], [], []
    for fresh, *rest in zip(doubles, previous, dose, cut_up(heat), cut_up(absorb)):
        fresh, *ahead = lax.optimization_barrier((fresh, *ahead))
        if ahead:
            sides.append(ahead)
        updated.append(update(fresh, *rest))
        ahead = halo(updated[-1][3:], not sides)
    sides.append(ahead)
    pressure = jnp.concatenate([each[0] for each in updated], axis=0)
    sources = [each[1] for each in updated]
    heats = [each[2] for each in updated]
    top = updated[-1][6]
    for _ in range(HEAT_STEPS - 2):
        heats = cut_up(warm(heats, sources, sides, top, perfuse, False))
        edges = [edges_of(each) for each in heats]
        sides = [halo(each, index == 0) for index, each in enumerate(edges)]
        top = edges[-1][3]
    return jnp.transpose(pressure, (1, 0, 2)), warm(heats, sources, sides, top, perfuse, True)


def solution(mesh):
    return jax.shard_map(
        on_device,
        mesh=mesh,
        in_specs=(
            P("pencil", None, None),
            P("pencil", None, None),
            P("term", "pencil", None, None),
            P("term", None, "pencil", None),
            P("pencil", "term", None),
            P(),
            P("pencil", "term", None),
        ),
        out_specs=(P("pencil", "term", None), P("pencil", "term", None)),
        check_vma=False,
    )
```

```python
import functools
import math

import jax
import jax.numpy as jnp
import ml_dtypes
import numpy as np
from jax import lax
from jax.experimental import pallas as pl
from jax.experimental.pallas import tpu as pltpu
from jax.sharding import PartitionSpec as P

WAVE_STEPS = 2
HEAT_STEPS = 2
DIFFUSION = 0.125
VMEM_BYTES = 56 * 1024 * 1024
F32 = jnp.float32
BF16 = jnp.bfloat16


def halves(table):
    high = table.astype(ml_dtypes.bfloat16)
    low = (table - high.astype(np.float64)).astype(ml_dtypes.bfloat16)
    return high, low


def angles(left, right, length):
    return (np.outer(left, right) % length) * (2.0 * math.pi / length)


def slot_wavenumbers(blocks, length_z):
    width = length_z // blocks
    half = width // 2
    slots = np.concatenate([[half], np.arange(1, half)])
    starts = np.arange(blocks) * width
    return starts[:, None] + slots[None, :], starts


def forward_z_table(blocks, length_z):
    main, first = slot_wavenumbers(blocks, length_z)
    z = np.arange(length_z)
    theta = angles(z, main.reshape(-1), length_z).reshape(length_z, blocks, -1)
    real, imag = np.cos(theta), -np.sin(theta)
    for q in range(blocks // 2):
        real[:, q, 0], imag[:, q, 0] = -imag[:, q, 0].copy(), real[:, q, 0].copy()
    theta = angles(z, first, length_z)
    real0, imag0 = np.cos(theta), -np.sin(theta)
    for q in range(blocks // 2 + 1, blocks):
        real0[:, q], imag0[:, q] = imag0[:, q].copy(), -real0[:, q].copy()
    table = np.concatenate(
        [np.stack([real, imag], 2).reshape(length_z, -1), np.stack([real0, imag0], 2).reshape(length_z, -1)], axis=1
    )
    spare = -table.shape[1] % 128
    return np.pad(table, ((0, 0), (0, spare)))


def inverse_z_table(blocks, length_z, scale):
    main, first = slot_wavenumbers(blocks, length_z)
    z = np.arange(length_z)
    theta = angles(main.reshape(-1), z, length_z).reshape(blocks, -1, length_z)
    real, imag = np.cos(theta), -np.sin(theta)
    for p in range(blocks):
        middle = theta[p, 0]
        imag[p, 0] = np.cos(middle) if p < blocks // 2 else -np.sin(middle)
        lowest = angles(first[p : p + 1], z, length_z)[0]
        real[p, 0] = np.cos(lowest) if p <= blocks // 2 else -np.sin(lowest)
    return scale * np.concatenate([real.reshape(-1, length_z), imag.reshape(-1, length_z)], axis=0)


def forward_x_table(length_x):
    x = np.arange(length_x)
    theta = angles(x, x, length_x)
    return np.concatenate([np.cos(theta), np.sin(theta)], axis=1)


def inverse_x_table(blocks, length_x):
    x = np.arange(length_x)
    theta = angles(x, x, length_x).reshape(length_x, blocks, -1)
    cosine, sine = np.cos(theta), np.sin(theta)
    real_rows = np.stack([cosine, sine], axis=2).reshape(length_x, -1)
    imag_rows = np.stack([-sine, cosine], axis=2).reshape(length_x, -1)
    return np.concatenate([real_rows, imag_rows], axis=0)


def mirror_table(length):
    x = np.arange(length)
    table = np.zeros((length, length), ml_dtypes.bfloat16)
    table[x, (-x) % length] = 1
    return table


def turned_by(a, b, k, count, sign):
    if k == 0:
        return a, b
    if 4 * k == count:
        return (-b, a) if sign > 0 else (b, -a)
    angle = 2.0 * math.pi * k / count
    c, s = math.cos(angle), sign * math.sin(angle)
    if 8 * k == count or 8 * k == 3 * count:
        root = math.sqrt(0.5)
        sum_ab, less_ab = root * (a + b), root * (a - b)
        if c > 0:
            return (less_ab, sum_ab) if s > 0 else (sum_ab, -less_ab)
        return (-sum_ab, less_ab) if s > 0 else (-less_ab, -sum_ab)
    return c * a - s * b, c * b + s * a


def fourier(values, sign, wanted=None):
    count = len(values)
    wanted = range(count) if wanted is None else wanted
    if not wanted:
        return {}
    if count == 1:
        return {0: values[0]}
    if count % 2:
        out = {}
        for k in wanted:
            real, imag = values[0]
            for n in range(1, count):
                angle = 2.0 * math.pi * (k * n % count) / count
                c, s = math.cos(angle), sign * math.sin(angle)
                a, b = values[n]
                real, imag = real + (c * a - s * b), imag + (c * b + s * a)
            out[k] = (real, imag)
        return out
    half = count // 2
    out = {}
    even = [k // 2 for k in wanted if k % 2 == 0]
    odd = [k // 2 for k in wanted if k % 2]
    if even:
        added = [(values[n][0] + values[n + half][0], values[n][1] + values[n + half][1]) for n in range(half)]
        for k, value in fourier(added, sign, even).items():
            out[2 * k] = value
    if odd:
        less = [
            turned_by(values[n][0] - values[n + half][0], values[n][1] - values[n + half][1], n, count, sign)
            for n in range(half)
        ]
        for k, value in fourier(less, sign, odd).items():
            out[2 * k + 1] = value
    return out


def split(values):
    high = values.astype(BF16)
    return high, (values - high.astype(F32)).astype(BF16)


def dot(left, right):
    return jnp.dot(left, right, preferred_element_type=F32)


def dot_across(left, right):
    return lax.dot_general(left, right, (((1,), (1,)), ((), ())), preferred_element_type=F32)


def dot_three(high, low, table_high, table_low):
    return dot(high, table_high) + (dot(low, table_high) + dot(high, table_low))


def dot_stacked(both, table_high, table_low):
    count = both.shape[0] // 2
    by_high = dot(both, table_high)
    return by_high[:count] + (by_high[count:] + dot(both[:count], table_low))


def params(count=0):
    return pltpu.CompilerParams(vmem_limit_bytes=VMEM_BYTES, dimension_semantics=("arbitrary",) * count)


def cost(flops, moved):
    return pl.CostEstimate(flops=int(flops), bytes_accessed=int(moved), transcendentals=0)


def whole(shape, grid_rank):
    return pl.BlockSpec(shape, lambda *_: (0,) * len(shape), pipeline_mode=pl.Buffered(1)) if grid_rank else pl.BlockSpec(
        memory_space=pltpu.VMEM
    )


def forward_z_kernel(*refs, inputs):
    fresh_ref, *older = refs[:inputs]
    high_ref, low_ref, first_high_ref, first_low_ref, out_ref, *state = refs[inputs:]
    width, rows, length_z = fresh_ref.shape
    blocks = out_ref.shape[0]
    main = length_z // blocks
    brick = fresh_ref[...]
    if older:
        brick = brick - older[0][...]
        state[0][...] = brick
        dose = brick * brick
        state[1][...] = dose + older[1][...] if len(older) > 1 else dose
    high, low = split(brick.reshape(width * rows, length_z))
    result = dot_three(high, low, high_ref[...], low_ref[...])
    first = (
        dot_across(first_high_ref[...], high)
        + (dot_across(first_low_ref[...], high) + dot_across(first_high_ref[...], low))
    )
    out_ref[:, rows:, :] = jnp.zeros_like(out_ref[:, rows:, :])
    for q in range(blocks):
        for w in range(width):
            out_ref[q, :rows, w * main : (w + 1) * main] = result[w * rows : (w + 1) * rows, q * main : (q + 1) * main]
            for c in range(2):
                row = rows + c * width + w
                out_ref[q, row : row + 1, :rows] = first[2 * q + c : 2 * q + c + 1, w * rows : (w + 1) * rows]


def forward_z(bricks, blocks):
    width, rows, length_z = bricks[0].shape
    lanes = max(width * length_z // blocks, rows)
    table = forward_z_table(blocks, length_z)
    high, low = halves(table[:, :length_z])
    first_high, first_low = halves(table[:, length_z : length_z + 2 * blocks].T)
    tables = [jnp.asarray(each) for each in (high, low, first_high, first_low)]
    out = [jax.ShapeDtypeStruct((blocks, rows + 2 * width + (-2 * width) % 8, lanes), F32)]
    if len(bricks) > 1:
        out += [jax.ShapeDtypeStruct(bricks[0].shape, F32)] * 2
    return pl.pallas_call(
        functools.partial(forward_z_kernel, inputs=len(bricks)),
        out_shape=out,
        compiler_params=params(),
        cost_estimate=cost(6 * width * rows * length_z * length_z, 16 * width * rows * length_z),
        name="forward_z",
    )(*bricks, *tables)


def forward_x_kernel(data_ref, high_ref, low_ref, out_ref, *, width, half, rows):
    blocks = data_ref.shape[0]
    length_x = blocks * rows
    main = width * 2 * half
    turned = data_ref[:, :rows, :main].reshape(length_x, main).T
    first = jnp.concatenate([data_ref[q, rows:, :rows] for q in range(blocks)], axis=1)
    high, low = split(jnp.concatenate([turned, first], axis=0))
    both = dot_three(high, low, high_ref[...], low_ref[...])
    by_cos, by_sin = both[:, :length_x], both[:, length_x:]
    for w in range(width):
        re, im = w * 2 * half, w * 2 * half + half
        out_ref[re : re + half] = by_cos[re : re + half] + by_sin[im : im + half]
        out_ref[im : im + half] = by_cos[im : im + half] - by_sin[re : re + half]
    re, im, end = main, main + width, main + 2 * width
    out_ref[re:im] = by_cos[re:im] + by_sin[im:end]
    out_ref[im:end] = by_cos[im:end] - by_sin[re:im]
    if end < out_ref.shape[0]:
        out_ref[end:] = jnp.zeros_like(out_ref[end:])


def forward_x(data, width, half, rows):
    blocks = data.shape[0]
    length_x = blocks * rows
    out_rows = width * 2 * half + data.shape[1] - rows
    high, low = halves(forward_x_table(length_x))
    return pl.pallas_call(
        functools.partial(forward_x_kernel, width=width, half=half, rows=rows),
        out_shape=jax.ShapeDtypeStruct((out_rows, length_x), F32),
        compiler_params=params(),
        cost_estimate=cost(12 * out_rows * length_x * length_x, 8 * out_rows * length_x),
        name="forward_x",
    )(data, jnp.asarray(high), jnp.asarray(low))


def spread_kernel(*refs, spans, counts, group, pieces, first_term):
    parts, at = [], 0
    for count in counts:
        parts.append(refs[at : at + count])
        at += count
    me_ref, first_ref, own_ref = refs[at : at + 3]
    others = refs[at + 3 : at + 3 + len(pieces)]
    (
        high_ref, low_ref, out_ref,
        fk_ref, edge_in_ref, edge_ref, u_ref, u_both_ref,
    ) = refs[at + 3 + len(pieces) :]
    length_y, _, half, length_x = fk_ref.shape
    lanes_out = out_ref.shape[-1]
    rows_x = lanes_out // 2
    count_y = out_ref.shape[2]
    width = spans[-1][1]
    holders = length_y // width
    step = pl.program_id(0)
    tiles = [slice(at, at + 128) for at in range(0, length_x, 128)]
    wanted = [y for y in range(length_y) if group[0] <= y % width < group[1]]

    @pl.when(step == 0)
    def _():
        for part, (start, end) in zip(parts, spans):
            wide = end - start
            for d in range(holders):
                if len(part) == 1:
                    source, holder = part[0].at[d], d
                else:
                    source, holder = part[d], lax.rem(me_ref[0] + d, holders)
                for w in range(wide):
                    y = holder * width + start + w
                    fk_ref[y, 0] = source[w * 2 * half : w * 2 * half + half]
                    fk_ref[y, 1] = source[w * 2 * half + half : (w + 1) * 2 * half]
                    row = wide * 2 * half + w
                    edge_in_ref[y, :1] = source[row : row + 1]
                    edge_in_ref[y, 1:2] = source[row + wide : row + wide + 1]

        @pl.loop(0, half // 8)
        def _(tile):
            at = pl.ds(pl.multiple_of(tile * 8, 8), 8)
            for lanes in tiles:
                values = [(fk_ref[y, 0, at, lanes], fk_ref[y, 1, at, lanes]) for y in range(length_y)]
                values = fourier(values, -1)
                for y in range(length_y):
                    fk_ref[y, 0, at, lanes] = values[y][0]
                    fk_ref[y, 1, at, lanes] = values[y][1]

        for index, lanes in enumerate(tiles):
            values = [(edge_in_ref[y, :1, lanes], edge_in_ref[y, 1:2, lanes]) for y in range(length_y)]
            values = fourier(values, -1)
            factors = [first_ref[y, :, lanes] for y in range(length_y)]
            values = [(factors[y] * values[y][0], factors[y] * values[y][1]) for y in range(length_y)]
            values = fourier(values, 1, wanted)
            for n, y in enumerate(wanted):
                edge_ref[n, :, index * 128 : index * 128 + 128] = values[y][0]
                edge_ref[n, :, length_x + index * 128 : length_x + index * 128 + 128] = values[y][1]
    row_index = lax.broadcasted_iota(jnp.int32, (8, 128), 0)

    def weigh(other_ref):
        @pl.loop(0, half // 8)
        def _(tile):
            at = pl.ds(pl.multiple_of(tile * 8, 8), 8)
            swapped = jnp.logical_and(row_index == 0, tile == 0)
            for index, lanes in enumerate(tiles):
                values = []
                for y in range(length_y):
                    own = jnp.where(swapped, own_ref[0, y, half : half + 1, lanes], own_ref[0, y, at, lanes])
                    factor = own + other_ref[0, y, at, lanes]
                    values.append((factor * fk_ref[y, 0, at, lanes], factor * fk_ref[y, 1, at, lanes]))
                values = fourier(values, 1, wanted)
                for n, y in enumerate(wanted):
                    rows = pl.ds(pl.multiple_of(n * half + tile * 8, 8), 8)
                    u_ref[rows, index * 128 : index * 128 + 128] = values[y][0]
                    u_ref[rows, length_x + index * 128 : length_x + index * 128 + 128] = values[y][1]

    if len(others) == 1:
        weigh(others[0])
    else:
        for other_ref, (start, end) in zip(others, pieces):
            pl.when(jnp.logical_and(step >= start, step < end))(functools.partial(weigh, other_ref))

    main_rows = count_y * half
    all_rows = u_ref.shape[0]
    for n in range(count_y):
        u_ref[main_rows + n : main_rows + n + 1, :] = edge_ref[n, pl.ds(first_term + step, 1), :]
    if main_rows + count_y < all_rows:
        u_ref[main_rows + count_y :, :] = jnp.zeros_like(u_ref[main_rows + count_y :, :])

    @pl.loop(0, all_rows // 16)
    def _(part):
        high, low = split(u_ref[pl.ds(pl.multiple_of(part * 16, 16), 16), :])
        u_both_ref[pl.ds(pl.multiple_of(part * 16, 16), 16), :] = high
        u_both_ref[pl.ds(pl.multiple_of(all_rows + part * 16, 16), 16), :] = low

    lane_index = lax.broadcasted_iota(jnp.int32, (8, lanes_out), 1)
    row_index = lax.broadcasted_iota(jnp.int32, (8, lanes_out), 0)
    swapped = jnp.logical_and(row_index == 0, lane_index < rows_x)
    count = 256 // lanes_out
    for part in range(2 * length_x // 256):
        cols = slice(part * 256, part * 256 + 256)
        result = dot_stacked(u_both_ref[...], high_ref[:, cols], low_ref[:, cols])
        edges = [result[main_rows + n : main_rows + n + 1] for n in range(count_y)]
        for k in range(count):
            q = part * count + k
            inside = slice(k * lanes_out, (k + 1) * lanes_out)
            piece = result[:, inside]
            for n in range(count_y):
                top = piece[n * half : n * half + 8]
                out_ref[q, 0, n, :8, :] = jnp.where(swapped, edges[n][:, inside], top)
                out_ref[q, 0, n, 8:, :] = piece[n * half + 8 : (n + 1) * half]


def spread(parts, spans, me, first, own, others, blocks, group, chosen):
    _, length_y, _, length_x = own.shape
    half = own.shape[2] // 2
    first_term, end_term = chosen
    terms = end_term - first_term
    count_y = length_y // spans[-1][1] * (group[1] - group[0])
    rows_x = length_x // blocks
    high, low = halves(inverse_x_table(blocks, length_x))
    high, low = jnp.asarray(high), jnp.asarray(low)
    rows = count_y * half
    spare = count_y + -count_y % 16
    others = [each for each in others if each[0] < end_term and each[1] > first_term]

    def piece_spec(start, end):
        return pl.BlockSpec(
            (1, length_y, half, length_x), lambda t: (jnp.clip(t + first_term - start, 0, end - start - 1), 0, 0, 0)
        )

    return pl.pallas_call(
        functools.partial(
            spread_kernel, spans=spans, counts=[len(part) for part in parts], group=group, first_term=first_term,
            pieces=[(start - first_term, end - first_term) for start, end, _ in others],
        ),
        grid=(terms,),
        in_specs=[whole(array.shape, 1) for part in parts for array in part] + [
            pl.BlockSpec(memory_space=pltpu.SMEM),
            whole(first.shape, 1),
            pl.BlockSpec((1, length_y, half + 8, length_x), lambda t: (t + first_term, 0, 0, 0)),
        ] + [piece_spec(start, end) for start, end, _ in others] + [
            whole(high.shape, 1),
            whole(low.shape, 1),
        ],
        out_specs=pl.BlockSpec((blocks, 1, count_y, half, 2 * rows_x), lambda t: (0, t, 0, 0, 0)),
        out_shape=jax.ShapeDtypeStruct((blocks, terms, count_y, half, 2 * rows_x), F32),
        scratch_shapes=[
            pltpu.VMEM((length_y, 2, half, length_x), F32),
            pltpu.VMEM((length_y, 8, length_x), F32),
            pltpu.VMEM((count_y, first.shape[1], 2 * length_x), F32),
            pltpu.VMEM((rows + spare, 2 * length_x), F32),
            pltpu.VMEM((2 * (rows + spare), 2 * length_x), BF16),
        ],
        compiler_params=params(1),
        cost_estimate=cost(terms * 24 * rows * length_x * length_x, terms * 16 * rows * length_x),
        name="spread",
    )(*[array for part in parts for array in part], me, first, own, *[array for _, _, array in others], high, low)


def gather_kernel(*refs):
    *data_refs, factor_ref, high_ref, low_ref, out_ref = refs
    blocks, _, wide, half, lanes = data_refs[0].shape
    rows = lanes // 2
    for y in range(wide):
        parts = []
        for data_ref in data_refs:
            for t in range(data_ref.shape[1]):
                turned = data_ref[:, t, y].reshape(blocks * half, lanes).T
                parts.append(jnp.concatenate([turned[:rows], turned[rows:]], axis=1))
        high, low = split(jnp.concatenate(parts, axis=0))
        fields = dot_stacked(jnp.concatenate([high, low], axis=0), high_ref[...], low_ref[...])
        total = factor_ref[0, y] * fields[:rows]
        for t in range(1, len(parts)):
            total = total + factor_ref[t, y] * fields[t * rows : (t + 1) * rows]
        out_ref[y] = total


def gather(chunks, factor, scale, width, group):
    blocks, _, _, half, lanes = chunks[0].shape
    terms, length_y, rows, length_z = factor.shape
    wide = group[1] - group[0]
    holders = length_y // width
    high, low = halves(inverse_z_table(blocks, length_z, scale))

    def row(n):
        return (n * width + group[0]) // wide

    def chunk_spec(shape):
        full = shape[2] == length_y
        return pl.BlockSpec((blocks, shape[1], wide, half, lanes), lambda n: (0, 0, row(n) if full else n, 0, 0))

    return pl.pallas_call(
        gather_kernel,
        grid=(holders,),
        in_specs=[chunk_spec(chunk.shape) for chunk in chunks] + [
            pl.BlockSpec((terms, wide, rows, length_z), lambda n: (0, row(n), 0, 0)),
            whole(high.shape, 1),
            whole(low.shape, 1),
        ],
        out_specs=pl.BlockSpec((wide, rows, length_z), lambda n: (n, 0, 0)),
        out_shape=jax.ShapeDtypeStruct((holders * wide, rows, length_z), F32),
        compiler_params=params(1),
        cost_estimate=cost(
            6 * terms * holders * wide * rows * length_z * length_z, 8 * terms * holders * wide * rows * length_z
        ),
        name="gather_z",
    )(*chunks, factor, jnp.asarray(high), jnp.asarray(low))


def mirror_kernel(in_ref, table_ref, out_ref, turned_ref):
    _, length_y, half, length_x = in_ref.shape
    high, low = split(in_ref[0].reshape(length_y * half, length_x))
    rest = in_ref[0].reshape(length_y * half, length_x) - high.astype(F32) - low.astype(F32)
    table = table_ref[...]
    turned = (dot(high, table) + dot(low, table)) + dot(rest.astype(BF16), table)
    turned_ref[...] = turned.reshape(length_y, half, length_x)
    for y in range(length_y):
        source = -y % length_y
        for s in range(half):
            row = -s % half
            out_ref[0, y, s : s + 1, :] = turned_ref[source, row : row + 1, :]


def mirror(multiplier, start, end):
    _, length_y, width, length_x = multiplier.shape
    half = width // 2
    terms = end - start
    table = mirror_table(length_x)
    return pl.pallas_call(
        mirror_kernel,
        grid=(terms,),
        in_specs=[
            pl.BlockSpec((1, length_y, half, length_x), lambda t: (t + start, 0, 1, 0)),
            whole(table.shape, 1),
        ],
        out_specs=pl.BlockSpec((1, length_y, half, length_x), lambda t: (t, 0, 0, 0)),
        out_shape=jax.ShapeDtypeStruct((terms, length_y, half, length_x), F32),
        scratch_shapes=[pltpu.VMEM((length_y, half, length_x), F32)],
        compiler_params=params(1),
        cost_estimate=cost(6 * terms * length_y * half * length_x * length_x, 8 * terms * length_y * half * length_x),
        name="mirror",
    )(multiplier, jnp.asarray(table))


def flip(values, axis):
    return jnp.roll(jnp.flip(values, axis), 1, axis)


def padded_by_one(block, sides):
    for axis, dim in sides:
        count = lax.axis_size(axis)
        forward = [(i, i + 1) for i in range(count - 1)]
        backward = [(target, source) for source, target in forward]
        size = block.shape[dim]
        low = lax.ppermute(lax.slice_in_dim(block, size - 1, size, axis=dim), axis, forward)
        high = lax.ppermute(lax.slice_in_dim(block, 0, 1, axis=dim), axis, backward)
        yield dim, low, high


def halos_of(heat):
    return [side for _, low, high in padded_by_one(heat, (("term", 0), ("pencil", 1))) for side in (low, high)]


def heat_step(heat, halos, perfuse):
    near = jnp.zeros_like(heat)
    for dim, (low, high) in enumerate(zip(halos[::2], halos[1::2])):
        size = heat.shape[dim]
        near = near + jnp.concatenate([low, lax.slice_in_dim(heat, 0, size - 1, axis=dim)], axis=dim)
        near = near + jnp.concatenate([lax.slice_in_dim(heat, 1, size, axis=dim), high], axis=dim)
    deep = jnp.pad(heat, ((0, 0), (0, 0), (1, 1)))
    near = near + deep[:, :, 2:] + deep[:, :, :-2]
    return heat + DIFFUSION * (near - 6.0 * heat) - perfuse * heat


def update_kernel(
    fresh_ref, old_ref, dose_ref, heat_ref, absorb_ref,
    pressure_ref, source_ref, out_ref, low_ref, high_ref, below_ref, above_ref,
):
    width, rows, _ = fresh_ref.shape
    field = fresh_ref[...] - old_ref[...]
    source = absorb_ref[...] * (dose_ref[...] + field * field)
    heat = heat_ref[...] + source
    pressure_ref[...] = field
    source_ref[...] = source
    out_ref[...] = heat
    low_ref[...] = heat[:, :1]
    high_ref[...] = heat[:, rows - 1 :]
    below_ref[...] = heat[:1]
    above_ref[...] = heat[width - 1 :]


def update(fresh, old, dose, heat, absorb):
    width, rows, length_z = fresh.shape
    shapes = [fresh.shape] * 3 + [(width, 1, length_z)] * 2 + [(1, rows, length_z)] * 2
    return pl.pallas_call(
        update_kernel,
        out_shape=[jax.ShapeDtypeStruct(shape, F32) for shape in shapes],
        compiler_params=params(),
        cost_estimate=cost(5 * fresh.size, 32 * fresh.size),
        name="update",
    )(fresh, old, dose, heat, absorb)


def warm_kernel(*refs, groups, turned):
    heat_refs, source_refs, low_refs, high_refs = [refs[k * groups : (k + 1) * groups] for k in range(4)]
    below_ref, above_ref, perfuse_ref, out_ref = refs[4 * groups :]
    rows, length_z = below_ref.shape[1:]
    planes, sources, lows, highs = [], [], [], []
    for heat_ref, source_ref, low_ref, high_ref in zip(heat_refs, source_refs, low_refs, high_refs):
        for w in range(heat_ref.shape[0]):
            planes.append(heat_ref[w])
            sources.append(source_ref[w])
            lows.append(low_ref[w])
            highs.append(high_ref[w])
    row = lax.broadcasted_iota(jnp.int32, (rows, length_z), 0)
    lane = lax.broadcasted_iota(jnp.int32, (rows, length_z), 1)
    for w, heat in enumerate(planes):
        near = jnp.where(row == 0, lows[w], pltpu.roll(heat, 1, 0))
        near = near + jnp.where(row == rows - 1, highs[w], pltpu.roll(heat, rows - 1, 0))
        near = near + (planes[w - 1] if w else below_ref[0])
        near = near + (planes[w + 1] if w + 1 < len(planes) else above_ref[0])
        near = near + jnp.where(lane == 0, 0.0, pltpu.roll(heat, 1, 1))
        near = near + jnp.where(lane == length_z - 1, 0.0, pltpu.roll(heat, length_z - 1, 1))
        fresh = heat + DIFFUSION * (near - 6.0 * heat) - perfuse_ref[w] * heat + sources[w]
        if turned:
            out_ref[:, w, :] = fresh
        else:
            out_ref[w] = fresh


def edges_of(heat):
    return heat[:, :1], heat[:, -1:], heat[:1], heat[-1:]


def halo(edges, lowest):
    count = lax.axis_size("pencil")
    low = lax.ppermute(edges[1], "pencil", [(i, i + 1) for i in range(count - 1)])
    high = lax.ppermute(edges[0], "pencil", [(i + 1, i) for i in range(count - 1)])
    if not lowest:
        return [low, high]
    backward = [(i + 1, i) for i in range(lax.axis_size("term") - 1)]
    return [low, high, lax.ppermute(edges[2], "term", backward)]


def warm(heats, sources, sides, top, perfuse, turned):
    width, rows, length_z = perfuse.shape
    above = sides[0][2]
    below = lax.ppermute(top, "term", [(i, i + 1) for i in range(lax.axis_size("term") - 1)])
    return pl.pallas_call(
        functools.partial(warm_kernel, groups=len(heats), turned=turned),
        out_shape=jax.ShapeDtypeStruct((rows, width, length_z) if turned else perfuse.shape, F32),
        compiler_params=params(),
        cost_estimate=cost(16 * perfuse.size, 16 * perfuse.size),
        name="warm",
    )(*heats, *sources, *[side[0] for side in sides], *[side[1] for side in sides], below, above, perfuse)


def on_device(
    present_acoustic,
    prior_acoustic,
    location_factor,
    spectral_multiplier,
    medium_kinds,
    organ_properties,
    thermal_increase,
):
    term_count = lax.axis_size("term")
    blocks = lax.axis_size("pencil")
    rows, length_y, length_z = present_acoustic.shape
    length_x = rows * blocks
    width = length_y // term_count
    half = length_z // blocks // 2
    terms = location_factor.shape[0]
    brick_start = lax.axis_index("term") * width
    scale = 2.0 / (length_x * length_y * length_z)

    cut = width // 2 if width >= 4 else width
    spans = [(0, cut), (cut, width)] if cut < width else [(0, width)]

    def to_brick(values):
        return jnp.transpose(lax.dynamic_slice_in_dim(values, brick_start, width, 1), (1, 0, 2))

    def cut_up(brick):
        return [brick[start:end] for start, end in spans]

    def exchange(values):
        return lax.all_to_all(values, "pencil", 0, 0, tiled=True)

    opposite = [(p, blocks - 1 - p) for p in range(blocks)]
    middle = terms // 2
    sent = forward_z([to_brick(present_acoustic)], blocks)[0]
    sent, multiplier = lax.optimization_barrier((sent, spectral_multiplier))
    sent = exchange(sent)
    lowest = spectral_multiplier[:, :, 0, :]
    others, before = [], None
    for start, end in ((0, middle), (middle, terms)):
        if end > start:
            mirrored = mirror(multiplier, start, end)
            if others:
                mirrored, before, lowest = lax.optimization_barrier((mirrored, before, lowest))
                others = [(*others[0][:2], before)]
            else:
                mirrored, lowest = lax.optimization_barrier((mirrored, lowest))
            before = lax.ppermute(mirrored, "pencil", opposite)
            if not others:
                lowest = lowest + lax.ppermute(
                    flip(flip(lowest, 1), 2),
                    "pencil",
                    [(p, blocks - p) for p in range(1, blocks) if 2 * p != blocks],
                )
            others.append((start, end, before))
    lowest = jnp.transpose(lowest, (1, 0, 2))
    lowest = jnp.pad(lowest, ((0, 0), (0, -terms % 8), (0, 0)))
    me = lax.axis_index("term").reshape(1).astype(jnp.int32)
    factor = jnp.transpose(location_factor, (0, 2, 1, 3))
    last, factor = lax.optimization_barrier((others[0][2], factor))
    others[0] = (*others[0][:2], last)

    def gathered(part, offload):
        if offload or term_count == 1:
            return [lax.all_gather(part, "term", axis=0, tiled=False)]
        return [part] + [
            lax.ppermute(part, "term", [(i, (i - d) % term_count) for i in range(term_count)])
            for d in range(1, term_count)
        ]

    def spread_from(parts, sent_spans, group, chosen):
        out = spread(parts, sent_spans, me, lowest, spectral_multiplier, others, blocks, group, chosen)
        flat, tree = jax.tree.flatten(parts)
        out, *flat = lax.optimization_barrier((out, *flat))
        return out, jax.tree.unflatten(tree, flat)

    def summed(chunks, group):
        partial = gather(chunks, factor, scale, width, group)
        return lax.psum_scatter(partial, "term", scatter_dimension=0, tiled=True)

    def doubled_first(part, halos, warmed):
        parts = [[lax.all_gather(part, "term", axis=0, tiled=False)]]
        shared, chunks, bricks = [], {}, []
        if middle:
            out, parts = spread_from(parts, [(0, width)], (0, width), (0, middle))
            out, last = lax.optimization_barrier((out, others[-1][2]))
            others[-1] = (*others[-1][:2], last)
            shared = [exchange(out)]
        before = shared
        for index, group in enumerate(spans):
            out, parts = spread_from(parts, [(0, width)], group, (middle, terms))
            out, *before = lax.optimization_barrier((out, *before))
            if index == 0:
                shared = before
            out = exchange(out)
            before = [out]
            if index == 0:
                out, *halos = lax.optimization_barrier((out, *halos))
                heat = warmed(halos)
            if index == len(spans) - 1:
                out, heat = lax.optimization_barrier((out, heat))
            bricks.append(summed(shared + [out], group))
        return bricks, heat

    def doubled(parts):
        bricks, before = [], []
        for group in spans:
            out, parts = spread_from(parts, spans, group, (0, terms))
            out, *before = lax.optimization_barrier((out, *before))
            if before:
                chunks[0] = before[0]
                bricks.append(summed(chunks, spans[0]))
            chunks = [exchange(out)]
            before = list(chunks)
        bricks.append(summed(chunks, spans[-1]))
        return bricks

    def forward(bricks):
        parts, states, before = [], [], []
        for (start, end), (fresh, *older) in zip(spans, bricks):
            fresh, *before = lax.optimization_barrier((fresh, *before))
            if before:
                parts.append(gathered(before[0], True))
            sent, *state = forward_z([fresh, *older], blocks)
            sent = exchange(sent)
            before = [forward_x(sent, end - start, half, rows)]
            states.append(state)
        parts.append(gathered(before[0], False))
        return parts, states

    kinds = jnp.transpose(medium_kinds, (1, 0, 2))
    absorb, perfuse = [
        jnp.where(
            kinds == 0,
            organ_properties[0, at],
            jnp.where(kinds == 1, organ_properties[1, at], organ_properties[2, at]),
        )
        for at in range(2)
    ]
    thermal = jnp.transpose(thermal_increase, (1, 0, 2))

    previous = cut_up(to_brick(prior_acoustic))
    current = cut_up(to_brick(present_acoustic))
    dose = []
    doubles, heat = doubled_first(
        forward_x(sent, width, half, rows), halos_of(thermal), lambda halos: heat_step(thermal, halos, perfuse)
    )
    for _ in range(WAVE_STEPS - 1):
        parts, states = forward(list(zip(doubles, previous, *dose)))
        previous, current = current, [field for field, _ in states]
        dose = [[total for _, total in states]]
        doubles = doubled(parts)
    dose = dose[0] if dose else [jnp.zeros(each.shape, F32) for each in current]
    updated, sides, ahead = [], [], []
    for fresh, *rest in zip(doubles, previous, dose, cut_up(heat), cut_up(absorb)):
        fresh, *ahead = lax.optimization_barrier((fresh, *ahead))
        if ahead:
            sides.append(ahead)
        updated.append(update(fresh, *rest))
        ahead = halo(updated[-1][3:], not sides)
    sides.append(ahead)
    pressure = jnp.concatenate([each[0] for each in updated], axis=0)
    sources = [each[1] for each in updated]
    heats = [each[2] for each in updated]
    top = updated[-1][6]
    for _ in range(HEAT_STEPS - 2):
        heats = cut_up(warm(heats, sources, sides, top, perfuse, False))
        edges = [edges_of(each) for each in heats]
        sides = [halo(each, index == 0) for index, each in enumerate(edges)]
        top = edges[-1][3]
    return jnp.transpose(pressure, (1, 0, 2)), warm(heats, sources, sides, top, perfuse, True)


def solution(mesh):
    return jax.shard_map(
        on_device,
        mesh=mesh,
        in_specs=(
            P("pencil", None, None),
            P("pencil", None, None),
            P("term", "pencil", None, None),
            P("term", None, "pencil", None),
            P("pencil", "term", None),
            P(),
            P("pencil", "term", None),
        ),
        out_specs=(P("pencil", "term", None), P("pencil", "term", None)),
        check_vma=False,
    )
```
